32 devices in a mesh: ctx: 8 (over y, x, core), wsh: 4 (over z).
Axes of the slice: x: 2, y: 2, z: 4, core: 2. Of those that a mesh axis runs over, the one named last changes fastest.
Arguments:
- hidden_state: bfloat16 [12, 2048, 512], P('wsh', 'ctx'), may hold values from -1.6953125 to 1.6953125
- prev_state: bfloat16 [12, 2048, 512], P('wsh', 'ctx'), may hold values from -1.6953125 to 1.6953125
- halt_sum: float32 [12, 2048], P('wsh', 'ctx'), may hold values from 0 to 0.9
- halt_code: int32 [12, 2048], P('wsh', 'ctx'), may hold values from 0 to 2
- step_count: int32 [12, 2048], P('wsh', 'ctx'), may hold values from 0 to 3
- w_query: bfloat16 [512, 512], P(None, 'wsh'), may hold values from -0.25 to 0.25
- w_key: bfloat16 [512, 512], P(None, 'wsh'), may hold values from -0.25 to 0.25
- w_value: bfloat16 [512, 512], P(None, 'wsh'), may hold values from -0.25 to 0.25
- w_out: bfloat16 [512, 512], P('wsh'), may hold values from -2.5 to 2.5
- w_inner: bfloat16 [512, 2048], P(None, 'wsh'), may hold values from -0.25 to 0.25
- b_inner: bfloat16 [2048], P('wsh'), may hold values from -2.5 to 2.5
- w_outer: bfloat16 [2048, 512], P('wsh'), may hold values from -0.125 to 0.125
- b_outer: bfloat16 [512], P('wsh'), may hold values from -2.5 to 2.5
- gain_attention: bfloat16 [512], P('wsh'), may hold values from 0.099609375 to 1.8984375
- shift_attention: bfloat16 [512], P('wsh'), may hold values from -2.5 to 2.5
- gain_feedforward: bfloat16 [512], P('wsh'), may hold values from 0.099609375 to 1.8984375
- shift_feedforward: bfloat16 [512], P('wsh'), may hold values from -2.5 to 2.5
- w_halt: bfloat16 [512], P('wsh'), may hold values from -0.25 to 0.25
- b_halt: float32 [1], replicated, may hold values from -1 to 1
- grad_transformed: bfloat16 [12, 2048, 512], P('wsh', 'ctx'), may hold values from -1.6953125 to 1.6953125
- grad_blended: bfloat16 [12, 2048, 512], P('wsh', 'ctx'), may hold values from -1.6953125 to 1.6953125
- grad_sum: float32 [12, 2048], P('wsh', 'ctx'), may hold values from -1.7 to 1.7
Outputs:
- transformed: bfloat16 [12, 2048, 512], P('wsh', 'ctx')
- blended: bfloat16 [12, 2048, 512], P('wsh', 'ctx')
- new_sum: float32 [12, 2048], P('wsh', 'ctx')
- grad_state: float32 [12, 2048, 512], P('wsh', 'ctx')
- grad_prev: float32 [12, 2048, 512], P('wsh', 'ctx')
- grad_halt_sum: float32 [12, 2048], P('wsh', 'ctx')
- grad_w_query: float32 [512, 512], P(None, 'wsh')
- grad_w_key: float32 [512, 512], P(None, 'wsh')
- grad_w_value: float32 [512, 512], P(None, 'wsh')
- grad_w_out: float32 [512, 512], P('wsh')
- grad_w_inner: float32 [512, 2048], P(None, 'wsh')
- grad_b_inner: float32 [2048], P('wsh')
- grad_w_outer: float32 [2048, 512], P('wsh')
- grad_b_outer: float32 [512], P('wsh')
- grad_gain_attention: float32 [512], P('wsh')
- grad_shift_attention: float32 [512], P('wsh')
- grad_gain_feedforward: float32 [512], P('wsh')
- grad_shift_feedforward: float32 [512], P('wsh')
- grad_w_halt: float32 [512], P('wsh')
- grad_b_halt: float32 [1], replicated
The draws below stay inside these ranges and needn't reach their ends.
Inputs may be any that keep to these rules, and one draw needn't show every extreme that they name: halt_code is 0 for a token that halted earlier, 1 for one that keeps running, 2 for one that halts at this step.
All inputs are finite; a program needn't handle non-finite values.
Results may differ from the reference program's by a relative error of at most 0.028.
Values may be sent and summed in bfloat16 or wider, within the bound.
No kernel may reach another device: no remote copies, remote signals or barrier semaphores. Data moves between devices by JAX's collectives and lax.ppermute only.
A program may use at most 320 MiB of HBM per device.

```python
import math
import jax
import jax.numpy as jnp
from jax import lax

D = 512
HEADS = 8
HEAD = 64
FF = 2048
SEQS = 12
LENGTH = 2048


def with_ends(values, own_key, smallest, top_value):
    longest = values.shape.index(max(values.shape))
    spots = []
    for shift in (0, 1):
        where = [jax.random.randint(jax.random.fold_in(own_key, axis), (), 0, length) for axis, length in enumerate(values.shape)]
        where[longest] = (where[longest] + shift) % values.shape[longest]
        spots.append(tuple(where))
    return values.at[spots[0]].set(smallest).at[spots[1]].set(top_value)


def block_scale(key, dims, cuts, low, largest):
    level = 1.0
    for axis_at, blocks in cuts:
        steps = jax.random.uniform(jax.random.fold_in(jax.random.fold_in(key, 6), axis_at), (blocks,), jnp.float32, low / len(cuts), largest / len(cuts))
        level = level * jnp.repeat(jnp.exp(steps), dims[axis_at] // blocks).reshape((-1,) + (1,) * (len(dims) - 1 - axis_at))
    return level


def noise(own_key, extent, scale, most, pieces=(), kind=jnp.bfloat16):
    level = block_scale(own_key, extent, pieces, -0.22, 0.18) if pieces else 1.0
    array = jax.random.normal(own_key, extent, jnp.float32) * scale * level
    return jnp.minimum(jnp.maximum(array, -most), most).astype(kind)


def setup_inputs(seed: int = 0) -> dict:
    key_list = jax.random.split(jax.random.key(seed), 23)
    return {
        "hidden_state": jnp.clip(jax.random.uniform(key_list[0], (SEQS, LENGTH, D), jnp.float32, -1.6953125, 1.6953125) * block_scale(key_list[0], (SEQS, LENGTH, D), ((0, 4), (1, 8)), -0.4, 0.0), -1.6953125, 1.6953125).astype(jnp.bfloat16),
        "prev_state": jnp.clip(jax.random.uniform(key_list[1], (SEQS, LENGTH, D), jnp.float32, -1.6953125, 1.6953125) * block_scale(key_list[1], (SEQS, LENGTH, D), ((0, 4), (1, 8)), -0.4, 0.0), -1.6953125, 1.6953125).astype(jnp.bfloat16),
        "halt_sum": jnp.clip(0.9 * jax.random.uniform(key_list[2], (SEQS, LENGTH), jnp.float32) ** block_scale(key_list[2], (SEQS, LENGTH), ((0, 4), (1, 8)), -0.2, 0.2), 0.0, 0.9),
        "halt_code": with_ends(jax.random.randint(key_list[3], (SEQS, LENGTH), 0, 3), jax.random.fold_in(key_list[3], 1), 0, 2).astype(jnp.int32),
        "step_count": with_ends(jax.random.randint(key_list[4], (SEQS, LENGTH), 0, 4), jax.random.fold_in(key_list[4], 1), 0, 3).astype(jnp.int32),
        "w_query": noise(key_list[5], (D, D), D ** -0.5, 0.25, ((1, 4),)),
        "w_key": noise(key_list[6], (D, D), D ** -0.5, 0.25, ((1, 4),)),
        "w_value": noise(key_list[7], (D, D), D ** -0.5, 0.25, ((1, 4),)),
        "w_out": noise(key_list[8], (D, D), 6 ** -0.5, 2.5, ((0, 4),)),
        "w_inner": noise(key_list[9], (D, FF), D ** -0.5, 0.25, ((1, 4),)),
        "b_inner": noise(key_list[10], (FF,), 0.5, 2.5, ((0, 4),)),
        "w_outer": noise(key_list[11], (FF, D), FF ** -0.5, 0.125, ((0, 4),)),
        "b_outer": noise(key_list[12], (D,), 0.5, 2.5, ((0, 4),)),
        "gain_attention": jnp.clip(1.0 + 0.18 * jax.random.normal(key_list[13], (D,), jnp.float32), 0.099609375, 1.8984375).astype(jnp.bfloat16),
        "shift_attention": noise(key_list[14], (D,), 0.3, 2.5, ((0, 4),)),
        "gain_feedforward": jnp.clip(1.0 + 0.18 * jax.random.normal(key_list[15], (D,), jnp.float32), 0.099609375, 1.8984375).astype(jnp.bfloat16),
        "shift_feedforward": noise(key_list[16], (D,), 0.3, 2.5, ((0, 4),)),
        "w_halt": noise(key_list[17], (D,), D ** -0.5, 0.25, ((0, 4),)),
        "b_halt": jnp.clip(jax.random.uniform(key_list[18], (1,), jnp.float32, -1.0, 1.0), -1.0, 1.0),
        "grad_transformed": jnp.clip(jax.random.uniform(key_list[19], (SEQS, LENGTH, D), jnp.float32, -1.6953125, 1.6953125) * block_scale(key_list[19], (SEQS, LENGTH, D), ((0, 4), (1, 8)), -0.4, 0.0), -1.6953125, 1.6953125).astype(jnp.bfloat16),
        "grad_blended": jnp.clip(jax.random.uniform(key_list[20], (SEQS, LENGTH, D), jnp.float32, -1.6953125, 1.6953125) * block_scale(key_list[20], (SEQS, LENGTH, D), ((0, 4), (1, 8)), -0.4, 0.0), -1.6953125, 1.6953125).astype(jnp.bfloat16),
        "grad_sum": jnp.clip(jax.random.uniform(key_list[21], (SEQS, LENGTH), jnp.float32, -1.7, 1.7) * block_scale(key_list[21], (SEQS, LENGTH), ((0, 4), (1, 8)), -0.4, 0.0), -1.7, 1.7),
    }


@jax.custom_vjp
def low(v):
    return lax.optimization_barrier(v.astype(jnp.bfloat16)).astype(jnp.float32)

@jax.custom_vjp
def low_back(v):
    return v

def low_keep(v):
    return (low(v), None)

def low_pass(kept, grad):
    return (grad,)

def back_keep(v):
    return (v, None)

def back_low(kept, grad):
    return (low(grad),)
low.defvjp(low_keep, low_pass)
low_back.defvjp(back_keep, back_low)
highest = lax.Precision.HIGHEST
epsilon = 1e-06

def gelu_exact(values):
    return 0.5 * values * (1.0 + lax.erf(values * 2.0 ** (-0.5)))

def signal(places, columns):
    halves = columns // 2
    frequency = jnp.exp(-math.log(10000.0) * jnp.arange(halves, dtype=jnp.float32) / (halves - 1))
    angles = places.astype(jnp.float32)[:, None] * frequency[None, :]
    return jnp.concatenate([jnp.sin(angles), jnp.cos(angles)], axis=1)

def layer_norm(summed, gain_row, shift_row):
    centre = summed - lax.optimization_barrier(jnp.mean(summed, axis=1, keepdims=True))
    inverse = lax.rsqrt(lax.optimization_barrier(jnp.mean(centre * centre, axis=1, keepdims=True)) + epsilon)
    return centre * inverse * gain_row + shift_row

def attention_block(query_block, key_heads, value_heads):
    scores = low_back(jnp.einsum('hqd,hkd->hqk', query_block, key_heads, precision=highest) * HEAD ** (-0.5))
    probs = jax.nn.softmax(scores, axis=-1)
    return jnp.einsum('hqk,hkd->hqd', low(probs), value_heads, precision=highest)

def forward(state_rows, prev_rows, sum_rows, params, code_rows, count_rows):
    w_query, w_key, w_value, w_out, w_inner, b_inner, w_outer, b_outer, gain_one, shift_one, gain_two, shift_two, w_halt, b_halt = params
    seq_length = state_rows.shape[0]
    places = jnp.arange(seq_length, dtype=jnp.int32)
    embedded = state_rows + signal(places, D) + signal(count_rows, D)
    halt_prob = jax.nn.sigmoid(jnp.dot(embedded, w_halt, precision=highest) + b_halt[0])
    embed_low = low(embedded)
    queries = low_back(low(jnp.dot(embed_low, w_query, precision=highest)))
    keys_all = low_back(low(jnp.dot(embed_low, w_key, precision=highest)))
    values_all = low_back(low(jnp.dot(embed_low, w_value, precision=highest)))

    def to_heads(matrix):
        return matrix.reshape(seq_length, HEADS, HEAD).transpose(1, 0, 2)
    block_size = math.gcd(seq_length, 512)
    key_heads = to_heads(keys_all)
    value_heads = to_heads(values_all)
    query_blocks = to_heads(queries).reshape(HEADS, seq_length // block_size, block_size, HEAD).transpose(1, 0, 2, 3)

    def one_block(query_block):
        return attention_block(query_block, key_heads, value_heads)
    attended_blocks = lax.map(jax.checkpoint(one_block), query_blocks)
    attended = attended_blocks.transpose(0, 2, 1, 3).reshape(seq_length, D)
    attended_low = low_back(low(attended))
    branch = low_back(jnp.dot(attended_low, w_out, precision=highest))
    norm_one = layer_norm(embedded + branch, gain_one, shift_one)
    norm_low = low(norm_one)
    inner = low_back(jnp.dot(norm_low, w_inner, precision=highest) + b_inner)
    inner_low = low(gelu_exact(inner))
    feed_out = low_back(jnp.dot(inner_low, w_outer, precision=highest) + b_outer)
    final = layer_norm(norm_one + feed_out, gain_two, shift_two)
    running = (code_rows > 0).astype(jnp.float32)
    halting = (code_rows == 2).astype(jnp.float32)
    update = running * (halting * (1.0 - sum_rows) + (1.0 - halting) * halt_prob)
    new_sum = sum_rows + update
    blended = prev_rows * (1.0 - update)[:, None] + final * update[:, None]
    return (final, blended, new_sum)

def reference(hidden_state, prev_state, halt_sum, halt_code, step_count, w_query, w_key, w_value, w_out, w_inner, b_inner, w_outer, b_outer, gain_attention, shift_attention, gain_feedforward, shift_feedforward, w_halt, b_halt, grad_transformed, grad_blended, grad_sum):
    params = (w_query.astype(jnp.float32), w_key.astype(jnp.float32), w_value.astype(jnp.float32), w_out.astype(jnp.float32), w_inner.astype(jnp.float32), b_inner.astype(jnp.float32), w_outer.astype(jnp.float32), b_outer.astype(jnp.float32), gain_attention.astype(jnp.float32), shift_attention.astype(jnp.float32), gain_feedforward.astype(jnp.float32), shift_feedforward.astype(jnp.float32), w_halt.astype(jnp.float32), b_halt.astype(jnp.float32))

    def per_sequence(totals, inputs):
        state_rows, prev_rows, sum_rows, code_rows, count_rows, final_grad, blend_grad, sum_grad = inputs

        def local_forward(state_float, prev_float, sum_float, param_set):
            return forward(state_float, prev_float, sum_float, param_set, code_rows, count_rows)
        outputs, pullback = jax.vjp(local_forward, state_rows.astype(jnp.float32), prev_rows.astype(jnp.float32), sum_rows, params)
        grad_state_rows, grad_prev_rows, grad_sum_rows, grad_params = pullback((final_grad.astype(jnp.float32), blend_grad.astype(jnp.float32), sum_grad))
        totals = jax.tree.map(jnp.add, totals, grad_params)
        return (totals, (outputs[0].astype(jnp.bfloat16), outputs[1].astype(jnp.bfloat16), outputs[2], grad_state_rows, grad_prev_rows, grad_sum_rows))
    zero_params = jax.tree.map(jnp.zeros_like, params)
    totals, results = lax.scan(per_sequence, zero_params, (hidden_state, prev_state, halt_sum, halt_code, step_count, grad_transformed, grad_blended, grad_sum))
    return (results[0], results[1], results[2], results[3], results[4], results[5], totals[0], totals[1], totals[2], totals[3], totals[4], totals[5], totals[6], totals[7], totals[8], totals[9], totals[10], totals[11], totals[12], totals[13])
```

```python
import functools
import math

import jax
import jax.numpy as jnp
from jax import lax
from jax.experimental import pallas as pl
from jax.experimental.pallas import tpu as pltpu
from jax.sharding import PartitionSpec as P

HEADS = 8
PAIRS = 4
WIDE = 128
SMALL = 16
epsilon = 1e-06
f32 = jnp.float32
bf16 = jnp.bfloat16
LOG2E = math.log2(math.e)
NT = (((1,), (1,)), ((), ()))
TN = (((0,), (0,)), ((), ()))
NN = (((1,), (0,)), ((), ()))
MIB = 1024 * 1024


def room(mebibytes):
    return pltpu.CompilerParams(vmem_limit_bytes=int(mebibytes) * MIB)


def cost(micros):
    return pl.CostEstimate(flops=int(micros * 1.1e9), bytes_accessed=1024, transcendentals=0)


def dot(a, b, dims=NN):
    return lax.dot_general(a, b, dims, preferred_element_type=f32)


def lane_masks(shape):
    lane = lax.broadcasted_iota(jnp.int32, shape, 1)
    return lane < WIDE // 2


def attend_kernel(blocks, carried, q_ref, *refs):
    kv_refs = refs[:blocks]
    refs = refs[blocks + carried :]
    o_ref, mass_ref, low_refs = refs[0], refs[1], refs[2:]
    scale = 0.125 * LOG2E
    q = q_ref[0]
    first = lane_masks(q.shape)
    none = jnp.zeros_like(q)
    outs, masses = [], []
    for head in range(2):
        mine = jnp.where(first, q, none) if head == 0 else jnp.where(first, none, q)
        chunks = []
        for ref in kv_refs:
            for start in range(0, ref.shape[1], 512):
                chunks.append((ref, start))
        scores = [dot(mine, ref[0, start : start + 512, :WIDE], NT) for ref, start in chunks]
        top = functools.reduce(jnp.maximum, scores)
        top = jnp.max(top, axis=1, keepdims=True)
        lift = top * scale
        total = None
        weighted = None
        for piece, (ref, start) in zip(scores, chunks):
            e = jnp.exp2(piece * scale - lift)
            part = sum(e[:, i : i + 128] for i in range(0, 512, 128))
            total = part if total is None else total + part
            w = dot(e.astype(bf16), ref[0, start : start + 512, WIDE:])
            weighted = w if weighted is None else weighted + w
        total = jnp.sum(total, axis=1, keepdims=True)
        outs.append(weighted * (1.0 / total))
        masses.append(lift + jnp.log2(total))
    out = jnp.where(first, outs[0], outs[1])
    o_ref[0] = out
    low = out.astype(bf16)
    for d, ref in enumerate(low_refs):

        @pl.when(pl.program_id(0) == d)
        def _(ref=ref):
            ref[0] = low

    table = jnp.where(first, masses[0], masses[1])
    turned = jnp.transpose(table)
    mass_ref[0] = jnp.concatenate([turned[0:4], turned[64:68]], axis=0)


def attend(at, seqs, q, kvs, before):
    _, rows, _ = q.shape
    step = rows // PAIRS
    keys = sum(kv.shape[1] for kv in kvs)
    shapes = [
        jax.ShapeDtypeStruct((seqs, rows, WIDE), f32),
        jax.ShapeDtypeStruct((seqs, 8, rows), f32),
    ] + [jax.ShapeDtypeStruct((seqs, step, WIDE), bf16)] * PAIRS
    carried = len(shapes) if before else 0
    return pl.pallas_call(
        functools.partial(attend_kernel, len(kvs), carried),
        grid=(PAIRS,),
        in_specs=[pl.BlockSpec((1, step, WIDE), lambda i: (0, i, 0))]
        + [full_spec(kv) for kv in kvs]
        + [pl.BlockSpec(memory_space=pl.ANY)] * carried,
        out_specs=[
            pl.BlockSpec((1, step, WIDE), lambda i: (at, i, 0)),
            pl.BlockSpec((1, 8, step), lambda i: (at, 0, i)),
        ]
        + [pl.BlockSpec((1, step, WIDE), lambda i: (at, 0, 0))] * PAIRS,
        out_shape=shapes,
        input_output_aliases={1 + len(kvs) + i: i for i in range(carried)},
        compiler_params=room(10 + keys // 256),
        cost_estimate=cost(4),
        name="attend",
    )(q, *kvs, *(before or ()))


def attend_back_kernel(blocks, q_ref, *refs):
    g_refs, o_ref, mass_ref = refs[:PAIRS], refs[PAIRS], refs[PAIRS + 1]
    refs = refs[PAIRS + 2 :]
    kv_refs = refs[:blocks]
    dq_ref = refs[blocks]
    dkv_refs = refs[blocks + 1 : 2 * blocks + 1]
    dq_acc = refs[2 * blocks + 1]
    scale = 0.125 * LOG2E
    q = q_ref[0]
    g = jnp.concatenate([ref[0] for ref in g_refs], axis=0)
    first = lane_masks(q.shape)
    none = jnp.zeros_like(q)
    qs = [jnp.where(first, q, none), jnp.where(first, none, q)]
    gs = [jnp.where(first, g, none), jnp.where(first, none, g)]
    product = g.astype(f32) * o_ref[0]
    which = lax.broadcasted_iota(jnp.int32, (8, WIDE), 0) == (
        lax.broadcasted_iota(jnp.int32, (8, WIDE), 1) // (WIDE // 2)
    )
    deltas = lax.dot_general(
        which.astype(f32), product, NT, precision=lax.Precision.HIGHEST, preferred_element_type=f32
    )
    delta = [deltas[0:1], deltas[1:2]]
    mass = [mass_ref[0, 0:1, :], mass_ref[0, 4:5, :]]
    dq_acc[...] = jnp.zeros_like(dq_acc)
    size = 256
    key_first = lane_masks((size, WIDE))
    key_none = jnp.zeros((size, WIDE), bf16)

    for kv_ref, dkv_ref in zip(kv_refs, dkv_refs):

        def chunk(i, carry, kv_ref=kv_ref, dkv_ref=dkv_ref):
            at = pl.ds(pl.multiple_of(i * size, size), size)
            k = kv_ref[0, at, :WIDE]
            v = kv_ref[0, at, WIDE:]
            dk = dv = dq = None
            for head in range(2):
                s = dot(k, qs[head], NT)
                p = jnp.exp2(s * scale - mass[head])
                dp = dot(v, gs[head], NT)
                ds = (p * (dp - delta[head])).astype(bf16)
                own_v = dot(p.astype(bf16), gs[head])
                own_k = dot(ds, qs[head])
                km = jnp.where(key_first, k, key_none) if head == 0 else jnp.where(key_first, key_none, k)
                own_q = dot(ds, km, TN)
                dv = own_v if dv is None else dv + own_v
                dk = own_k if dk is None else dk + own_k
                dq = own_q if dq is None else dq + own_q
            dkv_ref[0, at, :WIDE] = (dk * 0.125).astype(dkv_ref.dtype)
            dkv_ref[0, at, WIDE:] = dv.astype(dkv_ref.dtype)
            dq_acc[...] += dq
            return carry

        lax.fori_loop(0, kv_ref.shape[1] // size, chunk, 0)
    dq_ref[0] = (dq_acc[...] * 0.125).astype(bf16)


def attend_back(at, q, gs, o, mass, kvs, kinds):
    _, rows, _ = q.shape
    keys = sum(kv.shape[1] for kv in kvs)
    own = gs[0].shape[1]
    whole = lambda width: pl.BlockSpec((1, rows, width), lambda s: (0, 0, 0))
    kv_specs = [pl.BlockSpec((1, kv.shape[1], 2 * WIDE), lambda s: (0, 0, 0)) for kv in kvs]
    return pl.pallas_call(
        functools.partial(attend_back_kernel, len(kvs)),
        grid=(1,),
        in_specs=[whole(WIDE)]
        + [pl.BlockSpec((1, own, WIDE), lambda s: (at, 0, 0))] * PAIRS
        + [pl.BlockSpec((1, rows, WIDE), lambda s: (at, 0, 0)), pl.BlockSpec((1, 8, rows), lambda s: (at, 0, 0))]
        + kv_specs,
        out_specs=[whole(WIDE)] + kv_specs,
        out_shape=[jax.ShapeDtypeStruct((1, rows, WIDE), bf16)]
        + [jax.ShapeDtypeStruct(kv.shape, kind) for kv, kind in zip(kvs, kinds)],
        scratch_shapes=[pltpu.VMEM((rows, WIDE), f32)],
        compiler_params=room(14 + keys // 512),
        cost_estimate=cost(14),
        name="attend_back",
    )(q, *gs, o, mass, *kvs)


def full_spec(array):
    return pl.BlockSpec(array.shape, lambda *_: (0,) * array.ndim)


def pack_kernel(info_ref, *refs):
    parts, out_ref = refs[:-1], refs[-1]
    core = info_ref[0]
    half = out_ref.shape[0]

    @pl.when(core == 0)
    def _():
        out_ref[...] = jnp.concatenate([ref[:half] for ref in parts], axis=1)

    @pl.when(core != 0)
    def _():
        out_ref[...] = jnp.concatenate([ref[half:] for ref in parts], axis=1)


def pack(info, parts):
    rows, width = parts[0].shape
    shape = (rows // 2, len(parts) * width)
    return pl.pallas_call(
        pack_kernel,
        grid=(1,),
        in_specs=[pl.BlockSpec(memory_space=pltpu.SMEM)] + [full_spec(x) for x in parts],
        out_specs=pl.BlockSpec(shape, lambda i: (0, 0)),
        out_shape=jax.ShapeDtypeStruct(shape, bf16),
        compiler_params=room(6),
        cost_estimate=cost(1),
        name="pack",
    )(info, *parts)


def pack_feed_kernel(info_ref, inner_ref, outer_ref, wout_ref, bias_ref, *refs):
    vectors, out_ref = refs[:-1], refs[-1]
    core = info_ref[0]
    width = inner_ref.shape[0]
    cut = wout_ref.shape[0] // 2

    @pl.when(core == 0)
    def _():
        out_ref[:width] = inner_ref[...]
        out_ref[width : width + cut] = wout_ref[:cut]

    @pl.when(core != 0)
    def _():
        out_ref[:width] = outer_ref[...]
        out_ref[width : width + cut] = wout_ref[cut:]

    row = lax.broadcasted_iota(jnp.int32, (SMALL, WIDE), 0)
    table = jnp.zeros((SMALL, WIDE), f32)
    for i, ref in enumerate(vectors):
        table = jnp.where(row == i + 1, ref[...].astype(f32), table)
    row = lax.broadcasted_iota(jnp.int32, (SMALL, width), 0)
    table = jnp.concatenate([table, jnp.zeros((SMALL, width - WIDE), f32)], axis=1)
    table = jnp.where(row == 0, bias_ref[...].astype(f32), table)
    out_ref[width + cut :] = table.astype(bf16)


def pack_feed(info, w_inner, w_outer, w_out, b_inner, vectors):
    width = w_inner.shape[0]
    parts = [w_inner, w_outer, w_out, b_inner.reshape(1, -1)] + [v.reshape(1, -1) for v in vectors]
    shape = (width + w_out.shape[0] // 2 + SMALL, w_out.shape[1])
    return pl.pallas_call(
        pack_feed_kernel,
        grid=(1,),
        in_specs=[pl.BlockSpec(memory_space=pltpu.SMEM)] + [full_spec(x) for x in parts],
        out_specs=pl.BlockSpec(shape, lambda i: (0, 0)),
        out_shape=jax.ShapeDtypeStruct(shape, bf16),
        compiler_params=room(10),
        cost_estimate=cost(2),
        name="pack_feed",
    )(info, *parts)


def project_kernel(count, *refs):
    blocks, w_ref, q_ref, kv_ref = refs[:count], refs[count], refs[count + 1], refs[count + 2]
    at = 0
    for ref in blocks:
        rows = ref.shape[1]
        made = dot(ref[0], w_ref[0]).astype(bf16)
        q_ref[0, at : at + rows] = made[:, :WIDE]
        kv_ref[0, at : at + rows] = made[:, WIDE:]
        at += rows


def project(at, tokens, w_order):
    total = sum(x.shape[1] for x in tokens)
    return pl.pallas_call(
        functools.partial(project_kernel, len(tokens)),
        grid=(1,),
        in_specs=[pl.BlockSpec((1,) + x.shape[1:], lambda i: (at, 0, 0)) for x in tokens]
        + [pl.BlockSpec((1,) + w_order.shape[1:], lambda i: (0, 0, 0))],
        out_specs=[
            pl.BlockSpec((1, total, WIDE), lambda i: (0, 0, 0)),
            pl.BlockSpec((1, total, 2 * WIDE), lambda i: (0, 0, 0)),
        ],
        out_shape=[
            jax.ShapeDtypeStruct((1, total, WIDE), bf16),
            jax.ShapeDtypeStruct((1, total, 2 * WIDE), bf16),
        ],
        compiler_params=room(10),
        cost_estimate=cost(1),
        name="project",
    )(*tokens, w_order)


def combine_kernel(chosen, count, prior, final, info_ref, *refs):
    blocks, refs = refs[:count], refs[count:]
    backs, refs = refs[: 3 * len(chosen)], refs[3 * len(chosen) :]
    grad = None
    if prior:
        grad, refs = refs[0][...], refs[1:]
    outs, grad_refs = refs[:PAIRS], refs[PAIRS:]
    rows = outs[0].shape[1]
    for i, s in enumerate(chosen):
        dq_ref, kept_ref, got_ref = backs[3 * i : 3 * i + 3]
        at = 0
        for ref in blocks:
            size = ref.shape[1]
            part = slice(at, at + size)
            dkv = (kept_ref[0, part] + got_ref[0, part].astype(f32)).astype(bf16)
            piece = jnp.concatenate([dq_ref[0, part], dkv], axis=1)
            outs[at // rows][i, at % rows : at % rows + size] = piece
            term = dot(ref[s], piece, TN)
            grad = term if grad is None else grad + term
            at += size
    if not final:
        grad_refs[0][...] = grad
        return
    size = grad.shape[0] // (2 * PAIRS)

    def write(even_ref, odd_ref):
        for c in range(2 * PAIRS):
            ref = even_ref if c % 2 == 0 else odd_ref
            ref[jnp.bitwise_xor(c // 2, info_ref[2])] = grad[c * size : (c + 1) * size].astype(ref.dtype)

    @pl.when(info_ref[0] == 0)
    def _():
        write(grad_refs[0], grad_refs[1])

    @pl.when(info_ref[0] != 0)
    def _():
        write(grad_refs[1], grad_refs[0])


def combine(info, chosen, tokens, backs, prior, final):
    _, rows, width = tokens[0].shape
    flat = [x for back in backs for x in back]
    extra = [] if prior is None else [prior]
    if final:
        shape = (PAIRS, width // (2 * PAIRS), 3 * WIDE)
        grads = [jax.ShapeDtypeStruct(shape, f32), jax.ShapeDtypeStruct(shape, bf16)]
    else:
        grads = [jax.ShapeDtypeStruct((width, 3 * WIDE), f32)]
    pieces = [jax.ShapeDtypeStruct((len(chosen), rows, 3 * WIDE), bf16)] * PAIRS
    return pl.pallas_call(
        functools.partial(combine_kernel, chosen, len(tokens), len(extra), final),
        grid=(1,),
        in_specs=[pl.BlockSpec(memory_space=pltpu.SMEM)] + [full_spec(x) for x in tokens + flat + extra],
        out_specs=[full_spec(x) for x in pieces + grads],
        out_shape=pieces + grads,
        compiler_params=room(20),
        cost_estimate=cost(2),
        name="combine",
    )(info, *tokens, *flat, *extra)


def join_small_kernel(keep_ref, got_ref, *outs):
    for d, out in enumerate(outs):
        out[...] = (keep_ref[d] + got_ref[d].astype(f32)).astype(bf16)


def join_small(keep, got):
    return pl.pallas_call(
        join_small_kernel,
        grid=(1,),
        in_specs=[full_spec(keep), full_spec(got)],
        out_specs=[pl.BlockSpec(keep.shape[1:], lambda i: (0, 0))] * PAIRS,
        out_shape=[jax.ShapeDtypeStruct(keep.shape[1:], bf16)] * PAIRS,
        compiler_params=room(6),
        cost_estimate=cost(1),
        name="join_small",
    )(keep, got)


def share_small_kernel(info_ref, *refs):
    parts, outs = refs[:PAIRS], refs[PAIRS:]
    for step, out in enumerate(outs):
        at = jnp.bitwise_xor(jnp.bitwise_xor(info_ref[1], info_ref[2]), step)
        value = parts[0][...]
        for d in range(1, PAIRS):
            value = jnp.where(at == d, parts[d][...], value)
        out[...] = value


def share_small(info, parts):
    return pl.pallas_call(
        share_small_kernel,
        grid=(1,),
        in_specs=[pl.BlockSpec(memory_space=pltpu.SMEM)] + [full_spec(x) for x in parts],
        out_specs=[full_spec(x) for x in parts],
        out_shape=[jax.ShapeDtypeStruct(x.shape, bf16) for x in parts],
        compiler_params=room(6),
        cost_estimate=cost(1),
        name="share_small",
    )(info, *parts)


def state_kernel(base_ref, *refs):
    blocks, w_ref, out_ref = refs[:PAIRS], refs[PAIRS], refs[PAIRS + 1]
    total = base_ref[0]
    for d, ref in enumerate(blocks):
        total = total + dot(ref[0], w_ref[d], NT)
    out_ref[0] = total


def add_state(at, place, base, blocks, w_order):
    rows, width = base.shape[1:]
    return pl.pallas_call(
        state_kernel,
        grid=(1,),
        in_specs=[pl.BlockSpec((1, rows, width), lambda i: (at, 0, 0))]
        + [pl.BlockSpec((1,) + b.shape[1:], lambda i: (place, 0, 0)) for b in blocks]
        + [full_spec(w_order)],
        out_specs=pl.BlockSpec((1, rows, width), lambda i: (at, 0, 0)),
        out_shape=jax.ShapeDtypeStruct(base.shape, base.dtype),
        input_output_aliases={0: 0},
        compiler_params=room(10),
        cost_estimate=cost(2.5),
        name="add_state",
    )(base, *blocks, w_order)


def assemble_kernel(info_ref, *refs):
    mine, other, out_ref = refs[:PAIRS], refs[PAIRS : 2 * PAIRS], refs[2 * PAIRS]
    core, zed, pair = info_ref[0], info_ref[1], info_ref[2]
    half = mine[0].shape[0]
    for a in range(PAIRS):
        order = jnp.bitwise_xor(lax.rem(zed + a, PAIRS), pair)
        for side in range(2):
            step = (-a) % PAIRS if side == 0 else a
            piece = jnp.where(core == side, mine[step][...], other[step][...])
            out_ref[order, side * half : (side + 1) * half] = piece


def assemble(info, mine, other):
    half, width = mine[0].shape
    shape = (PAIRS, 2 * half, width)
    return pl.pallas_call(
        assemble_kernel,
        grid=(1,),
        in_specs=[pl.BlockSpec(memory_space=pltpu.SMEM)] + [full_spec(x) for x in mine + other],
        out_specs=pl.BlockSpec(shape, lambda i: (0, 0, 0)),
        out_shape=jax.ShapeDtypeStruct(shape, bf16),
        compiler_params=room(10),
        cost_estimate=cost(3),
        name="assemble",
    )(info, *mine, *other)


def keep_scalar(block):
    tail = block[-8:]
    total = tail[:, :WIDE] + tail[:, WIDE : 2 * WIDE]
    high = total.astype(bf16).astype(f32)
    split = jnp.concatenate([high, total - high, tail[:, 2 * WIDE :]], axis=1)
    row = lax.broadcasted_iota(jnp.int32, tail.shape, 0)
    tail = jnp.where(row == 6, split, tail)
    return tail if block.shape[0] == 8 else jnp.concatenate([block[:-8], tail], axis=0)


def flat_rows(ref):
    return ref[...].reshape(-1, ref.shape[-1])


def write_pieces(info_ref, even_ref, odd_ref, grads, small):
    pieces = 2 * PAIRS * even_ref.shape[1]

    def write(keep_ref, give_ref):
        for c in range(pieces):
            ref = keep_ref if c % 2 == 0 else give_ref
            order = jnp.bitwise_xor((c // 2) % PAIRS, info_ref[2])
            repeat = c // (2 * PAIRS)
            at = 0
            for grad in grads:
                size = grad.shape[0] // pieces
                ref[order, repeat, 0, at : at + size] = grad[c * size : (c + 1) * size]
                at += size
            if small is not None:
                ref[order, repeat, 0, at : at + 8] = small if c == 0 else jnp.zeros_like(small)

    @pl.when(info_ref[0] == 0)
    def _():
        write(even_ref, odd_ref)

    @pl.when(info_ref[0] != 0)
    def _():
        write(odd_ref, even_ref)


def outer_grad_kernel(
    info_ref, a0_ref, a1_ref, a2_ref, a3_ref, ilow_ref, gfeed_ref, gbranch_ref, even_ref, odd_ref
):
    g_outer = dot(flat_rows(ilow_ref), flat_rows(gfeed_ref), TN).astype(bf16)
    order = jnp.bitwise_xor(pl.program_id(0), info_ref[2])
    low, high = order % 2 == 0, order < 2
    att = jnp.where(
        high,
        jnp.where(low, flat_rows(a0_ref), flat_rows(a1_ref)),
        jnp.where(low, flat_rows(a2_ref), flat_rows(a3_ref)),
    )
    g_out = dot(att, flat_rows(gbranch_ref), TN).astype(bf16)
    write_pieces(info_ref, even_ref, odd_ref, (g_outer, g_out), None)


def inner_grad_kernel(info_ref, nlow_ref, gin_ref, vsum_ref, bsum_ref, even_ref, odd_ref):
    g_in = dot(flat_rows(nlow_ref), flat_rows(gin_ref), TN).astype(bf16)
    vectors = sum(vsum_ref[s] for s in range(vsum_ref.shape[0]))
    bias = sum(bsum_ref[s] for s in range(bsum_ref.shape[0]))
    width = g_in.shape[1]
    low = jnp.concatenate([vectors, jnp.zeros((8, width - WIDE), f32)], axis=1)
    row = lax.broadcasted_iota(jnp.int32, (8, width), 0)
    small = keep_scalar(jnp.where(row == 7, bias, low)).astype(bf16)
    write_pieces(info_ref, even_ref, odd_ref, (g_in,), small)


def split_grads(kernel, name, info, arrays, specs, piece, width, ctx):
    shape = (PAIRS, ctx // (2 * PAIRS), PAIRS, piece, width)
    out_spec = pl.BlockSpec(shape[:2] + (1, piece, width), lambda z, info: (0, 0, z, 0, 0))
    return pl.pallas_call(
        kernel,
        grid_spec=pltpu.PrefetchScalarGridSpec(
            num_scalar_prefetch=1, grid=(PAIRS,), in_specs=specs, out_specs=[out_spec, out_spec]
        ),
        out_shape=[jax.ShapeDtypeStruct(shape, bf16)] * 2,
        compiler_params=room(24),
        cost_estimate=cost(4.5),
        name=name,
    )(info, *arrays)


def hidden_spec(array):
    seqs, rows, hidden = array.shape
    return pl.BlockSpec(
        (seqs, rows, hidden // PAIRS), lambda z, info: (0, 0, lax.rem(z - info[1] + PAIRS, PAIRS))
    )


def outer_grads(info, att, ilow, gfeed, gbranch, ctx):
    width = gfeed.shape[2]
    piece = (ilow.shape[2] // PAIRS + width // PAIRS) // ctx
    arrays = [*att, ilow, gfeed, gbranch]
    specs = [full_spec(x) for x in arrays]
    specs[PAIRS] = hidden_spec(ilow)
    return split_grads(outer_grad_kernel, "outer_grads", info, arrays, specs, piece, width, ctx)


def inner_grads(info, nlow, gin, vsum, bsum, ctx):
    width = nlow.shape[2]
    seqs = vsum.shape[0]
    specs = [
        full_spec(nlow),
        hidden_spec(gin),
        pl.BlockSpec((seqs, 8, WIDE), lambda z, info: (0, 0, z)),
        hidden_spec(bsum),
    ]
    piece = width // ctx + 8
    return split_grads(
        inner_grad_kernel, "inner_grads", info, [nlow, gin, vsum, bsum], specs, piece, gin.shape[2] // PAIRS, ctx
    )


def join_kernel(scalar, keep_ref, got_ref, *outs):
    for d, out in enumerate(outs):
        for r in range(out.shape[0]):
            total = keep_ref[d, r, 0].astype(f32) + got_ref[d, r, 0].astype(f32)
            out[r, 0] = (keep_scalar(total) if scalar else total).astype(bf16)


def join(keep, got, scalar):
    _, repeats, wsh, piece, width = keep.shape
    spec = pl.BlockSpec((PAIRS, repeats, 1, piece, width), lambda z: (0, 0, z, 0, 0))
    return pl.pallas_call(
        functools.partial(join_kernel, scalar),
        grid=(wsh,),
        in_specs=[spec, spec],
        out_specs=[pl.BlockSpec((repeats, 1, piece, width), lambda z: (0, z, 0, 0))] * PAIRS,
        out_shape=[jax.ShapeDtypeStruct(keep.shape[1:], bf16)] * PAIRS,
        compiler_params=room(16),
        cost_estimate=cost(1.5),
        name="join",
    )(keep, got)


def share_kernel(info_ref, *refs):
    firsts, seconds, outs = refs[:PAIRS], refs[PAIRS : 2 * PAIRS], refs[2 * PAIRS :]
    for step in range(PAIRS):
        place = jnp.bitwise_xor(info_ref[1], step)
        out = outs[step % 2]
        for r in range(out.shape[0]):
            totals = []
            for parts in (firsts, seconds):
                total = parts[0][r, place].astype(f32)
                for part in parts[1:]:
                    total = total + part[r, place].astype(f32)
                totals.append(total)
            size = totals[0].shape[0]
            out[r, step // 2, :size] = totals[0].astype(bf16)
            out[r, step // 2, size:] = keep_scalar(totals[1]).astype(bf16)


def share_parts(info, firsts, seconds):
    repeats, wsh, piece, width = firsts[0].shape
    shape = (repeats, wsh // 2, piece + seconds[0].shape[2], width)
    return pl.pallas_call(
        share_kernel,
        grid=(1,),
        in_specs=[pl.BlockSpec(memory_space=pltpu.SMEM)] + [full_spec(x) for x in firsts + seconds],
        out_specs=[pl.BlockSpec(shape, lambda i: (0, 0, 0, 0))] * 2,
        out_shape=[jax.ShapeDtypeStruct(shape, bf16)] * 2,
        compiler_params=room(16),
        cost_estimate=cost(1.5),
        name="share",
    )(info, *firsts, *seconds)


def halve_kernel(keep_ref, got_ref, own_ref, send_ref):
    for at, out in enumerate((own_ref, send_ref)):
        out[...] = keep_scalar(keep_ref[at].astype(f32) + got_ref[at].astype(f32)).astype(bf16)


def halve(keep, got):
    shape = keep.shape[1:]
    return pl.pallas_call(
        halve_kernel,
        grid=(1,),
        in_specs=[full_spec(keep), full_spec(got)],
        out_specs=[pl.BlockSpec(shape, lambda i: (0, 0))] * 2,
        out_shape=[jax.ShapeDtypeStruct(shape, bf16)] * 2,
        compiler_params=room(6),
        cost_estimate=cost(1),
        name="halve",
    )(keep, got)


def total_kernel(count, *refs):
    feeds, heads, out = refs[:count], refs[count:-1], refs[-1]
    total = feeds[0][...].astype(f32)
    for part in feeds[1:]:
        total = total + part[...].astype(f32)
    out[: total.shape[0]] = keep_scalar(total).astype(bf16)
    if heads:
        at = total.shape[0]
        total = heads[0][...].astype(f32)
        for part in heads[1:]:
            total = total + part[...].astype(f32)
        rows = total.shape[0]
        kept = rows * 3 // 4
        rest = [total[kept:, i * WIDE : (i + 1) * WIDE] for i in range(3)]
        out[at:] = jnp.concatenate([total[:kept], jnp.concatenate(rest, axis=0)], axis=1).astype(bf16)


def total_parts(feeds, heads):
    rows, width = feeds[0].shape
    extra = heads[0].shape[0] * 3 // 4 if heads else 0
    shape = (rows + extra, width)
    return pl.pallas_call(
        functools.partial(total_kernel, len(feeds)),
        grid=(1,),
        in_specs=[full_spec(x) for x in feeds + heads],
        out_specs=pl.BlockSpec(shape, lambda i: (0, 0)),
        out_shape=jax.ShapeDtypeStruct(shape, bf16),
        compiler_params=room(6),
        cost_estimate=cost(1),
        name="total",
    )(*feeds, *heads)


def unpack_kernel(info_ref, *refs):
    pieces = refs[: 2 * PAIRS]
    outer_ref, out_ref, in_ref, tail_ref, *heads = refs[2 * PAIRS :]
    core, pair = info_ref[0], info_ref[2]
    for side in range(2):
        for d in range(PAIRS):
            ref = pieces[side * PAIRS + d]
            place = jnp.bitwise_xor(pair, d) * 2 + jnp.bitwise_xor(core, side)
            at = 0
            for target in (outer_ref, out_ref, in_ref):
                size = target.shape[0] // (2 * PAIRS)
                start = pl.multiple_of(place * size, size)
                target[pl.ds(start, size)] = ref[at : at + size].astype(f32)
                at += size

            @pl.when(place == 0)
            def _(ref=ref, at=at):
                tail_ref[...] = ref[at : at + 8].astype(f32)

            at += 8
            size = heads[0].shape[0] // (2 * PAIRS)
            kept = size * 3 // 4
            for i, target in enumerate(heads):
                start = pl.multiple_of(place * size, size)
                target[pl.ds(start, kept)] = ref[at : at + kept, i * WIDE : (i + 1) * WIDE].astype(f32)
                more = (size - kept) * i + at
                target[pl.ds(start + kept, size - kept)] = ref[more : more + size - kept, 3 * WIDE :].astype(f32)


def unpack(info, mine, other, part, out_rows):
    width = mine[0].shape[1]
    shapes = [(part, width), (out_rows, width), (width, part), (8, width)] + [(width, WIDE)] * 3
    return pl.pallas_call(
        unpack_kernel,
        grid=(1,),
        in_specs=[pl.BlockSpec(memory_space=pltpu.SMEM)] + [full_spec(x) for x in mine + other],
        out_specs=[pl.BlockSpec(shape, lambda i: (0, 0)) for shape in shapes],
        out_shape=[jax.ShapeDtypeStruct(shape, f32) for shape in shapes],
        compiler_params=room(16),
        cost_estimate=cost(3),
        name="unpack",
    )(info, *mine, *other)


def gelu_parts(x):
    half = 0.5 * (1.0 + lax.erf(x * 2.0 ** (-0.5)))
    density = jnp.exp(-0.5 * x * x) * (2.0 * math.pi) ** (-0.5)
    return x * half, half + x * density


def mean_rows(x):
    return jnp.sum(x, axis=1, keepdims=True) * (1.0 / x.shape[1])


def norm_rows(z, gain, shift):
    centre = z - mean_rows(z)
    inverse = lax.rsqrt(mean_rows(centre * centre) + epsilon)
    normed = centre * inverse
    return normed * gain + shift, normed, inverse


def norm_back(g, normed, inverse, gain):
    scaled = g * gain
    return inverse * (scaled - mean_rows(scaled) - normed * mean_rows(scaled * normed))


def dense_kernel(info_ref, bhalt_ref, *refs):
    mine, other, refs = refs[:PAIRS], refs[PAIRS : 2 * PAIRS], refs[2 * PAIRS :]
    att_refs, refs = refs[:PAIRS], refs[PAIRS:]
    emb_ref, prev_ref, gt_ref, gb_ref, scal_ref = refs[:5]
    refs = refs[5:]
    final_ref, blend_ref, rows_ref, gprev_ref, base_ref = refs[:5]
    gatt_refs = refs[5:9]
    nlow_ref, ilow_ref, gin_ref, gfeed_ref, gbranch_ref, vsum_ref, bsum_ref = refs[9:16]
    slope_ref, win_ref, wouter_ref, wout_ref, small_ref, sem = refs[16:]
    blocks, columns, width = win_ref.shape
    cut = wout_ref.shape[1] // 2
    core, zed, pair = info_ref[0], info_ref[1], info_ref[2]

    def load(firsts, seconds):
        copies = []

        def copy(source, start, size, target):
            copies.append(pltpu.make_async_copy(source.at[pl.ds(start, size)], target, sem.at[len(copies)]))

        for a in range(PAIRS):
            place = lax.rem(zed + a, PAIRS)
            order = jnp.bitwise_xor(place, pair)
            first, second = firsts[(-a) % PAIRS], seconds[a]
            copy(first, columns, cut, wout_ref.at[order, pl.ds(0, cut)])
            copy(second, width, cut, wout_ref.at[order, pl.ds(cut, cut)])
            copy(first, columns + cut, SMALL, small_ref.at[place])
            copy(first, 0, columns, win_ref.at[a])
            copy(second, 0, width, wouter_ref.at[a])
        for one in copies:
            one.start()
        for one in copies:
            one.wait()

    @pl.when((pl.program_id(0) == 0) & (core == 0))
    def _():
        load(mine, other)

    @pl.when((pl.program_id(0) == 0) & (core != 0))
    def _():
        load(other, mine)

    emb = emb_ref[0]
    att = jnp.concatenate([ref[0] for ref in att_refs], axis=1)
    w_out = wout_ref[...].reshape(emb.shape[1], emb.shape[1])
    b_outer, g1, s1, g2, s2, halt = [
        jnp.concatenate([small_ref[a, i + 1 : i + 2, :WIDE] for a in range(PAIRS)], axis=1).astype(f32)
        for i in range(6)
    ]
    cols = jnp.transpose(scal_ref[0])
    sum_col, code_col, gsum_col = cols[:, 0:1], cols[:, 1:2], cols[:, 2:3]
    z1 = emb + dot(att, w_out)
    one, n1, i1 = norm_rows(z1, g1, s1)
    nlow = one.astype(bf16)
    nlow_ref[0] = nlow
    feed = None
    for j in range(blocks):
        pre = dot(nlow, win_ref[j]) + small_ref[lax.rem(zed + j, PAIRS), 0:1, :].astype(f32)
        act, slope = gelu_parts(pre)
        act = act.astype(bf16)
        ilow_ref[0, :, j * width : (j + 1) * width] = act
        slope_ref[:, j * width : (j + 1) * width] = slope
        part = dot(act, wouter_ref[j])
        feed = part if feed is None else feed + part
    z2 = one + (feed + b_outer)
    final, n2, i2 = norm_rows(z2, g2, s2)
    halt_logit = jnp.sum(emb * halt, axis=1, keepdims=True) + bhalt_ref[0, 0]
    halt_prob = jax.nn.sigmoid(halt_logit)
    running = (code_col > 0.5).astype(f32)
    halting = (code_col > 1.5).astype(f32)
    update = running * (halting * (1.0 - sum_col) + (1.0 - halting) * halt_prob)
    prev = prev_ref[0].astype(f32)
    gb = gb_ref[0].astype(f32)
    final_ref[0] = final.astype(bf16)
    blend_ref[0] = (prev * (1.0 - update) + final * update).astype(bf16)
    gprev_ref[0] = gb * (1.0 - update)
    g_update = jnp.sum(gb * (final - prev), axis=1, keepdims=True) + gsum_col
    g_halt_sum = gsum_col - running * halting * g_update
    g_logit = g_update * running * (1.0 - halting) * halt_prob * (1.0 - halt_prob)
    lane = lax.broadcasted_iota(jnp.int32, (emb.shape[0], WIDE), 1)
    packed = jnp.where(lane == 0, sum_col + update, jnp.where(lane == 1, g_halt_sum, 0.0))
    rows_ref[0] = jnp.transpose(packed)[0:8]
    gf = gt_ref[0].astype(f32) + update * gb
    g_two = norm_back(gf, n2, i2, g2)
    gfeed = g_two.astype(bf16)
    gfeed_ref[0] = gfeed
    g_one = g_two
    for j in range(blocks):
        at = slice(j * width, (j + 1) * width)
        back = dot(gfeed, wouter_ref[j], NT)
        gin_f = back * slope_ref[:, at]
        gin = gin_f.astype(bf16)
        gin_ref[0, :, at] = gin
        bsum_ref[0, :, at] = jnp.sum(gin.astype(f32), axis=0, keepdims=True)
        g_one = g_one + dot(gin, win_ref[j], NT)
    g_emb = norm_back(g_one, n1, i1, g1)
    gbranch = g_emb.astype(bf16)
    gbranch_ref[0] = gbranch
    gatt = dot(gbranch, w_out, NT).astype(bf16)
    for d, ref in enumerate(gatt_refs):
        ref[0] = gatt[:, d * WIDE : (d + 1) * WIDE]
    base_ref[0] = g_emb + g_logit * halt
    total = lambda x: jnp.sum(x, axis=0, keepdims=True)
    logit_sum = jnp.broadcast_to(total(g_logit), (1, emb.shape[1]))
    vsum_ref[0] = jnp.concatenate(
        [
            total(gfeed.astype(f32)),
            total(g_one * n1),
            total(g_one),
            total(gf * n2),
            total(gf),
            total(g_logit * emb),
            logit_sum,
            jnp.zeros((1, emb.shape[1]), f32),
        ],
        axis=0,
    )


def dense(info, b_halt, mine, other, emb, att, prev, gt, gb, scal, part, out_rows):
    seqs, rows, width = emb.shape
    hidden = PAIRS * part
    anywhere = pl.BlockSpec(memory_space=pl.ANY)
    scalars = pl.BlockSpec(memory_space=pltpu.SMEM)
    rowspec = lambda w: pl.BlockSpec((1, rows, w), lambda s: (s, 0, 0))
    shape = lambda w, kind: jax.ShapeDtypeStruct((seqs, rows, w), kind)
    return pl.pallas_call(
        dense_kernel,
        grid=(seqs,),
        in_specs=[scalars, scalars]
        + [anywhere] * (2 * PAIRS)
        + [rowspec(WIDE)] * PAIRS
        + [
            rowspec(width),
            rowspec(width),
            rowspec(width),
            rowspec(width),
            pl.BlockSpec((1, 8, rows), lambda s: (s, 0, 0)),
        ],
        out_specs=[
            rowspec(width),
            rowspec(width),
            pl.BlockSpec((1, 8, rows), lambda s: (s, 0, 0)),
            rowspec(width),
            rowspec(width),
            rowspec(WIDE),
            rowspec(WIDE),
            rowspec(WIDE),
            rowspec(WIDE),
            rowspec(width),
            rowspec(hidden),
            rowspec(hidden),
            rowspec(width),
            rowspec(width),
            pl.BlockSpec((1, 8, width), lambda s: (s, 0, 0)),
            pl.BlockSpec((1, 1, hidden), lambda s: (s, 0, 0)),
        ],
        out_shape=[
            shape(width, bf16),
            shape(width, bf16),
            jax.ShapeDtypeStruct((seqs, 8, rows), f32),
            shape(width, f32),
            shape(width, f32),
            shape(WIDE, bf16),
            shape(WIDE, bf16),
            shape(WIDE, bf16),
            shape(WIDE, bf16),
            shape(width, bf16),
            shape(hidden, bf16),
            shape(hidden, bf16),
            shape(width, bf16),
            shape(width, bf16),
            jax.ShapeDtypeStruct((seqs, 8, width), f32),
            jax.ShapeDtypeStruct((seqs, 1, hidden), f32),
        ],
        scratch_shapes=[
            pltpu.VMEM((rows, hidden), f32),
            pltpu.VMEM((PAIRS, width, part), bf16),
            pltpu.VMEM((PAIRS, part, width), bf16),
            pltpu.VMEM((PAIRS, out_rows, width), bf16),
            pltpu.VMEM((PAIRS, SMALL, width), bf16),
            pltpu.SemaphoreType.DMA((5 * PAIRS,)),
        ],
        compiler_params=room(56),
        cost_estimate=cost(20),
        name="dense",
    )(info, b_halt, *mine, *other, *att, emb, prev, gt, gb, scal)


def frequencies(half):
    return jnp.exp(-math.log(10000.0) * jnp.arange(half, dtype=f32) / (half - 1))


def position_rows(first, rows, columns):
    half = columns // 2
    freq = frequencies(half)[None, :]
    coarse = (first + 16 * jnp.arange(rows // 16, dtype=jnp.int32)).astype(f32)[:, None] * freq
    fine = jnp.arange(16, dtype=f32)[:, None] * freq
    sa, ca = jnp.sin(coarse)[:, None], jnp.cos(coarse)[:, None]
    sb, cb = jnp.sin(fine)[None], jnp.cos(fine)[None]
    both = jnp.concatenate([sa * cb + ca * sb, ca * cb - sa * sb], axis=2)
    return both.reshape(rows, columns)


def step_rows(columns):
    half = columns // 2
    angles = jnp.arange(4, dtype=f32)[:, None] * frequencies(half)[None, :]
    return jnp.concatenate([jnp.sin(angles), jnp.cos(angles)], axis=1)


def body(
    hidden_state,
    prev_state,
    halt_sum,
    halt_code,
    step_count,
    w_query,
    w_key,
    w_value,
    w_out,
    w_inner,
    b_inner,
    w_outer,
    b_outer,
    gain_attention,
    shift_attention,
    gain_feedforward,
    shift_feedforward,
    w_halt,
    b_halt,
    grad_transformed,
    grad_blended,
    grad_sum,
):
    seqs, rows, width = hidden_state.shape
    ctx = lax.axis_size("ctx")
    wsh = lax.axis_size("wsh")
    repeats = ctx // (2 * PAIRS)
    me = lax.axis_index("ctx")
    zed = lax.axis_index("wsh")
    core = me % 2
    pair = (me // 2) % PAIRS

    def swap(x, distance):
        return lax.ppermute(x, "ctx", [(i, i ^ distance) for i in range(ctx)])

    def sibling(x):
        return swap(x, 1)

    def partners(x, distance):
        return swap(x, 2 * distance)

    freq_rows = position_rows(me * rows, rows, width)
    table = step_rows(width)
    steps = step_count[:, :, None]
    step_signal = jnp.where(
        steps == 0, table[0], jnp.where(steps == 1, table[1], jnp.where(steps == 2, table[2], table[3]))
    )
    emb = hidden_state.astype(f32) + freq_rows[None] + step_signal
    emb_low = emb.astype(bf16)

    after = lambda x, *others: lax.optimization_barrier((x,) + others)[0]

    info = jnp.stack([core, zed, pair]).astype(jnp.int32)
    ring = [
        (c * wsh + z, c * wsh + (z + (1 if c % 2 == 0 else -1)) % wsh) for c in range(ctx) for z in range(wsh)
    ]
    turn = lambda x: lax.ppermute(x, ("ctx", "wsh"), ring)
    out_rows = w_out.shape[0]
    part = w_inner.shape[1]
    half = rows // 2

    mine = [pack(info, [w_query, w_key, w_value])]
    mine.append(turn(mine[0]))
    mine.append(turn(after(mine[1], emb_low)))
    tokens = [emb_low] + [partners(emb_low, d) for d in (1, 2)]
    mine.append(turn(after(mine[2], *tokens[1:])))
    tokens.append(partners(tokens[2][:, :half], 1))
    tokens.append(partners(tokens[1][:, half:], 2))
    other = [sibling(x) for x in mine]
    vectors = [b_outer, gain_attention, shift_attention, gain_feedforward, shift_feedforward, w_halt]
    feed = pack_feed(after(info, mine[0]), w_inner, w_outer, w_out, b_inner, vectors)
    feed_mine = [feed, turn(after(feed, mine[1]))]
    w_order = assemble(after(info, feed_mine[1]), mine, other)

    groups = [[r * 2 * PAIRS + i for r in range(repeats)] for i in range(2 * PAIRS)]
    q_list, kvs_list, fold = [], [], None
    w_now = w_order
    for s in range(seqs):
        q, own = project(s, tokens, w_now)
        w_now = after(w_order, q)
        other = sibling(own)
        if repeats == 1:
            kvs = [own, other]
        else:
            both = jnp.concatenate([own, other], axis=1)
            kvs = [lax.all_gather(both, "ctx", axis=1, tiled=True, axis_index_groups=groups)]
        q_list.append(q)
        kvs_list.append(kvs)
    feed_mine.append(turn(after(feed_mine[1], q_list[0])))
    feed_other = [sibling(after(x, q_list[0])) for x in feed_mine[:2]]
    fold = attend(0, seqs, q_list[0], kvs_list[0], None)
    fold = attend(1, seqs, after(q_list[1], *feed_other, fold[1]), kvs_list[1], fold)
    feed_mine.append(turn(after(feed_mine[2], fold[1])))
    fold = attend(2, seqs, after(q_list[2], feed_mine[2]), kvs_list[2], fold)
    feed_other += [sibling(after(x, fold[1])) for x in feed_mine[2:]]
    o32, mass, *low = fold
    att = [low[0]] + [partners(low[d], d) for d in range(1, PAIRS)]

    zero_row = jnp.zeros_like(halt_sum)
    scal = jnp.stack([halt_sum, halt_code.astype(f32), grad_sum] + [zero_row] * 5, axis=1)
    (
        final,
        blended,
        row_out,
        grad_prev,
        base,
        gatt0,
        gatt1,
        gatt2,
        gatt3,
        nlow,
        ilow,
        gin,
        gfeed,
        gbranch,
        vsum,
        bsum,
    ) = dense(
        info, b_halt.reshape(1, 1), feed_mine, feed_other, emb, att, prev_state, grad_transformed, grad_blended,
        scal, part, out_rows,
    )
    new_sum = row_out[:, 0]
    grad_halt_sum = row_out[:, 1]
    gs = [gatt0] + [partners(x, d + 1) for d, x in enumerate((gatt1, gatt2, gatt3))]

    keep_a, give_a = outer_grads(info, att, ilow, gfeed, gbranch, ctx)
    keep_b, give_b = inner_grads(after(info, keep_a), nlow, gin, vsum, bsum, ctx)
    joined_a = join(after(keep_a, keep_b), sibling(give_a), False)

    def spread_pieces(pieces):
        return [pieces[0]] + [partners(pieces[d], d) for d in range(1, PAIRS)]

    shared_a = spread_pieces(joined_a)

    kinds = [f32, bf16] if repeats == 1 else [bf16]

    def split_back(s, token):
        dq, *dkv = attend_back(s, q_list[s], gs, o32, token, kvs_list[s], kinds)
        if repeats == 1:
            kept, sent = dkv
        else:
            summed = lax.psum_scatter(
                dkv[0], "ctx", scatter_dimension=1, tiled=True, axis_index_groups=groups
            )
            kept, sent = summed[:, : PAIRS * rows].astype(f32), summed[:, PAIRS * rows :]
        return dq, kept, sibling(sent)

    backs = [split_back(0, after(mass, *joined_a))]
    joined_b = join(after(keep_b, backs[0][0], *shared_a), sibling(give_b), True)
    shared_b = spread_pieces(joined_b)
    backs.append(split_back(1, after(mass, *joined_b)))
    *pieces, gq = combine(after(info, backs[1][0], *shared_b), (0,), tokens, backs[:1], None, False)
    blocks = [spread_pieces(pieces)]
    share_keep, share_send = share_parts(after(info, gq), shared_a, shared_b)
    if repeats > 1:
        share_keep, share_send = (
            lax.psum_scatter(x, "ctx", scatter_dimension=0, tiled=True, axis_index_groups=groups)
            for x in (share_keep, share_send)
        )
    cross = lambda x, step: lax.ppermute(x, "wsh", [(z, z ^ step) for z in range(wsh)])
    moved = cross(share_send[0], 1)
    backs.append(split_back(2, after(mass, share_keep)))
    own, sent = halve(after(share_keep[0], backs[2][0], *blocks[0]), moved)
    moved = cross(sent, 2)
    made = combine(after(info, own), (1, 2), tokens, backs[1:], gq, repeats == 1)
    pieces, keep, give = made[:PAIRS], made[PAIRS], made[-1]
    block = [pieces[0]] + [partners(pieces[d], d) for d in (1, 2)]
    if repeats == 1:
        heads = share_small(after(info, moved, *block), spread_pieces(join_small(keep, sibling(give))))
        block.append(partners(after(pieces[3], heads[0]), 3))
        heads = [heads[0]] + [cross(heads[step], step) for step in range(1, wsh)]
        share = total_parts([own, moved], heads)
        mine = spread_pieces([share] * PAIRS)
        (grad_w_outer, grad_w_out, grad_w_inner, tail, grad_w_query, grad_w_key, grad_w_value) = unpack(
            info, mine, [sibling(x) for x in mine], part, out_rows
        )
    else:
        block.append(partners(pieces[3], 3))
        share = total_parts([own, moved], [])
        whole = lax.all_gather(share, "ctx", axis=0).astype(f32)
        a, b, c = part // ctx, out_rows // ctx, width // ctx
        grad_w_outer = whole[:, :a].reshape(part, width)
        grad_w_out = whole[:, a : a + b].reshape(out_rows, width)
        grad_w_inner = whole[:, a + b : a + b + c].reshape(width, part)
        tail = whole[0, a + b + c :]
        own = lax.dynamic_update_index_in_dim(jnp.zeros((wsh,) + keep.shape, f32), keep, pair, 0)
        own = lax.psum(lax.psum_scatter(own.astype(bf16), "wsh", scatter_dimension=0).astype(f32), "ctx")
        grad_w_query, grad_w_key, grad_w_value = (own[:, i * WIDE : (i + 1) * WIDE] for i in range(3))
    blocks.append(block)
    grad_state = base
    for s in range(seqs):
        block, place = (blocks[0], 0) if s == 0 else (blocks[1], s - 1)
        grad_state = add_state(s, place, grad_state, block, w_order)

    grad_b_inner = tail[7]
    vec_grads = [tail[i, :out_rows] for i in range(6)]
    grad_b_halt = tail[6, :1] + tail[6, WIDE : WIDE + 1]

    return (
        final,
        blended,
        new_sum,
        grad_state,
        grad_prev,
        grad_halt_sum,
        grad_w_query,
        grad_w_key,
        grad_w_value,
        grad_w_out,
        grad_w_inner,
        grad_b_inner,
        grad_w_outer,
        vec_grads[0],
        vec_grads[1],
        vec_grads[2],
        vec_grads[3],
        vec_grads[4],
        vec_grads[5],
        grad_b_halt,
    )


def solution(mesh):
    rows = P("wsh", "ctx", None)
    marks = P("wsh", "ctx")
    column, row, vector = P(None, "wsh"), P("wsh", None), P("wsh")
    in_specs = (
        (rows, rows, marks, marks, marks, column, column, column, row, column, vector, row)
        + (vector,) * 6
        + (P(), rows, rows, marks)
    )
    out_specs = (
        (rows, rows, marks, rows, rows, marks, column, column, column, row, column, vector, row)
        + (vector,) * 6
        + (P(),)
    )
    return jax.shard_map(body, mesh=mesh, in_specs=in_specs, out_specs=out_specs, check_vma=False)
```

```python
import functools
import math

import jax
import jax.numpy as jnp
from jax import lax
from jax.experimental import pallas as pl
from jax.experimental.pallas import tpu as pltpu
from jax.sharding import PartitionSpec as P

HEADS = 8
PAIRS = 4
WIDE = 128
SMALL = 16
epsilon = 1e-06
f32 = jnp.float32
bf16 = jnp.bfloat16
LOG2E = math.log2(math.e)
NT = (((1,), (1,)), ((), ()))
TN = (((0,), (0,)), ((), ()))
NN = (((1,), (0,)), ((), ()))
MIB = 1024 * 1024
KEYS = 256


def room(mebibytes):
    return pltpu.CompilerParams(vmem_limit_bytes=int(mebibytes) * MIB)


def cost(micros):
    return pl.CostEstimate(flops=int(micros * 1.1e9), bytes_accessed=1024, transcendentals=0)


def dot(a, b, dims=NN):
    return lax.dot_general(a, b, dims, preferred_element_type=f32)


def lane_masks(shape):
    lane = lax.broadcasted_iota(jnp.int32, shape, 1)
    return lane < WIDE // 2


def largest_squares(refs):
    same = (
        lax.broadcasted_iota(jnp.int32, (WIDE, WIDE), 0) // (WIDE // 2)
        == lax.broadcasted_iota(jnp.int32, (WIDE, WIDE), 1) // (WIDE // 2)
    ).astype(bf16)
    most = None
    for ref in refs:
        for start in range(0, ref.shape[1], 1024):
            x = ref[0, start : start + 1024, :WIDE].astype(f32)
            top = jnp.max(dot((x * x).astype(bf16), same), axis=0, keepdims=True)
            most = top if most is None else jnp.maximum(most, top)
    return most


def attend_kernel(blocks, carried, q_ref, *refs):
    kv_refs = refs[:blocks]
    refs = refs[blocks + carried :]
    flag_ref = refs[-1]
    o_ref, mass_ref, low_refs = refs[0], refs[1], refs[2:-1]
    scale = 0.125 * LOG2E
    index = pl.program_id(0)
    step = o_ref.shape[1]

    @pl.when(index == 0)
    def _():
        bound = jnp.max(largest_squares([q_ref]) * largest_squares(kv_refs))
        flag_ref[0] = (bound < 0.98 * (8.0 * 70.0) ** 2).astype(jnp.int32)

    q = q_ref[0, pl.ds(pl.multiple_of(index * step, step), step)]
    first = lane_masks(q.shape)
    none = jnp.zeros_like(q)
    size = KEYS
    chunks = [(ref, start) for ref in kv_refs for start in range(0, ref.shape[1], size)]

    def run(shifted):
        outs, masses = [], []
        for head in range(2):
            mine = jnp.where(first, q, none) if head == 0 else jnp.where(first, none, q)
            score = lambda chunk: dot(mine, chunk[0][0, chunk[1] : chunk[1] + size, :WIDE], NT)
            lift = None
            if shifted:
                scores = [score(chunk) for chunk in chunks]
                lift = jnp.max(functools.reduce(jnp.maximum, scores), axis=1, keepdims=True) * scale
            total = None
            weighted = None
            for i, (ref, start) in enumerate(chunks):
                e = jnp.exp2(scores[i] * scale - lift) if shifted else jnp.exp2(score((ref, start)) * scale)
                part = sum(e[:, i : i + 128] for i in range(0, size, 128))
                total = part if total is None else total + part
                w = dot(e.astype(bf16), ref[0, start : start + size, WIDE:])
                weighted = w if weighted is None else weighted + w
            total = jnp.sum(total, axis=1, keepdims=True)
            outs.append(weighted * (1.0 / total))
            masses.append(lift + jnp.log2(total) if shifted else jnp.log2(total))
        out = jnp.where(first, outs[0], outs[1])
        o_ref[0] = out
        low = out.astype(bf16)
        block = low_refs[0].shape[1]
        for d, ref in enumerate(low_refs):

            @pl.when(index == d * block // step)
            def _(ref=ref, at=d * block % step):
                ref[0] = low[at : at + block]

        table = jnp.where(first, masses[0], masses[1])
        turned = jnp.transpose(table)
        mass_ref[0] = jnp.concatenate([turned[0:4], turned[64:68]], axis=0)

    @pl.when(flag_ref[0] == 1)
    def _():
        run(False)

    @pl.when(flag_ref[0] != 1)
    def _():
        run(True)


def attend(at, seqs, q, kvs, before):
    _, rows, _ = q.shape
    block = rows // PAIRS
    keys = sum(kv.shape[1] for kv in kvs)
    step = 2 * block if keys <= 2048 else block
    shapes = [
        jax.ShapeDtypeStruct((seqs, rows, WIDE), f32),
        jax.ShapeDtypeStruct((seqs, 8, rows), f32),
    ] + [jax.ShapeDtypeStruct((seqs, block, WIDE), bf16)] * PAIRS
    carried = len(shapes) if before else 0
    return pl.pallas_call(
        functools.partial(attend_kernel, len(kvs), carried),
        grid=(rows // step,),
        in_specs=[full_spec(q)]
        + [full_spec(kv) for kv in kvs]
        + [pl.BlockSpec(memory_space=pl.ANY)] * carried,
        out_specs=[
            pl.BlockSpec((1, step, WIDE), lambda i: (at, i, 0)),
            pl.BlockSpec((1, 8, step), lambda i: (at, 0, i)),
        ]
        + [pl.BlockSpec((1, block, WIDE), lambda i: (at, 0, 0))] * PAIRS,
        out_shape=shapes,
        input_output_aliases={1 + len(kvs) + i: i for i in range(carried)},
        scratch_shapes=[pltpu.SMEM((1,), jnp.int32)],
        compiler_params=room(24 if keys <= 2048 else 10 + keys // 256),
        cost_estimate=cost(4),
        name="attend",
    )(q, *kvs, *(before or ()))


def attend_back_kernel(blocks, q_ref, *refs):
    g_refs, o_ref, mass_ref = refs[:PAIRS], refs[PAIRS], refs[PAIRS + 1]
    refs = refs[PAIRS + 2 :]
    kv_refs = refs[:blocks]
    dq_ref = refs[blocks]
    dkv_refs = refs[blocks + 1 : 2 * blocks + 1]
    dq_acc = refs[2 * blocks + 1]
    scale = 0.125 * LOG2E
    q = q_ref[0]
    g = jnp.concatenate([ref[0] for ref in g_refs], axis=0)
    first = lane_masks(q.shape)
    none = jnp.zeros_like(q)
    qs = [jnp.where(first, q, none), jnp.where(first, none, q)]
    gs = [jnp.where(first, g, none), jnp.where(first, none, g)]
    product = g.astype(f32) * o_ref[0]
    which = lax.broadcasted_iota(jnp.int32, (8, WIDE), 0) == (
        lax.broadcasted_iota(jnp.int32, (8, WIDE), 1) // (WIDE // 2)
    )
    deltas = lax.dot_general(
        which.astype(f32), product, NT, precision=lax.Precision.HIGHEST, preferred_element_type=f32
    )
    delta = [deltas[0:1], deltas[1:2]]
    mass = [mass_ref[0, 0:1, :], mass_ref[0, 4:5, :]]
    dq_acc[...] = jnp.zeros_like(dq_acc)
    size = 256
    key_first = lane_masks((size, WIDE))
    key_none = jnp.zeros((size, WIDE), bf16)

    for kv_ref, dkv_ref in zip(kv_refs, dkv_refs):

        def chunk(i, carry, kv_ref=kv_ref, dkv_ref=dkv_ref):
            at = pl.ds(pl.multiple_of(i * size, size), size)
            k = kv_ref[0, at, :WIDE]
            v = kv_ref[0, at, WIDE:]
            dk = dv = dq = None
            for head in range(2):
                s = dot(k, qs[head], NT)
                p = jnp.exp2(s * scale - mass[head])
                dp = dot(v, gs[head], NT)
                ds = (p * (dp - delta[head])).astype(bf16)
                own_v = dot(p.astype(bf16), gs[head])
                own_k = dot(ds, qs[head])
                km = jnp.where(key_first, k, key_none) if head == 0 else jnp.where(key_first, key_none, k)
                own_q = dot(ds, km, TN)
                dv = own_v if dv is None else dv + own_v
                dk = own_k if dk is None else dk + own_k
                dq = own_q if dq is None else dq + own_q
            dkv_ref[0, at, :WIDE] = (dk * 0.125).astype(dkv_ref.dtype)
            dkv_ref[0, at, WIDE:] = dv.astype(dkv_ref.dtype)
            dq_acc[...] += dq
            return carry

        lax.fori_loop(0, kv_ref.shape[1] // size, chunk, 0, unroll=4)
    dq_ref[0] = (dq_acc[...] * 0.125).astype(bf16)


def attend_back(at, q, gs, o, mass, kvs, kinds):
    _, rows, _ = q.shape
    keys = sum(kv.shape[1] for kv in kvs)
    own = gs[0].shape[1]
    whole = lambda width: pl.BlockSpec((1, rows, width), lambda s: (0, 0, 0))
    kv_specs = [pl.BlockSpec((1, kv.shape[1], 2 * WIDE), lambda s: (0, 0, 0)) for kv in kvs]
    return pl.pallas_call(
        functools.partial(attend_back_kernel, len(kvs)),
        grid=(1,),
        in_specs=[whole(WIDE)]
        + [pl.BlockSpec((1, own, WIDE), lambda s: (at, 0, 0))] * PAIRS
        + [pl.BlockSpec((1, rows, WIDE), lambda s: (at, 0, 0)), pl.BlockSpec((1, 8, rows), lambda s: (at, 0, 0))]
        + kv_specs,
        out_specs=[whole(WIDE)] + kv_specs,
        out_shape=[jax.ShapeDtypeStruct((1, rows, WIDE), bf16)]
        + [jax.ShapeDtypeStruct(kv.shape, kind) for kv, kind in zip(kvs, kinds)],
        scratch_shapes=[pltpu.VMEM((rows, WIDE), f32)],
        compiler_params=room(14 + keys // 512),
        cost_estimate=cost(14),
        name="attend_back",
    )(q, *gs, o, mass, *kvs)


def full_spec(array):
    return pl.BlockSpec(array.shape, lambda *_: (0,) * array.ndim)


def pack_kernel(info_ref, *refs):
    parts, out_ref = refs[:-1], refs[-1]
    core = info_ref[0]
    half = out_ref.shape[0]

    @pl.when(core == 0)
    def _():
        out_ref[...] = jnp.concatenate([ref[:half] for ref in parts], axis=1)

    @pl.when(core != 0)
    def _():
        out_ref[...] = jnp.concatenate([ref[half:] for ref in parts], axis=1)


def pack(info, parts):
    rows, width = parts[0].shape
    shape = (rows // 2, len(parts) * width)
    return pl.pallas_call(
        pack_kernel,
        grid=(1,),
        in_specs=[pl.BlockSpec(memory_space=pltpu.SMEM)] + [full_spec(x) for x in parts],
        out_specs=pl.BlockSpec(shape, lambda i: (0, 0)),
        out_shape=jax.ShapeDtypeStruct(shape, bf16),
        compiler_params=room(6),
        cost_estimate=cost(1),
        name="pack",
    )(info, *parts)


def pack_feed_kernel(info_ref, inner_ref, outer_ref, wout_ref, bias_ref, *refs):
    vectors, out_ref = refs[:-1], refs[-1]
    core = info_ref[0]
    width = inner_ref.shape[0]
    cut = wout_ref.shape[0] // 2

    @pl.when(core == 0)
    def _():
        out_ref[:width] = inner_ref[...]
        out_ref[width : width + cut] = wout_ref[:cut]

    @pl.when(core != 0)
    def _():
        out_ref[:width] = outer_ref[...]
        out_ref[width : width + cut] = wout_ref[cut:]

    row = lax.broadcasted_iota(jnp.int32, (SMALL, WIDE), 0)
    table = jnp.zeros((SMALL, WIDE), f32)
    for i, ref in enumerate(vectors):
        table = jnp.where(row == i + 1, ref[...].astype(f32), table)
    row = lax.broadcasted_iota(jnp.int32, (SMALL, width), 0)
    table = jnp.concatenate([table, jnp.zeros((SMALL, width - WIDE), f32)], axis=1)
    table = jnp.where(row == 0, bias_ref[...].astype(f32), table)
    out_ref[width + cut :] = table.astype(bf16)


def pack_feed(info, w_inner, w_outer, w_out, b_inner, vectors):
    width = w_inner.shape[0]
    parts = [w_inner, w_outer, w_out, b_inner.reshape(1, -1)] + [v.reshape(1, -1) for v in vectors]
    shape = (width + w_out.shape[0] // 2 + SMALL, w_out.shape[1])
    return pl.pallas_call(
        pack_feed_kernel,
        grid=(1,),
        in_specs=[pl.BlockSpec(memory_space=pltpu.SMEM)] + [full_spec(x) for x in parts],
        out_specs=pl.BlockSpec(shape, lambda i: (0, 0)),
        out_shape=jax.ShapeDtypeStruct(shape, bf16),
        compiler_params=room(10),
        cost_estimate=cost(2),
        name="pack_feed",
    )(info, *parts)


def project_kernel(count, *refs):
    blocks, w_ref, q_ref, kv_ref = refs[:count], refs[count], refs[count + 1], refs[count + 2]
    at = 0
    for ref in blocks:
        rows = ref.shape[1]
        made = dot(ref[0], w_ref[...]).astype(bf16)
        q_ref[0, at : at + rows] = made[:, :WIDE]
        kv_ref[0, at : at + rows] = made[:, WIDE:]
        at += rows


def project(at, tokens, w_mine):
    total = sum(x.shape[1] for x in tokens)
    return pl.pallas_call(
        functools.partial(project_kernel, len(tokens)),
        grid=(1,),
        in_specs=[pl.BlockSpec((1,) + x.shape[1:], lambda i: (at, 0, 0)) for x in tokens]
        + [full_spec(w_mine)],
        out_specs=[
            pl.BlockSpec((1, total, WIDE), lambda i: (0, 0, 0)),
            pl.BlockSpec((1, total, 2 * WIDE), lambda i: (0, 0, 0)),
        ],
        out_shape=[
            jax.ShapeDtypeStruct((1, total, WIDE), bf16),
            jax.ShapeDtypeStruct((1, total, 2 * WIDE), bf16),
        ],
        compiler_params=room(10),
        cost_estimate=cost(1),
        name="project",
    )(*tokens, w_mine)


def combine_kernel(chosen, count, prior, final, info_ref, *refs):
    blocks, refs = refs[:count], refs[count:]
    backs, refs = refs[: 3 * len(chosen)], refs[3 * len(chosen) :]
    grad = None
    if prior:
        grad, refs = refs[0][...], refs[1:]
    outs, grad_refs = refs[:PAIRS], refs[PAIRS:]
    rows = outs[0].shape[1]
    for i, s in enumerate(chosen):
        dq_ref, kept_ref, got_ref = backs[3 * i : 3 * i + 3]
        at = 0
        for ref in blocks:
            size = ref.shape[1]
            part = slice(at, at + size)
            dkv = (kept_ref[0, part] + got_ref[0, part].astype(f32)).astype(bf16)
            piece = jnp.concatenate([dq_ref[0, part], dkv], axis=1)
            outs[at // rows][i, at % rows : at % rows + size] = piece
            term = dot(ref[s], piece, TN)
            grad = term if grad is None else grad + term
            at += size
    if not final:
        grad_refs[0][...] = grad
        return
    size = grad.shape[0] // (2 * PAIRS)

    def write(even_ref, odd_ref):
        for c in range(2 * PAIRS):
            ref = even_ref if c % 2 == 0 else odd_ref
            ref[jnp.bitwise_xor(c // 2, info_ref[2])] = grad[c * size : (c + 1) * size].astype(ref.dtype)

    @pl.when(info_ref[0] == 0)
    def _():
        write(grad_refs[0], grad_refs[1])

    @pl.when(info_ref[0] != 0)
    def _():
        write(grad_refs[1], grad_refs[0])


def combine(info, chosen, tokens, backs, prior, final):
    _, rows, width = tokens[0].shape
    flat = [x for back in backs for x in back]
    extra = [] if prior is None else [prior]
    if final:
        shape = (PAIRS, width // (2 * PAIRS), 3 * WIDE)
        grads = [jax.ShapeDtypeStruct(shape, f32), jax.ShapeDtypeStruct(shape, bf16)]
    else:
        grads = [jax.ShapeDtypeStruct((width, 3 * WIDE), f32)]
    pieces = [jax.ShapeDtypeStruct((len(chosen), rows, 3 * WIDE), bf16)] * PAIRS
    return pl.pallas_call(
        functools.partial(combine_kernel, chosen, len(tokens), len(extra), final),
        grid=(1,),
        in_specs=[pl.BlockSpec(memory_space=pltpu.SMEM)] + [full_spec(x) for x in tokens + flat + extra],
        out_specs=[full_spec(x) for x in pieces + grads],
        out_shape=pieces + grads,
        compiler_params=room(20),
        cost_estimate=cost(2),
        name="combine",
    )(info, *tokens, *flat, *extra)


def join_small_kernel(keep_ref, got_ref, *outs):
    for d, out in enumerate(outs):
        out[...] = (keep_ref[d] + got_ref[d].astype(f32)).astype(bf16)


def join_small(keep, got):
    return pl.pallas_call(
        join_small_kernel,
        grid=(1,),
        in_specs=[full_spec(keep), full_spec(got)],
        out_specs=[pl.BlockSpec(keep.shape[1:], lambda i: (0, 0))] * PAIRS,
        out_shape=[jax.ShapeDtypeStruct(keep.shape[1:], bf16)] * PAIRS,
        compiler_params=room(6),
        cost_estimate=cost(1),
        name="join_small",
    )(keep, got)


def pack_heads(total):
    kept = total.shape[0] * 3 // 4
    rest = [total[kept:, i * WIDE : (i + 1) * WIDE] for i in range(3)]
    return jnp.concatenate([total[:kept], jnp.concatenate(rest, axis=0)], axis=1)


def share_small_kernel(info_ref, feed_ref, *refs):
    parts, outs = refs[:PAIRS], refs[PAIRS:]
    for step, out in enumerate(outs):
        at = jnp.bitwise_xor(jnp.bitwise_xor(info_ref[1], info_ref[2]), step)
        value = parts[0][...]
        for d in range(1, PAIRS):
            value = jnp.where(at == d, parts[d][...], value)
        value = pack_heads(value)
        if step == 2:
            rows = feed_ref.shape[0]
            out[:rows] = feed_ref[...]
            out[rows:] = value
        else:
            out[...] = value


def share_small(info, feed, parts):
    small = (parts[0].shape[0] * 3 // 4, feed.shape[1])
    large = (small[0] + feed.shape[0], feed.shape[1])
    shapes = [small, small, large, small]
    return pl.pallas_call(
        share_small_kernel,
        grid=(1,),
        in_specs=[pl.BlockSpec(memory_space=pltpu.SMEM)] + [full_spec(x) for x in [feed] + parts],
        out_specs=[pl.BlockSpec(shape, lambda i: (0, 0)) for shape in shapes],
        out_shape=[jax.ShapeDtypeStruct(shape, bf16) for shape in shapes],
        compiler_params=room(6),
        cost_estimate=cost(1),
        name="share_small",
    )(info, feed, *parts)


def state_kernel(base_ref, *refs):
    blocks, weights, out_ref = refs[:PAIRS], refs[PAIRS : 2 * PAIRS], refs[2 * PAIRS]
    total = base_ref[0]
    for ref, w_ref in zip(blocks, weights):
        total = total + dot(ref[0], w_ref[...], NT)
    out_ref[0] = total


def add_state(at, base, blocks, weights):
    rows, width = base.shape[1:]
    count = blocks[0].shape[0]
    spec = pl.BlockSpec((1, rows, width), lambda i: (at + i, 0, 0))
    return pl.pallas_call(
        state_kernel,
        grid=(count,),
        in_specs=[spec]
        + [pl.BlockSpec((1,) + b.shape[1:], lambda i: (i, 0, 0)) for b in blocks]
        + [full_spec(w) for w in weights],
        out_specs=spec,
        out_shape=jax.ShapeDtypeStruct(base.shape, base.dtype),
        input_output_aliases={0: 0},
        compiler_params=room(10),
        cost_estimate=cost(2.5 * count),
        name="add_state",
    )(base, *blocks, *weights)


def choose_kernel(info_ref, own_ref, *refs):
    parts, out_ref = refs[:-1], refs[-1]
    got = parts[0][...]
    for part in parts[1:]:
        got = got + part[...]
    out_ref[...] = jnp.where(info_ref[1] == info_ref[2], own_ref[...], got)


def choose(info, own, parts):
    return pl.pallas_call(
        choose_kernel,
        grid=(1,),
        in_specs=[pl.BlockSpec(memory_space=pltpu.SMEM)] + [full_spec(x) for x in [own] + parts],
        out_specs=full_spec(own),
        out_shape=jax.ShapeDtypeStruct(own.shape, bf16),
        compiler_params=room(6),
        cost_estimate=cost(1),
        name="choose",
    )(info, own, *parts)


def assemble_kernel(info_ref, mine_ref, other_ref, out_ref):
    half = mine_ref.shape[0]
    out_ref[:half] = jnp.where(info_ref[0] == 0, mine_ref[...], other_ref[...])
    out_ref[half:] = jnp.where(info_ref[0] == 0, other_ref[...], mine_ref[...])


def assemble(info, mine, other):
    shape = (2 * mine.shape[0], mine.shape[1])
    return pl.pallas_call(
        assemble_kernel,
        grid=(1,),
        in_specs=[pl.BlockSpec(memory_space=pltpu.SMEM), full_spec(mine), full_spec(other)],
        out_specs=pl.BlockSpec(shape, lambda i: (0, 0)),
        out_shape=jax.ShapeDtypeStruct(shape, bf16),
        compiler_params=room(6),
        cost_estimate=cost(1),
        name="assemble",
    )(info, mine, other)


def keep_scalar(block):
    tail = block[-8:]
    total = tail[:, :WIDE] + tail[:, WIDE : 2 * WIDE]
    high = total.astype(bf16).astype(f32)
    split = jnp.concatenate([high, total - high, tail[:, 2 * WIDE :]], axis=1)
    row = lax.broadcasted_iota(jnp.int32, tail.shape, 0)
    tail = jnp.where(row == 6, split, tail)
    return tail if block.shape[0] == 8 else jnp.concatenate([block[:-8], tail], axis=0)


def flat_rows(ref):
    return ref[...].reshape(-1, ref.shape[-1])


def write_pieces(info_ref, even_ref, odd_ref, grads, small):
    pieces = 2 * PAIRS * even_ref.shape[1]

    def write(keep_ref, give_ref):
        for c in range(pieces):
            ref = keep_ref if c % 2 == 0 else give_ref
            order = jnp.bitwise_xor((c // 2) % PAIRS, info_ref[2])
            repeat = c // (2 * PAIRS)
            at = 0
            for grad in grads:
                size = grad.shape[0] // pieces
                ref[order, repeat, 0, at : at + size] = grad[c * size : (c + 1) * size]
                at += size
            if small is not None:
                ref[order, repeat, 0, at : at + 8] = small if c == 0 else jnp.zeros_like(small)

    @pl.when(info_ref[0] == 0)
    def _():
        write(even_ref, odd_ref)

    @pl.when(info_ref[0] != 0)
    def _():
        write(odd_ref, even_ref)


def outer_grad_kernel(
    info_ref, a0_ref, a1_ref, a2_ref, a3_ref, ilow_ref, gfeed_ref, gbranch_ref, even_ref, odd_ref
):
    g_outer = dot(flat_rows(ilow_ref), flat_rows(gfeed_ref), TN).astype(bf16)
    order = jnp.bitwise_xor(pl.program_id(0), info_ref[2])
    low, high = order % 2 == 0, order < 2
    att = jnp.where(
        high,
        jnp.where(low, flat_rows(a0_ref), flat_rows(a1_ref)),
        jnp.where(low, flat_rows(a2_ref), flat_rows(a3_ref)),
    )
    g_out = dot(att, flat_rows(gbranch_ref), TN).astype(bf16)
    write_pieces(info_ref, even_ref, odd_ref, (g_outer, g_out), None)


def inner_grad_kernel(info_ref, nlow_ref, gin_ref, vsum_ref, bsum_ref, even_ref, odd_ref):
    g_in = dot(flat_rows(nlow_ref), flat_rows(gin_ref), TN).astype(bf16)
    vectors = sum(vsum_ref[s] for s in range(vsum_ref.shape[0]))
    bias = sum(bsum_ref[s] for s in range(bsum_ref.shape[0]))
    width = g_in.shape[1]
    low = jnp.concatenate([vectors, jnp.zeros((8, width - WIDE), f32)], axis=1)
    row = lax.broadcasted_iota(jnp.int32, (8, width), 0)
    small = keep_scalar(jnp.where(row == 7, bias, low)).astype(bf16)
    write_pieces(info_ref, even_ref, odd_ref, (g_in,), small)


def split_grads(kernel, name, info, arrays, specs, piece, width, ctx):
    shape = (PAIRS, ctx // (2 * PAIRS), PAIRS, piece, width)
    out_spec = pl.BlockSpec(shape[:2] + (1, piece, width), lambda z, info: (0, 0, z, 0, 0))
    return pl.pallas_call(
        kernel,
        grid_spec=pltpu.PrefetchScalarGridSpec(
            num_scalar_prefetch=1, grid=(PAIRS,), in_specs=specs, out_specs=[out_spec, out_spec]
        ),
        out_shape=[jax.ShapeDtypeStruct(shape, bf16)] * 2,
        compiler_params=room(24),
        cost_estimate=cost(4.5),
        name=name,
    )(info, *arrays)


def hidden_spec(array):
    seqs, rows, hidden = array.shape
    return pl.BlockSpec(
        (seqs, rows, hidden // PAIRS), lambda z, info: (0, 0, lax.rem(z - info[1] + PAIRS, PAIRS))
    )


def outer_grads(info, att, ilow, gfeed, gbranch, ctx):
    width = gfeed.shape[2]
    piece = (ilow.shape[2] // PAIRS + width // PAIRS) // ctx
    arrays = [*att, ilow, gfeed, gbranch]
    specs = [full_spec(x) for x in arrays]
    specs[PAIRS] = hidden_spec(ilow)
    return split_grads(outer_grad_kernel, "outer_grads", info, arrays, specs, piece, width, ctx)


def inner_grads(info, nlow, gin, vsum, bsum, ctx):
    width = nlow.shape[2]
    seqs = vsum.shape[0]
    specs = [
        full_spec(nlow),
        hidden_spec(gin),
        pl.BlockSpec((seqs, 8, WIDE), lambda z, info: (0, 0, z)),
        hidden_spec(bsum),
    ]
    piece = width // ctx + 8
    return split_grads(
        inner_grad_kernel, "inner_grads", info, [nlow, gin, vsum, bsum], specs, piece, gin.shape[2] // PAIRS, ctx
    )


def join_kernel(scalar, keep_ref, got_ref, *outs):
    for d, out in enumerate(outs):
        for r in range(out.shape[0]):
            total = keep_ref[d, r, 0].astype(f32) + got_ref[d, r, 0].astype(f32)
            out[r, 0] = (keep_scalar(total) if scalar else total).astype(bf16)


def join(keep, got, scalar):
    _, repeats, wsh, piece, width = keep.shape
    spec = pl.BlockSpec((PAIRS, repeats, 1, piece, width), lambda z: (0, 0, z, 0, 0))
    return pl.pallas_call(
        functools.partial(join_kernel, scalar),
        grid=(wsh,),
        in_specs=[spec, spec],
        out_specs=[pl.BlockSpec((repeats, 1, piece, width), lambda z: (0, z, 0, 0))] * PAIRS,
        out_shape=[jax.ShapeDtypeStruct(keep.shape[1:], bf16)] * PAIRS,
        compiler_params=room(16),
        cost_estimate=cost(1.5),
        name="join",
    )(keep, got)


def share_kernel(info_ref, *refs):
    firsts, seconds, outs = refs[:PAIRS], refs[PAIRS : 2 * PAIRS], refs[2 * PAIRS :]
    for step in range(PAIRS):
        place = jnp.bitwise_xor(info_ref[1], step)
        out = outs[step % 2]
        for r in range(out.shape[0]):
            totals = []
            for parts in (firsts, seconds):
                total = parts[0][r, place].astype(f32)
                for part in parts[1:]:
                    total = total + part[r, place].astype(f32)
                totals.append(total)
            size = totals[0].shape[0]
            out[r, step // 2, :size] = totals[0].astype(bf16)
            out[r, step // 2, size:] = keep_scalar(totals[1]).astype(bf16)


def share_parts(info, firsts, seconds):
    repeats, wsh, piece, width = firsts[0].shape
    shape = (repeats, wsh // 2, piece + seconds[0].shape[2], width)
    return pl.pallas_call(
        share_kernel,
        grid=(1,),
        in_specs=[pl.BlockSpec(memory_space=pltpu.SMEM)] + [full_spec(x) for x in firsts + seconds],
        out_specs=[pl.BlockSpec(shape, lambda i: (0, 0, 0, 0))] * 2,
        out_shape=[jax.ShapeDtypeStruct(shape, bf16)] * 2,
        compiler_params=room(16),
        cost_estimate=cost(1.5),
        name="share",
    )(info, *firsts, *seconds)


def halve_kernel(keep_ref, got_ref, own_ref, send_ref):
    for at, out in enumerate((own_ref, send_ref)):
        out[...] = keep_scalar(keep_ref[at].astype(f32) + got_ref[at].astype(f32)).astype(bf16)


def halve(keep, got):
    shape = keep.shape[1:]
    return pl.pallas_call(
        halve_kernel,
        grid=(1,),
        in_specs=[full_spec(keep), full_spec(got)],
        out_specs=[pl.BlockSpec(shape, lambda i: (0, 0))] * 2,
        out_shape=[jax.ShapeDtypeStruct(shape, bf16)] * 2,
        compiler_params=room(6),
        cost_estimate=cost(1),
        name="halve",
    )(keep, got)


def total_kernel(own_ref, *refs):
    parts, out = refs[:-1], refs[-1]
    rows = own_ref.shape[0]
    if len(parts) == 1:
        out[...] = keep_scalar(own_ref[...].astype(f32) + parts[0][...].astype(f32)).astype(bf16)
        return
    out[:rows] = keep_scalar(own_ref[...].astype(f32) + parts[2][:rows].astype(f32)).astype(bf16)
    total = parts[2][rows:].astype(f32)
    for i in (0, 1, 3):
        total = total + parts[i][...].astype(f32)
    out[rows:] = total.astype(bf16)


def total_parts(own, parts):
    shape = max((x.shape for x in parts), key=lambda x: x[0])
    return pl.pallas_call(
        total_kernel,
        grid=(1,),
        in_specs=[full_spec(x) for x in [own] + parts],
        out_specs=pl.BlockSpec(shape, lambda i: (0, 0)),
        out_shape=jax.ShapeDtypeStruct(shape, bf16),
        compiler_params=room(6),
        cost_estimate=cost(1),
        name="total",
    )(own, *parts)


def unpack_kernel(info_ref, *refs):
    pieces = refs[: 2 * PAIRS]
    outer_ref, out_ref, in_ref, tail_ref, *heads = refs[2 * PAIRS :]
    core, pair = info_ref[0], info_ref[2]
    for side in range(2):
        for d in range(PAIRS):
            ref = pieces[side * PAIRS + d]
            place = jnp.bitwise_xor(pair, d) * 2 + jnp.bitwise_xor(core, side)
            at = 0
            for target in (outer_ref, out_ref, in_ref):
                size = target.shape[0] // (2 * PAIRS)
                start = pl.multiple_of(place * size, size)
                target[pl.ds(start, size)] = ref[at : at + size].astype(f32)
                at += size

            @pl.when(place == 0)
            def _(ref=ref, at=at):
                tail_ref[...] = ref[at : at + 8].astype(f32)

            at += 8
            size = heads[0].shape[0] // (2 * PAIRS)
            kept = size * 3 // 4
            for i, target in enumerate(heads):
                start = pl.multiple_of(place * size, size)
                target[pl.ds(start, kept)] = ref[at : at + kept, i * WIDE : (i + 1) * WIDE].astype(f32)
                more = (size - kept) * i + at
                target[pl.ds(start + kept, size - kept)] = ref[more : more + size - kept, 3 * WIDE :].astype(f32)


def unpack(info, mine, other, part, out_rows):
    width = mine[0].shape[1]
    shapes = [(part, width), (out_rows, width), (width, part), (8, width)] + [(width, WIDE)] * 3
    return pl.pallas_call(
        unpack_kernel,
        grid=(1,),
        in_specs=[pl.BlockSpec(memory_space=pltpu.SMEM)] + [full_spec(x) for x in mine + other],
        out_specs=[pl.BlockSpec(shape, lambda i: (0, 0)) for shape in shapes],
        out_shape=[jax.ShapeDtypeStruct(shape, f32) for shape in shapes],
        compiler_params=room(16),
        cost_estimate=cost(3),
        name="unpack",
    )(info, *mine, *other)


def gelu_parts(x):
    half = 0.5 * (1.0 + lax.erf(x * 2.0 ** (-0.5)))
    density = jnp.exp(-0.5 * x * x) * (2.0 * math.pi) ** (-0.5)
    return x * half, half + x * density


def mean_rows(x):
    return jnp.sum(x, axis=1, keepdims=True) * (1.0 / x.shape[1])


def norm_rows(z, gain, shift):
    centre = z - mean_rows(z)
    inverse = lax.rsqrt(mean_rows(centre * centre) + epsilon)
    normed = centre * inverse
    return normed * gain + shift, normed, inverse


def norm_back(g, normed, inverse, gain):
    scaled = g * gain
    return inverse * (scaled - mean_rows(scaled) - normed * mean_rows(scaled * normed))


def dense_kernel(info_ref, bhalt_ref, *refs):
    mine, other, refs = refs[:PAIRS], refs[PAIRS : 2 * PAIRS], refs[2 * PAIRS :]
    att_refs, refs = refs[:PAIRS], refs[PAIRS:]
    emb_ref, prev_ref, gt_ref, gb_ref, hsum_ref, code_ref, gsum_ref = refs[:7]
    refs = refs[7:]
    final_ref, blend_ref, rows_ref, gprev_ref, base_ref = refs[:5]
    gatt_refs = refs[5:9]
    nlow_ref, ilow_ref, gin_ref, gfeed_ref, gbranch_ref, vsum_ref, bsum_ref = refs[9:16]
    slope_ref, win_ref, wouter_ref, wout_ref, small_ref, sem = refs[16:22]
    buffers, row_sem = refs[22:26], refs[26]
    me = pl.program_id(0)

    def fetch(step):
        slot = lax.rem(step, 2)
        return [
            pltpu.make_async_copy(source.at[step], buffer.at[slot], row_sem.at[i, slot])
            for i, (source, buffer) in enumerate(zip((emb_ref, prev_ref, gt_ref, gb_ref), buffers))
        ]

    @pl.when(me == 0)
    def _():
        for one in fetch(0):
            one.start()

    @pl.when(me + 1 < pl.num_programs(0))
    def _():
        for one in fetch(me + 1):
            one.start()

    blocks, columns, width = win_ref.shape
    cut = wout_ref.shape[1] // 2
    core, zed, pair = info_ref[0], info_ref[1], info_ref[2]

    def load(firsts, seconds):
        copies = []

        def copy(source, start, size, target):
            copies.append(pltpu.make_async_copy(source.at[pl.ds(start, size)], target, sem.at[len(copies)]))

        for a in range(PAIRS):
            place = lax.rem(zed + a, PAIRS)
            order = jnp.bitwise_xor(place, pair)
            first, second = firsts[(-a) % PAIRS], seconds[a]
            copy(first, columns, cut, wout_ref.at[order, pl.ds(0, cut)])
            copy(second, width, cut, wout_ref.at[order, pl.ds(cut, cut)])
            copy(first, columns + cut, SMALL, small_ref.at[place])
            copy(first, 0, columns, win_ref.at[a])
            copy(second, 0, width, wouter_ref.at[a])
        for one in copies:
            one.start()
        for one in copies:
            one.wait()

    @pl.when((pl.program_id(0) == 0) & (core == 0))
    def _():
        load(mine, other)

    @pl.when((pl.program_id(0) == 0) & (core != 0))
    def _():
        load(other, mine)

    for one in fetch(me):
        one.wait()
    emb, prev, gt, gb = [buffer[lax.rem(me, 2)] for buffer in buffers]
    att = jnp.concatenate([ref[0] for ref in att_refs], axis=1)
    w_out = wout_ref[...].reshape(emb.shape[1], emb.shape[1])
    b_outer, g1, s1, g2, s2, halt = [
        jnp.concatenate([small_ref[a, i + 1 : i + 2, :WIDE] for a in range(PAIRS)], axis=1).astype(f32)
        for i in range(6)
    ]
    at = pl.ds(pl.program_id(0), 1)
    row = lax.broadcasted_iota(jnp.int32, (8, emb.shape[0]), 0)
    lines = jnp.where(row == 0, hsum_ref[at], jnp.where(row == 1, code_ref[at].astype(f32), gsum_ref[at]))
    cols = jnp.transpose(lines)
    sum_col, code_col, gsum_col = cols[:, 0:1], cols[:, 1:2], cols[:, 2:3]
    z1 = emb + dot(att, w_out)
    one, n1, i1 = norm_rows(z1, g1, s1)
    nlow = one.astype(bf16)
    nlow_ref[0] = nlow
    feed = None
    for j in range(blocks):
        pre = dot(nlow, win_ref[j]) + small_ref[lax.rem(zed + j, PAIRS), 0:1, :].astype(f32)
        act, slope = gelu_parts(pre)
        act = act.astype(bf16)
        ilow_ref[0, :, j * width : (j + 1) * width] = act
        slope_ref[:, j * width : (j + 1) * width] = slope
        part = dot(act, wouter_ref[j])
        feed = part if feed is None else feed + part
    z2 = one + (feed + b_outer)
    final, n2, i2 = norm_rows(z2, g2, s2)
    halt_logit = jnp.sum(emb * halt, axis=1, keepdims=True) + bhalt_ref[0, 0]
    halt_prob = jax.nn.sigmoid(halt_logit)
    running = (code_col > 0.5).astype(f32)
    halting = (code_col > 1.5).astype(f32)
    update = running * (halting * (1.0 - sum_col) + (1.0 - halting) * halt_prob)
    prev = prev.astype(f32)
    gb = gb.astype(f32)
    final_ref[0] = final.astype(bf16)
    blend_ref[0] = (prev * (1.0 - update) + final * update).astype(bf16)
    gprev_ref[0] = gb * (1.0 - update)
    g_update = jnp.sum(gb * (final - prev), axis=1, keepdims=True) + gsum_col
    g_halt_sum = gsum_col - running * halting * g_update
    g_logit = g_update * running * (1.0 - halting) * halt_prob * (1.0 - halt_prob)
    lane = lax.broadcasted_iota(jnp.int32, (emb.shape[0], WIDE), 1)
    packed = jnp.where(lane == 0, sum_col + update, jnp.where(lane == 1, g_halt_sum, 0.0))
    rows_ref[0] = jnp.transpose(packed)[0:8]
    gf = gt.astype(f32) + update * gb
    g_two = norm_back(gf, n2, i2, g2)
    gfeed = g_two.astype(bf16)
    gfeed_ref[0] = gfeed
    g_one = g_two
    for j in range(blocks):
        at = slice(j * width, (j + 1) * width)
        back = dot(gfeed, wouter_ref[j], NT)
        gin_f = back * slope_ref[:, at]
        gin = gin_f.astype(bf16)
        gin_ref[0, :, at] = gin
        bsum_ref[0, :, at] = jnp.sum(gin.astype(f32), axis=0, keepdims=True)
        g_one = g_one + dot(gin, win_ref[j], NT)
    g_emb = norm_back(g_one, n1, i1, g1)
    gbranch = g_emb.astype(bf16)
    gbranch_ref[0] = gbranch
    gatt = dot(gbranch, w_out, NT).astype(bf16)
    for d, ref in enumerate(gatt_refs):
        ref[0] = gatt[:, d * WIDE : (d + 1) * WIDE]
    base_ref[0] = g_emb + g_logit * halt
    total = lambda x: jnp.sum(x, axis=0, keepdims=True)
    logit_sum = jnp.broadcast_to(total(g_logit), (1, emb.shape[1]))
    vsum_ref[0] = jnp.concatenate(
        [
            total(gfeed.astype(f32)),
            total(g_one * n1),
            total(g_one),
            total(gf * n2),
            total(gf),
            total(g_logit * emb),
            logit_sum,
            jnp.zeros((1, emb.shape[1]), f32),
        ],
        axis=0,
    )


def dense(info, b_halt, mine, other, emb, att, prev, gt, gb, marks, part, out_rows):
    seqs, rows, width = emb.shape
    hidden = PAIRS * part
    outside = pl.BlockSpec(memory_space=pltpu.HBM)
    scalars = pl.BlockSpec(memory_space=pltpu.SMEM)
    rowspec = lambda w: pl.BlockSpec((1, rows, w), lambda s: (s, 0, 0))
    shape = lambda w, kind: jax.ShapeDtypeStruct((seqs, rows, w), kind)
    return pl.pallas_call(
        dense_kernel,
        grid=(seqs,),
        in_specs=[scalars, scalars]
        + [outside] * (2 * PAIRS)
        + [rowspec(WIDE)] * PAIRS
        + [outside] * 4
        + [full_spec(x) for x in marks],
        out_specs=[
            rowspec(width),
            rowspec(width),
            pl.BlockSpec((1, 8, rows), lambda s: (s, 0, 0)),
            rowspec(width),
            rowspec(width),
            rowspec(WIDE),
            rowspec(WIDE),
            rowspec(WIDE),
            rowspec(WIDE),
            rowspec(width),
            rowspec(hidden),
            rowspec(hidden),
            rowspec(width),
            rowspec(width),
            pl.BlockSpec((1, 8, width), lambda s: (s, 0, 0)),
            pl.BlockSpec((1, 1, hidden), lambda s: (s, 0, 0)),
        ],
        out_shape=[
            shape(width, bf16),
            shape(width, bf16),
            jax.ShapeDtypeStruct((seqs, 8, rows), f32),
            shape(width, f32),
            shape(width, f32),
            shape(WIDE, bf16),
            shape(WIDE, bf16),
            shape(WIDE, bf16),
            shape(WIDE, bf16),
            shape(width, bf16),
            shape(hidden, bf16),
            shape(hidden, bf16),
            shape(width, bf16),
            shape(width, bf16),
            jax.ShapeDtypeStruct((seqs, 8, width), f32),
            jax.ShapeDtypeStruct((seqs, 1, hidden), f32),
        ],
        scratch_shapes=[
            pltpu.VMEM((rows, hidden), f32),
            pltpu.VMEM((PAIRS, width, part), bf16),
            pltpu.VMEM((PAIRS, part, width), bf16),
            pltpu.VMEM((PAIRS, out_rows, width), bf16),
            pltpu.VMEM((PAIRS, SMALL, width), bf16),
            pltpu.SemaphoreType.DMA((5 * PAIRS,)),
            pltpu.VMEM((2, rows, width), f32),
            pltpu.VMEM((2, rows, width), bf16),
            pltpu.VMEM((2, rows, width), bf16),
            pltpu.VMEM((2, rows, width), bf16),
            pltpu.SemaphoreType.DMA((4, 2)),
        ],
        compiler_params=room(36),
        cost_estimate=cost(20),
        name="dense",
    )(info, b_halt, *mine, *other, *att, emb, prev, gt, gb, *marks)


def frequencies(half):
    return jnp.exp(-math.log(10000.0) * jnp.arange(half, dtype=f32) / (half - 1))


def position_rows(first, rows, columns):
    half = columns // 2
    freq = frequencies(half)[None, :]
    coarse = (first + 16 * jnp.arange(rows // 16, dtype=jnp.int32)).astype(f32)[:, None] * freq
    fine = jnp.arange(16, dtype=f32)[:, None] * freq
    sa, ca = jnp.sin(coarse)[:, None], jnp.cos(coarse)[:, None]
    sb, cb = jnp.sin(fine)[None], jnp.cos(fine)[None]
    both = jnp.concatenate([sa * cb + ca * sb, ca * cb - sa * sb], axis=2)
    return both.reshape(rows, columns)


def step_rows(columns):
    half = columns // 2
    angles = jnp.arange(4, dtype=f32)[:, None] * frequencies(half)[None, :]
    return jnp.concatenate([jnp.sin(angles), jnp.cos(angles)], axis=1)


def body(
    hidden_state,
    prev_state,
    halt_sum,
    halt_code,
    step_count,
    w_query,
    w_key,
    w_value,
    w_out,
    w_inner,
    b_inner,
    w_outer,
    b_outer,
    gain_attention,
    shift_attention,
    gain_feedforward,
    shift_feedforward,
    w_halt,
    b_halt,
    grad_transformed,
    grad_blended,
    grad_sum,
):
    seqs, rows, width = hidden_state.shape
    ctx = lax.axis_size("ctx")
    wsh = lax.axis_size("wsh")
    repeats = ctx // (2 * PAIRS)
    me = lax.axis_index("ctx")
    zed = lax.axis_index("wsh")
    core = me % 2
    pair = (me // 2) % PAIRS

    def swap(x, distance):
        return lax.ppermute(x, "ctx", [(i, i ^ distance) for i in range(ctx)])

    def sibling(x):
        return swap(x, 1)

    def partners(x, distance):
        return swap(x, 2 * distance)

    freq_rows = position_rows(me * rows, rows, width)
    table = step_rows(width)
    steps = step_count[:, :, None]
    step_signal = jnp.where(
        steps == 0, table[0], jnp.where(steps == 1, table[1], jnp.where(steps == 2, table[2], table[3]))
    )
    emb = hidden_state.astype(f32) + freq_rows[None] + step_signal
    emb_low = emb.astype(bf16)

    after = lambda x, *others: lax.optimization_barrier((x,) + others)[0]

    info = jnp.stack([core, zed, pair]).astype(jnp.int32)
    ring = [
        (c * wsh + z, c * wsh + (z + (1 if c % 2 == 0 else -1)) % wsh) for c in range(ctx) for z in range(wsh)
    ]
    turn = lambda x: lax.ppermute(x, ("ctx", "wsh"), ring)
    out_rows = w_out.shape[0]
    part = w_inner.shape[1]
    half = rows // 2

    tokens = [emb_low] + [partners(emb_low, d) for d in (1, 2)]
    pair_of = lambda c: (c // 2) % PAIRS
    held = pack(info, [w_query, w_key, w_value])
    sent = []
    for step in range(1, wsh):
        moves = [(c * wsh + pair_of(c), c * wsh + (pair_of(c) + step) % wsh) for c in range(ctx)]
        sent.append(lax.ppermute(held, ("ctx", "wsh"), moves))
    tokens.append(partners(tokens[2][:, :half], 1))
    tokens.append(partners(tokens[1][:, half:], 2))
    vectors = [b_outer, gain_attention, shift_attention, gain_feedforward, shift_feedforward, w_halt]
    feed = pack_feed(after(info, held), w_inner, w_outer, w_out, b_inner, vectors)
    feed_mine = [feed, turn(feed)]
    chosen = choose(after(info, feed_mine[1], *tokens[1:3]), held, sent)
    w_mine = assemble(info, chosen, sibling(chosen))

    groups = [[r * 2 * PAIRS + i for r in range(repeats)] for i in range(2 * PAIRS)]
    q_list, kvs_list, fold = [], [], None
    w_now = w_mine
    own_list = []
    for s in range(seqs):
        q, own = project(s, tokens, w_now)
        w_now = after(w_mine, q)
        q_list.append(q)
        own_list.append(own)

    def keys_values(own):
        other = sibling(own)
        if repeats == 1:
            return [own, other]
        both = jnp.concatenate([own, other], axis=1)
        return [lax.all_gather(both, "ctx", axis=1, tiled=True, axis_index_groups=groups)]

    feed_mine.append(turn(feed_mine[1]))
    feed_other = [sibling(after(x, q_list[0])) for x in feed_mine[:2]]
    kvs_list = [keys_values(own) for own in own_list[:2]]
    fold = attend(0, seqs, q_list[0], kvs_list[0], None)
    kvs_list.append(keys_values(after(own_list[2], fold[1])))
    fold = attend(1, seqs, after(q_list[1], *feed_other, fold[1]), kvs_list[1], fold)
    feed_mine.append(turn(after(feed_mine[2], fold[1])))
    fold = attend(2, seqs, after(q_list[2], feed_mine[2]), kvs_list[2], fold)
    o32, mass, *low = fold
    att = [low[0]] + [partners(low[d], d) for d in range(1, PAIRS)]
    feed_other.append(sibling(after(feed_mine[2], mass)))
    feed_other.append(sibling(after(feed_mine[3], *att[1:])))
    w_order = [w_mine] + [partners(after(w_mine, *att[1:]), d) for d in range(1, PAIRS)]

    (
        final,
        blended,
        row_out,
        grad_prev,
        base,
        gatt0,
        gatt1,
        gatt2,
        gatt3,
        nlow,
        ilow,
        gin,
        gfeed,
        gbranch,
        vsum,
        bsum,
    ) = dense(
        info, b_halt.reshape(1, 1), feed_mine, feed_other, emb, att, prev_state, grad_transformed, grad_blended,
        [halt_sum, halt_code, grad_sum], part, out_rows,
    )
    new_sum = row_out[:, 0]
    grad_halt_sum = row_out[:, 1]
    gs = [gatt0] + [partners(x, d + 1) for d, x in enumerate((gatt1, gatt2, gatt3))]

    keep_a, give_a = outer_grads(after(info, vsum, *w_order[1:]), att, ilow, gfeed, gbranch, ctx)
    keep_b, give_b = inner_grads(after(info, keep_a), nlow, gin, vsum, bsum, ctx)
    joined_a = join(after(keep_a, keep_b), sibling(give_a), False)

    def spread_pieces(pieces):
        return [pieces[0]] + [partners(pieces[d], d) for d in range(1, PAIRS)]

    shared_a = spread_pieces(joined_a)

    kinds = [f32, bf16] if repeats == 1 else [bf16]

    def split_back(s, token):
        dq, *dkv = attend_back(s, q_list[s], gs, o32, token, kvs_list[s], kinds)
        if repeats == 1:
            kept, sent = dkv
        else:
            summed = lax.psum_scatter(
                dkv[0], "ctx", scatter_dimension=1, tiled=True, axis_index_groups=groups
            )
            kept, sent = summed[:, : PAIRS * rows].astype(f32), summed[:, PAIRS * rows :]
        return dq, kept, sent

    backs = [split_back(0, after(mass, *joined_a))]
    joined_b = join(after(keep_b, backs[0][0], *shared_a), sibling(give_b), True)
    shared_b = spread_pieces(joined_b)
    backs.append(split_back(1, after(mass, *joined_b)))
    got = lambda back, *others: back[:2] + (sibling(after(back[2], *others)),)
    share_keep, share_send = share_parts(after(info, backs[1][0]), shared_a, shared_b)
    if repeats > 1:
        share_keep, share_send = (
            lax.psum_scatter(x, "ctx", scatter_dimension=0, tiled=True, axis_index_groups=groups)
            for x in (share_keep, share_send)
        )
    cross = lambda x, step: lax.ppermute(x, "wsh", [(z, z ^ step) for z in range(wsh)])
    moved = cross(share_send[0], 1)
    *pieces, gq = combine(
        after(info, share_keep), (0, 1), tokens, [got(backs[0]), got(backs[1], share_keep)], None, False
    )
    blocks = spread_pieces(pieces)
    backs.append(split_back(2, after(mass, gq)))
    own, sent = halve(after(share_keep[0], backs[2][0], *blocks[1:]), moved)
    made = combine(info, (2,), tokens, [got(backs[2], own)], gq, repeats == 1)
    pieces, keep, give = made[:PAIRS], made[PAIRS], made[-1]
    block = [pieces[0]] + [partners(pieces[d], d) for d in (1, 2)]
    if repeats == 1:
        heads = share_small(after(info, *block), sent, spread_pieces(join_small(keep, sibling(give))))
        block.append(partners(after(pieces[3], heads[0]), 3))
        heads = [heads[0]] + [cross(heads[step], step) for step in range(1, wsh)]
        grad_state = add_state(0, after(base, heads[0]), blocks, w_order)
        share = total_parts(after(own, grad_state), heads)
        grad_state = add_state(2, after(grad_state, share), block, w_order)
        mine = spread_pieces([share] * PAIRS)
        (grad_w_outer, grad_w_out, grad_w_inner, tail, grad_w_query, grad_w_key, grad_w_value) = unpack(
            info, mine, [sibling(after(x, grad_state)) for x in mine], part, out_rows
        )
    else:
        block.append(partners(pieces[3], 3))
        share = total_parts(own, [cross(sent, 2)])
        grad_state = add_state(2, add_state(0, base, blocks, w_order), block, w_order)
        whole = lax.all_gather(share, "ctx", axis=0).astype(f32)
        a, b, c = part // ctx, out_rows // ctx, width // ctx
        grad_w_outer = whole[:, :a].reshape(part, width)
        grad_w_out = whole[:, a : a + b].reshape(out_rows, width)
        grad_w_inner = whole[:, a + b : a + b + c].reshape(width, part)
        tail = whole[0, a + b + c :]
        own = lax.dynamic_update_index_in_dim(jnp.zeros((wsh,) + keep.shape, f32), keep, pair, 0)
        own = lax.psum(lax.psum_scatter(own.astype(bf16), "wsh", scatter_dimension=0).astype(f32), "ctx")
        grad_w_query, grad_w_key, grad_w_value = (own[:, i * WIDE : (i + 1) * WIDE] for i in range(3))
    grad_b_inner = tail[7]
    vec_grads = [tail[i, :out_rows] for i in range(6)]
    grad_b_halt = tail[6, :1] + tail[6, WIDE : WIDE + 1]

    return (
        final,
        blended,
        new_sum,
        grad_state,
        grad_prev,
        grad_halt_sum,
        grad_w_query,
        grad_w_key,
        grad_w_value,
        grad_w_out,
        grad_w_inner,
        grad_b_inner,
        grad_w_outer,
        vec_grads[0],
        vec_grads[1],
        vec_grads[2],
        vec_grads[3],
        vec_grads[4],
        vec_grads[5],
        grad_b_halt,
    )


def solution(mesh):
    rows = P("wsh", "ctx", None)
    marks = P("wsh", "ctx")
    column, row, vector = P(None, "wsh"), P("wsh", None), P("wsh")
    in_specs = (
        (rows, rows, marks, marks, marks, column, column, column, row, column, vector, row)
        + (vector,) * 6
        + (P(), rows, rows, marks)
    )
    out_specs = (
        (rows, rows, marks, rows, rows, marks, column, column, column, row, column, vector, row)
        + (vector,) * 6
        + (P(),)
    )
    return jax.shard_map(body, mesh=mesh, in_specs=in_specs, out_specs=out_specs, check_vma=False)
```

```python
import functools
import math

import jax
import jax.numpy as jnp
from jax import lax
from jax.experimental import pallas as pl
from jax.experimental.pallas import tpu as pltpu
from jax.sharding import PartitionSpec as P

HEADS = 8
PAIRS = 4
WIDE = 128
SMALL = 16
epsilon = 1e-06
f32 = jnp.float32
bf16 = jnp.bfloat16
LOG2E = math.log2(math.e)
NT = (((1,), (1,)), ((), ()))
TN = (((0,), (0,)), ((), ()))
NN = (((1,), (0,)), ((), ()))
MIB = 1024 * 1024
KEYS = 256


def room(mebibytes):
    return pltpu.CompilerParams(vmem_limit_bytes=int(mebibytes) * MIB)


def cost(micros):
    return pl.CostEstimate(flops=int(micros * 1.1e9), bytes_accessed=1024, transcendentals=0)


def dot(a, b, dims=NN):
    return lax.dot_general(a, b, dims, preferred_element_type=f32)


def lane_masks(shape):
    lane = lax.broadcasted_iota(jnp.int32, shape, 1)
    return lane < WIDE // 2


def largest_squares(refs):
    same = (
        lax.broadcasted_iota(jnp.int32, (WIDE, WIDE), 0) // (WIDE // 2)
        == lax.broadcasted_iota(jnp.int32, (WIDE, WIDE), 1) // (WIDE // 2)
    ).astype(bf16)
    most = None
    for ref in refs:
        for start in range(0, ref.shape[1], 1024):
            x = ref[0, start : start + 1024, :WIDE].astype(f32)
            top = jnp.max(dot((x * x).astype(bf16), same), axis=0, keepdims=True)
            most = top if most is None else jnp.maximum(most, top)
    return most


def attend_kernel(blocks, carried, q_ref, *refs):
    kv_refs = refs[:blocks]
    refs = refs[blocks + carried :]
    flag_ref = refs[-1]
    o_ref, mass_ref, low_refs = refs[0], refs[1], refs[2:-1]
    scale = 0.125 * LOG2E
    index = pl.program_id(0)
    step = o_ref.shape[1]

    @pl.when(index == 0)
    def _():
        bound = jnp.max(largest_squares([q_ref]) * largest_squares(kv_refs))
        flag_ref[0] = (bound < 0.98 * (8.0 * 70.0) ** 2).astype(jnp.int32)

    q = q_ref[0, pl.ds(pl.multiple_of(index * step, step), step)]
    first = lane_masks(q.shape)
    none = jnp.zeros_like(q)
    size = KEYS
    chunks = [(ref, start) for ref in kv_refs for start in range(0, ref.shape[1], size)]

    def finish(outs, masses):
        out = jnp.where(first, outs[0], outs[1])
        o_ref[0] = out
        low = out.astype(bf16)
        block = low_refs[0].shape[1]
        for d, ref in enumerate(low_refs):

            @pl.when(index == d * block // step)
            def _(ref=ref, at=d * block % step):
                ref[0] = low[at : at + block]

        table = jnp.where(first, masses[0], masses[1])
        turned = jnp.transpose(table)
        mass_ref[0] = jnp.concatenate([turned[0:4], turned[64:68]], axis=0)

    def masked(head):
        return jnp.where(first, q, none) if head == 0 else jnp.where(first, none, q)

    def lanes(e):
        return sum(e[:, i : i + 128] for i in range(0, size, 128))

    @pl.when(flag_ref[0] == 1)
    def _():
        outs, masses = [], []
        for head in range(2):
            mine = masked(head)
            total = None
            weighted = None
            for ref, start in chunks:
                e = jnp.exp2(dot(mine, ref[0, start : start + size, :WIDE], NT) * scale)
                w = dot(e.astype(bf16), ref[0, start : start + size, WIDE:])
                total = lanes(e) if total is None else total + lanes(e)
                weighted = w if weighted is None else weighted + w
            total = jnp.sum(total, axis=1, keepdims=True)
            outs.append(weighted * (1.0 / total))
            masses.append(jnp.log2(total))
        finish(outs, masses)

    @pl.when(flag_ref[0] != 1)
    def _():
        outs, masses = [], []
        for head in range(2):
            mine = masked(head)
            fold = (
                jnp.zeros((step, WIDE), f32),
                jnp.full((step, 1), -jnp.inf, f32),
                jnp.zeros((step, 1), f32),
            )
            for ref in kv_refs:

                def body(i, fold, ref=ref, mine=mine):
                    weighted, top, total = fold
                    at = pl.ds(pl.multiple_of(i * size, size), size)
                    scores = dot(mine, ref[0, at, :WIDE], NT) * scale
                    now = jnp.maximum(top, jnp.max(scores, axis=1, keepdims=True))
                    factor = jnp.exp2(top - now)
                    e = jnp.exp2(scores - now)
                    total = total * factor + jnp.sum(e, axis=1, keepdims=True)
                    weighted = weighted * factor + dot(e.astype(bf16), ref[0, at, WIDE:])
                    return weighted, now, total

                fold = lax.fori_loop(0, ref.shape[1] // size, body, fold)
            weighted, top, total = fold
            outs.append(weighted * (1.0 / total))
            masses.append(top + jnp.log2(total))
        finish(outs, masses)


def attend(at, seqs, q, kvs, before):
    _, rows, _ = q.shape
    block = rows // PAIRS
    keys = sum(kv.shape[1] for kv in kvs)
    step = 2 * block if keys <= 2048 else block
    shapes = [
        jax.ShapeDtypeStruct((seqs, rows, WIDE), f32),
        jax.ShapeDtypeStruct((seqs, 8, rows), f32),
    ] + [jax.ShapeDtypeStruct((seqs, block, WIDE), bf16)] * PAIRS
    carried = len(shapes) if before else 0
    return pl.pallas_call(
        functools.partial(attend_kernel, len(kvs), carried),
        grid=(rows // step,),
        in_specs=[full_spec(q)]
        + [full_spec(kv) for kv in kvs]
        + [pl.BlockSpec(memory_space=pl.ANY)] * carried,
        out_specs=[
            pl.BlockSpec((1, step, WIDE), lambda i: (at, i, 0)),
            pl.BlockSpec((1, 8, step), lambda i: (at, 0, i)),
        ]
        + [pl.BlockSpec((1, block, WIDE), lambda i: (at, 0, 0))] * PAIRS,
        out_shape=shapes,
        input_output_aliases={1 + len(kvs) + i: i for i in range(carried)},
        scratch_shapes=[pltpu.SMEM((1,), jnp.int32)],
        compiler_params=room(24 if keys <= 2048 else 10 + keys // 256),
        cost_estimate=cost(1),
        name="attend",
    )(q, *kvs, *(before or ()))


def attend_back_kernel(blocks, q_ref, *refs):
    g_refs, o_ref, mass_ref = refs[:PAIRS], refs[PAIRS], refs[PAIRS + 1]
    refs = refs[PAIRS + 2 :]
    kv_refs = refs[:blocks]
    dq_ref = refs[blocks]
    dkv_refs = refs[blocks + 1 : 2 * blocks + 1]
    dq_acc = refs[2 * blocks + 1]
    scale = 0.125 * LOG2E
    q = q_ref[0]
    g = jnp.concatenate([ref[0] for ref in g_refs], axis=0)
    first = lane_masks(q.shape)
    none = jnp.zeros_like(q)
    qs = [jnp.where(first, q, none), jnp.where(first, none, q)]
    gs = [jnp.where(first, g, none), jnp.where(first, none, g)]
    product = g.astype(f32) * o_ref[0]
    which = lax.broadcasted_iota(jnp.int32, (8, WIDE), 0) == (
        lax.broadcasted_iota(jnp.int32, (8, WIDE), 1) // (WIDE // 2)
    )
    deltas = lax.dot_general(
        which.astype(f32), product, NT, precision=lax.Precision.HIGHEST, preferred_element_type=f32
    )
    delta = [deltas[0:1], deltas[1:2]]
    mass = [mass_ref[0, 0:1, :], mass_ref[0, 4:5, :]]
    dq_acc[...] = jnp.zeros_like(dq_acc)
    size = 256
    key_first = lane_masks((size, WIDE))
    key_none = jnp.zeros((size, WIDE), bf16)

    for kv_ref, dkv_ref in zip(kv_refs, dkv_refs):

        def chunk(i, carry, kv_ref=kv_ref, dkv_ref=dkv_ref):
            at = pl.ds(pl.multiple_of(i * size, size), size)
            k = kv_ref[0, at, :WIDE]
            v = kv_ref[0, at, WIDE:]
            dk = dv = dq = None
            for head in range(2):
                s = dot(k, qs[head], NT)
                p = jnp.exp2(s * scale - mass[head])
                dp = dot(v, gs[head], NT)
                ds = (p * (dp - delta[head])).astype(bf16)
                own_v = dot(p.astype(bf16), gs[head])
                own_k = dot(ds, qs[head])
                km = jnp.where(key_first, k, key_none) if head == 0 else jnp.where(key_first, key_none, k)
                own_q = dot(ds, km, TN)
                dv = own_v if dv is None else dv + own_v
                dk = own_k if dk is None else dk + own_k
                dq = own_q if dq is None else dq + own_q
            dkv_ref[0, at, :WIDE] = (dk * 0.125).astype(dkv_ref.dtype)
            dkv_ref[0, at, WIDE:] = dv.astype(dkv_ref.dtype)
            dq_acc[...] += dq
            return carry

        lax.fori_loop(0, kv_ref.shape[1] // size, chunk, 0, unroll=2)
    dq_ref[0] = (dq_acc[...] * 0.125).astype(bf16)


def attend_back(at, q, gs, o, mass, kvs, kinds):
    _, rows, _ = q.shape
    keys = sum(kv.shape[1] for kv in kvs)
    own = gs[0].shape[1]
    whole = lambda width: pl.BlockSpec((1, rows, width), lambda s: (0, 0, 0))
    kv_specs = [pl.BlockSpec((1, kv.shape[1], 2 * WIDE), lambda s: (0, 0, 0)) for kv in kvs]
    return pl.pallas_call(
        functools.partial(attend_back_kernel, len(kvs)),
        grid=(1,),
        in_specs=[whole(WIDE)]
        + [pl.BlockSpec((1, own, WIDE), lambda s: (at, 0, 0))] * PAIRS
        + [pl.BlockSpec((1, rows, WIDE), lambda s: (at, 0, 0)), pl.BlockSpec((1, 8, rows), lambda s: (at, 0, 0))]
        + kv_specs,
        out_specs=[whole(WIDE)] + kv_specs,
        out_shape=[jax.ShapeDtypeStruct((1, rows, WIDE), bf16)]
        + [jax.ShapeDtypeStruct(kv.shape, kind) for kv, kind in zip(kvs, kinds)],
        scratch_shapes=[pltpu.VMEM((rows, WIDE), f32)],
        compiler_params=room(14 + keys // 512),
        cost_estimate=cost(14),
        name="attend_back",
    )(q, *gs, o, mass, *kvs)


def full_spec(array):
    return pl.BlockSpec(array.shape, lambda *_: (0,) * array.ndim)


def pack_kernel(info_ref, *refs):
    parts, out_ref = refs[:-1], refs[-1]
    core = info_ref[0]
    half = out_ref.shape[0]

    @pl.when(core == 0)
    def _():
        out_ref[...] = jnp.concatenate([ref[:half] for ref in parts], axis=1)

    @pl.when(core != 0)
    def _():
        out_ref[...] = jnp.concatenate([ref[half:] for ref in parts], axis=1)


def pack(info, parts):
    rows, width = parts[0].shape
    shape = (rows // 2, len(parts) * width)
    return pl.pallas_call(
        pack_kernel,
        grid=(1,),
        in_specs=[pl.BlockSpec(memory_space=pltpu.SMEM)] + [full_spec(x) for x in parts],
        out_specs=pl.BlockSpec(shape, lambda i: (0, 0)),
        out_shape=jax.ShapeDtypeStruct(shape, bf16),
        compiler_params=room(6),
        cost_estimate=cost(1),
        name="pack",
    )(info, *parts)


def pack_feed_kernel(info_ref, inner_ref, outer_ref, wout_ref, bias_ref, *refs):
    vectors, out_ref = refs[:-1], refs[-1]
    core = info_ref[0]
    width = inner_ref.shape[0]
    cut = wout_ref.shape[0] // 2

    @pl.when(core == 0)
    def _():
        out_ref[:width] = inner_ref[...]
        out_ref[width : width + cut] = wout_ref[:cut]

    @pl.when(core != 0)
    def _():
        out_ref[:width] = outer_ref[...]
        out_ref[width : width + cut] = wout_ref[cut:]

    row = lax.broadcasted_iota(jnp.int32, (SMALL, WIDE), 0)
    table = jnp.zeros((SMALL, WIDE), f32)
    for i, ref in enumerate(vectors):
        table = jnp.where(row == i + 1, ref[...].astype(f32), table)
    row = lax.broadcasted_iota(jnp.int32, (SMALL, width), 0)
    table = jnp.concatenate([table, jnp.zeros((SMALL, width - WIDE), f32)], axis=1)
    table = jnp.where(row == 0, bias_ref[...].astype(f32), table)
    out_ref[width + cut :] = table.astype(bf16)


def pack_feed(info, w_inner, w_outer, w_out, b_inner, vectors):
    width = w_inner.shape[0]
    parts = [w_inner, w_outer, w_out, b_inner.reshape(1, -1)] + [v.reshape(1, -1) for v in vectors]
    shape = (width + w_out.shape[0] // 2 + SMALL, w_out.shape[1])
    return pl.pallas_call(
        pack_feed_kernel,
        grid=(1,),
        in_specs=[pl.BlockSpec(memory_space=pltpu.SMEM)] + [full_spec(x) for x in parts],
        out_specs=pl.BlockSpec(shape, lambda i: (0, 0)),
        out_shape=jax.ShapeDtypeStruct(shape, bf16),
        compiler_params=room(10),
        cost_estimate=cost(2),
        name="pack_feed",
    )(info, *parts)


def project_kernel(count, *refs):
    blocks, w_ref, q_ref, kv_ref = refs[:count], refs[count], refs[count + 1], refs[count + 2]
    at = 0
    for ref in blocks:
        rows = ref.shape[1]
        made = dot(ref[0], w_ref[...]).astype(bf16)
        q_ref[0, at : at + rows] = made[:, :WIDE]
        kv_ref[0, at : at + rows] = made[:, WIDE:]
        at += rows


def project(at, tokens, w_mine):
    total = sum(x.shape[1] for x in tokens)
    return pl.pallas_call(
        functools.partial(project_kernel, len(tokens)),
        grid=(1,),
        in_specs=[pl.BlockSpec((1,) + x.shape[1:], lambda i: (at, 0, 0)) for x in tokens]
        + [full_spec(w_mine)],
        out_specs=[
            pl.BlockSpec((1, total, WIDE), lambda i: (0, 0, 0)),
            pl.BlockSpec((1, total, 2 * WIDE), lambda i: (0, 0, 0)),
        ],
        out_shape=[
            jax.ShapeDtypeStruct((1, total, WIDE), bf16),
            jax.ShapeDtypeStruct((1, total, 2 * WIDE), bf16),
        ],
        compiler_params=room(10),
        cost_estimate=cost(1),
        name="project",
    )(*tokens, w_mine)


def combine_kernel(chosen, count, prior, final, info_ref, *refs):
    blocks, refs = refs[:count], refs[count:]
    backs, refs = refs[: 3 * len(chosen)], refs[3 * len(chosen) :]
    grad = None
    if prior:
        grad, refs = refs[0][...], refs[1:]
    outs, grad_refs = refs[:PAIRS], refs[PAIRS:]
    rows = outs[0].shape[1]
    for i, s in enumerate(chosen):
        dq_ref, kept_ref, got_ref = backs[3 * i : 3 * i + 3]
        at = 0
        for ref in blocks:
            size = ref.shape[1]
            part = slice(at, at + size)
            dkv = (kept_ref[0, part] + got_ref[0, part].astype(f32)).astype(bf16)
            piece = jnp.concatenate([dq_ref[0, part], dkv], axis=1)
            outs[at // rows][i, at % rows : at % rows + size] = piece
            term = dot(ref[s], piece, TN)
            grad = term if grad is None else grad + term
            at += size
    if not final:
        grad_refs[0][...] = grad
        return
    size = grad.shape[0] // (2 * PAIRS)

    def write(even_ref, odd_ref):
        for c in range(2 * PAIRS):
            ref = even_ref if c % 2 == 0 else odd_ref
            ref[jnp.bitwise_xor(c // 2, info_ref[2])] = grad[c * size : (c + 1) * size].astype(ref.dtype)

    @pl.when(info_ref[0] == 0)
    def _():
        write(grad_refs[0], grad_refs[1])

    @pl.when(info_ref[0] != 0)
    def _():
        write(grad_refs[1], grad_refs[0])


def combine(info, chosen, tokens, backs, prior, final):
    _, rows, width = tokens[0].shape
    flat = [x for back in backs for x in back]
    extra = [] if prior is None else [prior]
    if final:
        shape = (PAIRS, width // (2 * PAIRS), 3 * WIDE)
        grads = [jax.ShapeDtypeStruct(shape, f32), jax.ShapeDtypeStruct(shape, bf16)]
    else:
        grads = [jax.ShapeDtypeStruct((width, 3 * WIDE), f32)]
    pieces = [jax.ShapeDtypeStruct((len(chosen), rows, 3 * WIDE), bf16)] * PAIRS
    return pl.pallas_call(
        functools.partial(combine_kernel, chosen, len(tokens), len(extra), final),
        grid=(1,),
        in_specs=[pl.BlockSpec(memory_space=pltpu.SMEM)] + [full_spec(x) for x in tokens + flat + extra],
        out_specs=[full_spec(x) for x in pieces + grads],
        out_shape=pieces + grads,
        compiler_params=room(20),
        cost_estimate=cost(2),
        name="combine",
    )(info, *tokens, *flat, *extra)


def join_small_kernel(keep_ref, got_ref, *outs):
    for d, out in enumerate(outs):
        out[...] = (keep_ref[d] + got_ref[d].astype(f32)).astype(bf16)


def join_small(keep, got):
    return pl.pallas_call(
        join_small_kernel,
        grid=(1,),
        in_specs=[full_spec(keep), full_spec(got)],
        out_specs=[pl.BlockSpec(keep.shape[1:], lambda i: (0, 0))] * PAIRS,
        out_shape=[jax.ShapeDtypeStruct(keep.shape[1:], bf16)] * PAIRS,
        compiler_params=room(6),
        cost_estimate=cost(1),
        name="join_small",
    )(keep, got)


def pack_heads(total):
    kept = total.shape[0] * 3 // 4
    rest = [total[kept:, i * WIDE : (i + 1) * WIDE] for i in range(3)]
    return jnp.concatenate([total[:kept], jnp.concatenate(rest, axis=0)], axis=1)


def share_small_kernel(info_ref, feed_ref, *refs):
    parts, outs = refs[:PAIRS], refs[PAIRS:]
    for step, out in enumerate(outs):
        at = jnp.bitwise_xor(jnp.bitwise_xor(info_ref[1], info_ref[2]), step)
        value = parts[0][...]
        for d in range(1, PAIRS):
            value = jnp.where(at == d, parts[d][...], value)
        value = pack_heads(value)
        if step == 2:
            rows = feed_ref.shape[0]
            out[:rows] = feed_ref[...]
            out[rows:] = value
        else:
            out[...] = value


def share_small(info, feed, parts):
    small = (parts[0].shape[0] * 3 // 4, feed.shape[1])
    large = (small[0] + feed.shape[0], feed.shape[1])
    shapes = [small, small, large, small]
    return pl.pallas_call(
        share_small_kernel,
        grid=(1,),
        in_specs=[pl.BlockSpec(memory_space=pltpu.SMEM)] + [full_spec(x) for x in [feed] + parts],
        out_specs=[pl.BlockSpec(shape, lambda i: (0, 0)) for shape in shapes],
        out_shape=[jax.ShapeDtypeStruct(shape, bf16) for shape in shapes],
        compiler_params=room(6),
        cost_estimate=cost(1),
        name="share_small",
    )(info, feed, *parts)


def state_kernel(base_ref, *refs):
    blocks, weights, out_ref = refs[:PAIRS], refs[PAIRS : 2 * PAIRS], refs[2 * PAIRS]
    total = base_ref[0]
    for ref, w_ref in zip(blocks, weights):
        total = total + dot(ref[0], w_ref[...], NT)
    out_ref[0] = total


def add_state(at, base, blocks, weights):
    rows, width = base.shape[1:]
    count = blocks[0].shape[0]
    spec = pl.BlockSpec((1, rows, width), lambda i: (at + i, 0, 0))
    return pl.pallas_call(
        state_kernel,
        grid=(count,),
        in_specs=[spec]
        + [pl.BlockSpec((1,) + b.shape[1:], lambda i: (i, 0, 0)) for b in blocks]
        + [full_spec(w) for w in weights],
        out_specs=spec,
        out_shape=jax.ShapeDtypeStruct(base.shape, base.dtype),
        input_output_aliases={0: 0},
        compiler_params=room(10),
        cost_estimate=cost(2.5 * count),
        name="add_state",
    )(base, *blocks, *weights)


def choose_kernel(info_ref, near_ref, far_ref, out_ref):
    close = jnp.bitwise_xor(info_ref[1], info_ref[2]) < 2
    out_ref[...] = jnp.where(close, near_ref[...], far_ref[...])


def choose(info, near, far):
    return pl.pallas_call(
        choose_kernel,
        grid=(1,),
        in_specs=[pl.BlockSpec(memory_space=pltpu.SMEM), full_spec(near), full_spec(far)],
        out_specs=full_spec(near),
        out_shape=jax.ShapeDtypeStruct(near.shape, bf16),
        compiler_params=room(6),
        cost_estimate=cost(1),
        name="choose",
    )(info, near, far)


def assemble_kernel(info_ref, mine_ref, other_ref, out_ref):
    half = mine_ref.shape[0]
    out_ref[:half] = jnp.where(info_ref[0] == 0, mine_ref[...], other_ref[...])
    out_ref[half:] = jnp.where(info_ref[0] == 0, other_ref[...], mine_ref[...])


def assemble(info, mine, other):
    shape = (2 * mine.shape[0], mine.shape[1])
    return pl.pallas_call(
        assemble_kernel,
        grid=(1,),
        in_specs=[pl.BlockSpec(memory_space=pltpu.SMEM), full_spec(mine), full_spec(other)],
        out_specs=pl.BlockSpec(shape, lambda i: (0, 0)),
        out_shape=jax.ShapeDtypeStruct(shape, bf16),
        compiler_params=room(6),
        cost_estimate=cost(1),
        name="assemble",
    )(info, mine, other)


def keep_scalar(block):
    tail = block[-8:]
    total = tail[:, :WIDE] + tail[:, WIDE : 2 * WIDE]
    high = total.astype(bf16).astype(f32)
    split = jnp.concatenate([high, total - high, tail[:, 2 * WIDE :]], axis=1)
    row = lax.broadcasted_iota(jnp.int32, tail.shape, 0)
    tail = jnp.where(row == 6, split, tail)
    return tail if block.shape[0] == 8 else jnp.concatenate([block[:-8], tail], axis=0)


def flat_rows(ref):
    return ref[...].reshape(-1, ref.shape[-1])


def write_pieces(info_ref, even_ref, odd_ref, grads, small):
    pieces = 2 * PAIRS * even_ref.shape[1]

    def write(keep_ref, give_ref):
        for c in range(pieces):
            ref = keep_ref if c % 2 == 0 else give_ref
            order = jnp.bitwise_xor((c // 2) % PAIRS, info_ref[2])
            repeat = c // (2 * PAIRS)
            at = 0
            for grad in grads:
                size = grad.shape[0] // pieces
                ref[order, repeat, 0, at : at + size] = grad[c * size : (c + 1) * size]
                at += size
            if small is not None:
                ref[order, repeat, 0, at : at + 8] = small if c == 0 else jnp.zeros_like(small)

    @pl.when(info_ref[0] == 0)
    def _():
        write(even_ref, odd_ref)

    @pl.when(info_ref[0] != 0)
    def _():
        write(odd_ref, even_ref)


def outer_grad_kernel(
    info_ref, a0_ref, a1_ref, a2_ref, a3_ref, ilow_ref, gfeed_ref, gbranch_ref, even_ref, odd_ref
):
    g_outer = dot(flat_rows(ilow_ref), flat_rows(gfeed_ref), TN).astype(bf16)
    order = jnp.bitwise_xor(pl.program_id(0), info_ref[2])
    low, high = order % 2 == 0, order < 2
    att = jnp.where(
        high,
        jnp.where(low, flat_rows(a0_ref), flat_rows(a1_ref)),
        jnp.where(low, flat_rows(a2_ref), flat_rows(a3_ref)),
    )
    g_out = dot(att, flat_rows(gbranch_ref), TN).astype(bf16)
    write_pieces(info_ref, even_ref, odd_ref, (g_outer, g_out), None)


def inner_grad_kernel(info_ref, nlow_ref, gin_ref, vsum_ref, bsum_ref, even_ref, odd_ref):
    g_in = dot(flat_rows(nlow_ref), flat_rows(gin_ref), TN).astype(bf16)
    vectors = sum(vsum_ref[s] for s in range(vsum_ref.shape[0]))
    bias = sum(bsum_ref[s] for s in range(bsum_ref.shape[0]))
    width = g_in.shape[1]
    low = jnp.concatenate([vectors, jnp.zeros((8, width - WIDE), f32)], axis=1)
    row = lax.broadcasted_iota(jnp.int32, (8, width), 0)
    small = keep_scalar(jnp.where(row == 7, bias, low)).astype(bf16)
    write_pieces(info_ref, even_ref, odd_ref, (g_in,), small)


def split_grads(kernel, name, info, arrays, specs, piece, width, ctx):
    shape = (PAIRS, ctx // (2 * PAIRS), PAIRS, piece, width)
    out_spec = pl.BlockSpec(shape[:2] + (1, piece, width), lambda z, info: (0, 0, z, 0, 0))
    return pl.pallas_call(
        kernel,
        grid_spec=pltpu.PrefetchScalarGridSpec(
            num_scalar_prefetch=1, grid=(PAIRS,), in_specs=specs, out_specs=[out_spec, out_spec]
        ),
        out_shape=[jax.ShapeDtypeStruct(shape, bf16)] * 2,
        compiler_params=room(24),
        cost_estimate=cost(4.5),
        name=name,
    )(info, *arrays)


def hidden_spec(array):
    seqs, rows, hidden = array.shape
    return pl.BlockSpec(
        (seqs, rows, hidden // PAIRS), lambda z, info: (0, 0, lax.rem(z - info[1] + PAIRS, PAIRS))
    )


def outer_grads(info, att, ilow, gfeed, gbranch, ctx):
    width = gfeed.shape[2]
    piece = (ilow.shape[2] // PAIRS + width // PAIRS) // ctx
    arrays = [*att, ilow, gfeed, gbranch]
    specs = [full_spec(x) for x in arrays]
    specs[PAIRS] = hidden_spec(ilow)
    return split_grads(outer_grad_kernel, "outer_grads", info, arrays, specs, piece, width, ctx)


def inner_grads(info, nlow, gin, vsum, bsum, ctx):
    width = nlow.shape[2]
    seqs = vsum.shape[0]
    specs = [
        full_spec(nlow),
        hidden_spec(gin),
        pl.BlockSpec((seqs, 8, WIDE), lambda z, info: (0, 0, z)),
        hidden_spec(bsum),
    ]
    piece = width // ctx + 8
    return split_grads(
        inner_grad_kernel, "inner_grads", info, [nlow, gin, vsum, bsum], specs, piece, gin.shape[2] // PAIRS, ctx
    )


def join_kernel(scalar, keep_ref, got_ref, *outs):
    for d, out in enumerate(outs):
        for r in range(out.shape[0]):
            total = keep_ref[d, r, 0].astype(f32) + got_ref[d, r, 0].astype(f32)
            out[r, 0] = (keep_scalar(total) if scalar else total).astype(bf16)


def join(keep, got, scalar):
    _, repeats, wsh, piece, width = keep.shape
    spec = pl.BlockSpec((PAIRS, repeats, 1, piece, width), lambda z: (0, 0, z, 0, 0))
    return pl.pallas_call(
        functools.partial(join_kernel, scalar),
        grid=(wsh,),
        in_specs=[spec, spec],
        out_specs=[pl.BlockSpec((repeats, 1, piece, width), lambda z: (0, z, 0, 0))] * PAIRS,
        out_shape=[jax.ShapeDtypeStruct(keep.shape[1:], bf16)] * PAIRS,
        compiler_params=room(16),
        cost_estimate=cost(1.5),
        name="join",
    )(keep, got)


def share_kernel(info_ref, *refs):
    firsts, seconds, outs = refs[:PAIRS], refs[PAIRS : 2 * PAIRS], refs[2 * PAIRS :]
    for step in range(PAIRS):
        place = jnp.bitwise_xor(info_ref[1], step)
        out = outs[step % 2]
        for r in range(out.shape[0]):
            totals = []
            for parts in (firsts, seconds):
                total = parts[0][r, place].astype(f32)
                for part in parts[1:]:
                    total = total + part[r, place].astype(f32)
                totals.append(total)
            size = totals[0].shape[0]
            out[r, step // 2, :size] = totals[0].astype(bf16)
            out[r, step // 2, size:] = keep_scalar(totals[1]).astype(bf16)


def share_parts(info, firsts, seconds):
    repeats, wsh, piece, width = firsts[0].shape
    shape = (repeats, wsh // 2, piece + seconds[0].shape[2], width)
    return pl.pallas_call(
        share_kernel,
        grid=(1,),
        in_specs=[pl.BlockSpec(memory_space=pltpu.SMEM)] + [full_spec(x) for x in firsts + seconds],
        out_specs=[pl.BlockSpec(shape, lambda i: (0, 0, 0, 0))] * 2,
        out_shape=[jax.ShapeDtypeStruct(shape, bf16)] * 2,
        compiler_params=room(16),
        cost_estimate=cost(1.5),
        name="share",
    )(info, *firsts, *seconds)


def halve_kernel(keep_ref, got_ref, own_ref, send_ref):
    for at, out in enumerate((own_ref, send_ref)):
        out[...] = keep_scalar(keep_ref[at].astype(f32) + got_ref[at].astype(f32)).astype(bf16)


def halve(keep, got):
    shape = keep.shape[1:]
    return pl.pallas_call(
        halve_kernel,
        grid=(1,),
        in_specs=[full_spec(keep), full_spec(got)],
        out_specs=[pl.BlockSpec(shape, lambda i: (0, 0))] * 2,
        out_shape=[jax.ShapeDtypeStruct(shape, bf16)] * 2,
        compiler_params=room(6),
        cost_estimate=cost(1),
        name="halve",
    )(keep, got)


def total_kernel(own_ref, *refs):
    parts, out = refs[:-1], refs[-1]
    rows = own_ref.shape[0]
    if len(parts) == 1:
        out[...] = keep_scalar(own_ref[...].astype(f32) + parts[0][...].astype(f32)).astype(bf16)
        return
    out[:rows] = keep_scalar(own_ref[...].astype(f32) + parts[2][:rows].astype(f32)).astype(bf16)
    total = parts[2][rows:].astype(f32)
    for i in (0, 1, 3):
        total = total + parts[i][...].astype(f32)
    out[rows:] = total.astype(bf16)


def total_parts(own, parts):
    shape = max((x.shape for x in parts), key=lambda x: x[0])
    return pl.pallas_call(
        total_kernel,
        grid=(1,),
        in_specs=[full_spec(x) for x in [own] + parts],
        out_specs=pl.BlockSpec(shape, lambda i: (0, 0)),
        out_shape=jax.ShapeDtypeStruct(shape, bf16),
        compiler_params=room(6),
        cost_estimate=cost(1),
        name="total",
    )(own, *parts)


def unpack_kernel(info_ref, *refs):
    pieces = refs[: 2 * PAIRS]
    outer_ref, out_ref, in_ref, tail_ref, *heads = refs[2 * PAIRS :]
    core, pair = info_ref[0], info_ref[2]
    for side in range(2):
        for d in range(PAIRS):
            ref = pieces[side * PAIRS + d]
            place = jnp.bitwise_xor(pair, d) * 2 + jnp.bitwise_xor(core, side)
            at = 0
            for target in (outer_ref, out_ref, in_ref):
                size = target.shape[0] // (2 * PAIRS)
                start = pl.multiple_of(place * size, size)
                target[pl.ds(start, size)] = ref[at : at + size].astype(f32)
                at += size

            @pl.when(place == 0)
            def _(ref=ref, at=at):
                tail_ref[...] = ref[at : at + 8].astype(f32)

            at += 8
            size = heads[0].shape[0] // (2 * PAIRS)
            kept = size * 3 // 4
            for i, target in enumerate(heads):
                start = pl.multiple_of(place * size, size)
                target[pl.ds(start, kept)] = ref[at : at + kept, i * WIDE : (i + 1) * WIDE].astype(f32)
                more = (size - kept) * i + at
                target[pl.ds(start + kept, size - kept)] = ref[more : more + size - kept, 3 * WIDE :].astype(f32)


def unpack(info, mine, other, part, out_rows):
    width = mine[0].shape[1]
    shapes = [(part, width), (out_rows, width), (width, part), (8, width)] + [(width, WIDE)] * 3
    return pl.pallas_call(
        unpack_kernel,
        grid=(1,),
        in_specs=[pl.BlockSpec(memory_space=pltpu.SMEM)] + [full_spec(x) for x in mine + other],
        out_specs=[pl.BlockSpec(shape, lambda i: (0, 0)) for shape in shapes],
        out_shape=[jax.ShapeDtypeStruct(shape, f32) for shape in shapes],
        compiler_params=room(16),
        cost_estimate=cost(3),
        name="unpack",
    )(info, *mine, *other)


def gelu_parts(x):
    half = 0.5 * (1.0 + lax.erf(x * 2.0 ** (-0.5)))
    density = jnp.exp(-0.5 * x * x) * (2.0 * math.pi) ** (-0.5)
    return x * half, half + x * density


def mean_rows(x):
    return jnp.sum(x, axis=1, keepdims=True) * (1.0 / x.shape[1])


def norm_rows(z, gain, shift):
    centre = z - mean_rows(z)
    inverse = lax.rsqrt(mean_rows(centre * centre) + epsilon)
    normed = centre * inverse
    return normed * gain + shift, normed, inverse


def norm_back(g, normed, inverse, gain):
    scaled = g * gain
    return inverse * (scaled - mean_rows(scaled) - normed * mean_rows(scaled * normed))


def dense_kernel(info_ref, bhalt_ref, *refs):
    mine, other, refs = refs[:PAIRS], refs[PAIRS : 2 * PAIRS], refs[2 * PAIRS :]
    att_refs, refs = refs[:PAIRS], refs[PAIRS:]
    emb_ref, prev_ref, gt_ref, gb_ref, hsum_ref, code_ref, gsum_ref = refs[:7]
    refs = refs[7:]
    final_ref, blend_ref, rows_ref, gprev_ref, base_ref = refs[:5]
    gatt_refs = refs[5:9]
    nlow_ref, ilow_ref, gin_ref, gfeed_ref, gbranch_ref, vsum_ref, bsum_ref = refs[9:16]
    slope_ref, win_ref, wouter_ref, wout_ref, small_ref, sem = refs[16:22]
    buffers, row_sem = refs[22:26], refs[26]
    me = pl.program_id(0)

    def fetch(step):
        slot = lax.rem(step, 2)
        return [
            pltpu.make_async_copy(source.at[step], buffer.at[slot], row_sem.at[i, slot])
            for i, (source, buffer) in enumerate(zip((emb_ref, prev_ref, gt_ref, gb_ref), buffers))
        ]

    @pl.when(me == 0)
    def _():
        for one in fetch(0):
            one.start()

    @pl.when(me + 1 < pl.num_programs(0))
    def _():
        for one in fetch(me + 1):
            one.start()

    blocks, columns, width = win_ref.shape
    cut = wout_ref.shape[1] // 2
    core, zed, pair = info_ref[0], info_ref[1], info_ref[2]

    def load(firsts, seconds):
        copies = []

        def copy(source, start, size, target):
            copies.append(pltpu.make_async_copy(source.at[pl.ds(start, size)], target, sem.at[len(copies)]))

        for a in range(PAIRS):
            place = lax.rem(zed + a, PAIRS)
            order = jnp.bitwise_xor(place, pair)
            first, second = firsts[(-a) % PAIRS], seconds[a]
            copy(first, columns, cut, wout_ref.at[order, pl.ds(0, cut)])
            copy(second, width, cut, wout_ref.at[order, pl.ds(cut, cut)])
            copy(first, columns + cut, SMALL, small_ref.at[place])
            copy(first, 0, columns, win_ref.at[a])
            copy(second, 0, width, wouter_ref.at[a])
        for one in copies:
            one.start()
        for one in copies:
            one.wait()

    @pl.when((pl.program_id(0) == 0) & (core == 0))
    def _():
        load(mine, other)

    @pl.when((pl.program_id(0) == 0) & (core != 0))
    def _():
        load(other, mine)

    for one in fetch(me):
        one.wait()
    emb, prev, gt, gb = [buffer[lax.rem(me, 2)] for buffer in buffers]
    att = jnp.concatenate([ref[0] for ref in att_refs], axis=1)
    w_out = wout_ref[...].reshape(emb.shape[1], emb.shape[1])
    b_outer, g1, s1, g2, s2, halt = [
        jnp.concatenate([small_ref[a, i + 1 : i + 2, :WIDE] for a in range(PAIRS)], axis=1).astype(f32)
        for i in range(6)
    ]
    at = pl.ds(pl.program_id(0), 1)
    row = lax.broadcasted_iota(jnp.int32, (8, emb.shape[0]), 0)
    lines = jnp.where(row == 0, hsum_ref[at], jnp.where(row == 1, code_ref[at].astype(f32), gsum_ref[at]))
    cols = jnp.transpose(lines)
    sum_col, code_col, gsum_col = cols[:, 0:1], cols[:, 1:2], cols[:, 2:3]
    z1 = emb + dot(att, w_out)
    one, n1, i1 = norm_rows(z1, g1, s1)
    nlow = one.astype(bf16)
    nlow_ref[0] = nlow
    feed = None
    for j in range(blocks):
        pre = dot(nlow, win_ref[j]) + small_ref[lax.rem(zed + j, PAIRS), 0:1, :].astype(f32)
        act, slope = gelu_parts(pre)
        act = act.astype(bf16)
        ilow_ref[0, :, j * width : (j + 1) * width] = act
        slope_ref[:, j * width : (j + 1) * width] = slope
        part = dot(act, wouter_ref[j])
        feed = part if feed is None else feed + part
    z2 = one + (feed + b_outer)
    final, n2, i2 = norm_rows(z2, g2, s2)
    halt_logit = jnp.sum(emb * halt, axis=1, keepdims=True) + bhalt_ref[0, 0]
    halt_prob = jax.nn.sigmoid(halt_logit)
    running = (code_col > 0.5).astype(f32)
    halting = (code_col > 1.5).astype(f32)
    update = running * (halting * (1.0 - sum_col) + (1.0 - halting) * halt_prob)
    prev = prev.astype(f32)
    gb = gb.astype(f32)
    final_ref[0] = final.astype(bf16)
    blend_ref[0] = (prev * (1.0 - update) + final * update).astype(bf16)
    gprev_ref[0] = gb * (1.0 - update)
    g_update = jnp.sum(gb * (final - prev), axis=1, keepdims=True) + gsum_col
    g_halt_sum = gsum_col - running * halting * g_update
    g_logit = g_update * running * (1.0 - halting) * halt_prob * (1.0 - halt_prob)
    lane = lax.broadcasted_iota(jnp.int32, (emb.shape[0], WIDE), 1)
    packed = jnp.where(lane == 0, sum_col + update, jnp.where(lane == 1, g_halt_sum, 0.0))
    rows_ref[0] = jnp.transpose(packed)[0:8]
    gf = gt.astype(f32) + update * gb
    g_two = norm_back(gf, n2, i2, g2)
    gfeed = g_two.astype(bf16)
    gfeed_ref[0] = gfeed
    g_one = g_two
    for j in range(blocks):
        at = slice(j * width, (j + 1) * width)
        back = dot(gfeed, wouter_ref[j], NT)
        gin_f = back * slope_ref[:, at]
        gin = gin_f.astype(bf16)
        gin_ref[0, :, at] = gin
        bsum_ref[0, :, at] = jnp.sum(gin.astype(f32), axis=0, keepdims=True)
        g_one = g_one + dot(gin, win_ref[j], NT)
    g_emb = norm_back(g_one, n1, i1, g1)
    gbranch = g_emb.astype(bf16)
    gbranch_ref[0] = gbranch
    gatt = dot(gbranch, w_out, NT).astype(bf16)
    for d, ref in enumerate(gatt_refs):
        ref[0] = gatt[:, d * WIDE : (d + 1) * WIDE]
    base_ref[0] = g_emb + g_logit * halt
    total = lambda x: jnp.sum(x, axis=0, keepdims=True)
    logit_sum = jnp.broadcast_to(total(g_logit), (1, emb.shape[1]))
    vsum_ref[0] = jnp.concatenate(
        [
            total(gfeed.astype(f32)),
            total(g_one * n1),
            total(g_one),
            total(gf * n2),
            total(gf),
            total(g_logit * emb),
            logit_sum,
            jnp.zeros((1, emb.shape[1]), f32),
        ],
        axis=0,
    )


def dense(info, b_halt, mine, other, emb, att, prev, gt, gb, marks, part, out_rows):
    seqs, rows, width = emb.shape
    hidden = PAIRS * part
    outside = pl.BlockSpec(memory_space=pltpu.HBM)
    scalars = pl.BlockSpec(memory_space=pltpu.SMEM)
    rowspec = lambda w: pl.BlockSpec((1, rows, w), lambda s: (s, 0, 0))
    shape = lambda w, kind: jax.ShapeDtypeStruct((seqs, rows, w), kind)
    return pl.pallas_call(
        dense_kernel,
        grid=(seqs,),
        in_specs=[scalars, scalars]
        + [outside] * (2 * PAIRS)
        + [rowspec(WIDE)] * PAIRS
        + [outside] * 4
        + [full_spec(x) for x in marks],
        out_specs=[
            rowspec(width),
            rowspec(width),
            pl.BlockSpec((1, 8, rows), lambda s: (s, 0, 0)),
            rowspec(width),
            rowspec(width),
            rowspec(WIDE),
            rowspec(WIDE),
            rowspec(WIDE),
            rowspec(WIDE),
            rowspec(width),
            rowspec(hidden),
            rowspec(hidden),
            rowspec(width),
            rowspec(width),
            pl.BlockSpec((1, 8, width), lambda s: (s, 0, 0)),
            pl.BlockSpec((1, 1, hidden), lambda s: (s, 0, 0)),
        ],
        out_shape=[
            shape(width, bf16),
            shape(width, bf16),
            jax.ShapeDtypeStruct((seqs, 8, rows), f32),
            shape(width, f32),
            shape(width, f32),
            shape(WIDE, bf16),
            shape(WIDE, bf16),
            shape(WIDE, bf16),
            shape(WIDE, bf16),
            shape(width, bf16),
            shape(hidden, bf16),
            shape(hidden, bf16),
            shape(width, bf16),
            shape(width, bf16),
            jax.ShapeDtypeStruct((seqs, 8, width), f32),
            jax.ShapeDtypeStruct((seqs, 1, hidden), f32),
        ],
        scratch_shapes=[
            pltpu.VMEM((rows, hidden), f32),
            pltpu.VMEM((PAIRS, width, part), bf16),
            pltpu.VMEM((PAIRS, part, width), bf16),
            pltpu.VMEM((PAIRS, out_rows, width), bf16),
            pltpu.VMEM((PAIRS, SMALL, width), bf16),
            pltpu.SemaphoreType.DMA((5 * PAIRS,)),
            pltpu.VMEM((2, rows, width), f32),
            pltpu.VMEM((2, rows, width), bf16),
            pltpu.VMEM((2, rows, width), bf16),
            pltpu.VMEM((2, rows, width), bf16),
            pltpu.SemaphoreType.DMA((4, 2)),
        ],
        compiler_params=room(36),
        cost_estimate=cost(20),
        name="dense",
    )(info, b_halt, *mine, *other, *att, emb, prev, gt, gb, *marks)


def frequencies(half):
    return jnp.exp(-math.log(10000.0) * jnp.arange(half, dtype=f32) / (half - 1))


def position_rows(first, rows, columns):
    half = columns // 2
    freq = frequencies(half)[None, :]
    coarse = (first + 16 * jnp.arange(rows // 16, dtype=jnp.int32)).astype(f32)[:, None] * freq
    fine = jnp.arange(16, dtype=f32)[:, None] * freq
    sa, ca = jnp.sin(coarse)[:, None], jnp.cos(coarse)[:, None]
    sb, cb = jnp.sin(fine)[None], jnp.cos(fine)[None]
    both = jnp.concatenate([sa * cb + ca * sb, ca * cb - sa * sb], axis=2)
    return both.reshape(rows, columns)


def step_rows(columns):
    half = columns // 2
    angles = jnp.arange(4, dtype=f32)[:, None] * frequencies(half)[None, :]
    return jnp.concatenate([jnp.sin(angles), jnp.cos(angles)], axis=1)


def body(
    hidden_state,
    prev_state,
    halt_sum,
    halt_code,
    step_count,
    w_query,
    w_key,
    w_value,
    w_out,
    w_inner,
    b_inner,
    w_outer,
    b_outer,
    gain_attention,
    shift_attention,
    gain_feedforward,
    shift_feedforward,
    w_halt,
    b_halt,
    grad_transformed,
    grad_blended,
    grad_sum,
):
    seqs, rows, width = hidden_state.shape
    ctx = lax.axis_size("ctx")
    wsh = lax.axis_size("wsh")
    repeats = ctx // (2 * PAIRS)
    me = lax.axis_index("ctx")
    zed = lax.axis_index("wsh")
    core = me % 2
    pair = (me // 2) % PAIRS

    def swap(x, distance):
        return lax.ppermute(x, "ctx", [(i, i ^ distance) for i in range(ctx)])

    def sibling(x):
        return swap(x, 1)

    def partners(x, distance):
        return swap(x, 2 * distance)

    freq_rows = position_rows(me * rows, rows, width)
    table = step_rows(width)
    steps = step_count[:, :, None]
    step_signal = jnp.where(
        steps == 0, table[0], jnp.where(steps == 1, table[1], jnp.where(steps == 2, table[2], table[3]))
    )
    emb = hidden_state.astype(f32) + freq_rows[None] + step_signal
    emb_low = emb.astype(bf16)

    after = lambda x, *others: lax.optimization_barrier((x,) + others)[0]

    info = jnp.stack([core, zed, pair]).astype(jnp.int32)
    ring = [
        (c * wsh + z, c * wsh + (z + (1 if c % 2 == 0 else -1)) % wsh) for c in range(ctx) for z in range(wsh)
    ]
    turn = lambda x: lax.ppermute(x, ("ctx", "wsh"), ring)
    out_rows = w_out.shape[0]
    part = w_inner.shape[1]
    half = rows // 2

    tokens = [emb_low] + [partners(emb_low, d) for d in (1, 2)]
    pair_of = lambda c: (c // 2) % PAIRS
    held = pack(info, [w_query, w_key, w_value])
    hop = lambda x, starts, step: lax.ppermute(
        x,
        ("ctx", "wsh"),
        [(c * wsh + (pair_of(c) ^ z), c * wsh + (pair_of(c) ^ z ^ step)) for c in range(ctx) for z in starts],
    )
    near = jnp.where(zed == pair, held, hop(held, (0,), 1))
    far = hop(near, (0, 1), 2)
    tokens.append(partners(tokens[2][:, :half], 1))
    tokens.append(partners(tokens[1][:, half:], 2))
    vectors = [b_outer, gain_attention, shift_attention, gain_feedforward, shift_feedforward, w_halt]
    feed = pack_feed(after(info, held), w_inner, w_outer, w_out, b_inner, vectors)
    feed_mine = [feed, turn(feed)]
    chosen = choose(after(info, feed_mine[1], *tokens[1:3]), near, far)
    w_mine = assemble(info, chosen, sibling(chosen))

    groups = [[r * 2 * PAIRS + i for r in range(repeats)] for i in range(2 * PAIRS)]
    q_list, kvs_list, fold = [], [], None
    w_now = w_mine
    own_list = []
    for s in range(seqs):
        q, own = project(s, tokens, w_now)
        w_now = after(w_mine, q)
        q_list.append(q)
        own_list.append(own)

    def keys_values(own):
        other = sibling(own)
        if repeats == 1:
            return [own, other]
        both = jnp.concatenate([own, other], axis=1)
        return [lax.all_gather(both, "ctx", axis=1, tiled=True, axis_index_groups=groups)]

    feed_mine.append(turn(feed_mine[1]))
    kvs_list = [keys_values(own) for own in own_list]
    fold = attend(0, seqs, q_list[0], kvs_list[0], None)
    feed_mine.append(turn(after(feed_mine[2], fold[1])))
    fold = attend(1, seqs, after(q_list[1], feed_mine[2], kvs_list[2][-1]), kvs_list[1], fold)
    feed_other = [sibling(after(x, fold[1])) for x in feed_mine[:2]]
    fold = attend(2, seqs, after(q_list[2], *feed_other), kvs_list[2], fold)
    o32, mass, *low = fold
    att = [low[0]] + [partners(low[d], d) for d in range(1, PAIRS)]
    feed_other.append(sibling(after(feed_mine[2], mass)))
    feed_other.append(sibling(after(feed_mine[3], *att[1:])))
    w_order = [w_mine] + [partners(after(w_mine, *att[1:]), d) for d in range(1, PAIRS)]

    (
        final,
        blended,
        row_out,
        grad_prev,
        base,
        gatt0,
        gatt1,
        gatt2,
        gatt3,
        nlow,
        ilow,
        gin,
        gfeed,
        gbranch,
        vsum,
        bsum,
    ) = dense(
        info, b_halt.reshape(1, 1), feed_mine, feed_other, emb, att, prev_state, grad_transformed, grad_blended,
        [halt_sum, halt_code, grad_sum], part, out_rows,
    )
    new_sum = row_out[:, 0]
    grad_halt_sum = row_out[:, 1]
    gs = [gatt0] + [partners(x, d + 1) for d, x in enumerate((gatt1, gatt2, gatt3))]

    keep_a, give_a = outer_grads(after(info, vsum, *w_order[1:]), att, ilow, gfeed, gbranch, ctx)
    keep_b, give_b = inner_grads(after(info, keep_a), nlow, gin, vsum, bsum, ctx)
    joined_a = join(after(keep_a, keep_b), sibling(give_a), False)

    def spread_pieces(pieces):
        return [pieces[0]] + [partners(pieces[d], d) for d in range(1, PAIRS)]

    shared_a = spread_pieces(joined_a)

    kinds = [f32, bf16] if repeats == 1 else [bf16]

    def split_back(s, token):
        dq, *dkv = attend_back(s, q_list[s], gs, o32, token, kvs_list[s], kinds)
        if repeats == 1:
            kept, sent = dkv
        else:
            summed = lax.psum_scatter(
                dkv[0], "ctx", scatter_dimension=1, tiled=True, axis_index_groups=groups
            )
            kept, sent = summed[:, : PAIRS * rows].astype(f32), summed[:, PAIRS * rows :]
        return dq, kept, sent

    backs = [split_back(0, after(mass, *joined_a))]
    joined_b = join(after(keep_b, backs[0][0], *shared_a), sibling(give_b), True)
    shared_b = spread_pieces(joined_b)
    backs.append(split_back(1, after(mass, *joined_b)))
    got = lambda back, *others: back[:2] + (sibling(after(back[2], *others)),)
    share_keep, share_send = share_parts(after(info, backs[1][0]), shared_a, shared_b)
    if repeats > 1:
        share_keep, share_send = (
            lax.psum_scatter(x, "ctx", scatter_dimension=0, tiled=True, axis_index_groups=groups)
            for x in (share_keep, share_send)
        )
    cross = lambda x, step: lax.ppermute(x, "wsh", [(z, z ^ step) for z in range(wsh)])
    moved = cross(share_send[0], 1)
    *pieces, gq = combine(
        after(info, share_keep), (0, 1), tokens, [got(backs[0]), got(backs[1], share_keep)], None, False
    )
    blocks = spread_pieces(pieces)
    backs.append(split_back(2, after(mass, gq)))
    own, sent = halve(after(share_keep[0], backs[2][0], *blocks[1:]), moved)
    made = combine(info, (2,), tokens, [got(backs[2], own)], gq, repeats == 1)
    pieces, keep, give = made[:PAIRS], made[PAIRS], made[-1]
    block = [pieces[0]] + [partners(pieces[d], d) for d in (1, 2)]
    if repeats == 1:
        heads = share_small(after(info, *block), sent, spread_pieces(join_small(keep, sibling(give))))
        block.append(partners(after(pieces[3], heads[0]), 3))
        heads = [heads[0]] + [cross(heads[step], step) for step in range(1, wsh)]
        grad_state = add_state(0, after(base, heads[0]), blocks, w_order)
        share = total_parts(after(own, grad_state), heads)
        grad_state = add_state(2, after(grad_state, share), block, w_order)
        mine = spread_pieces([share] * PAIRS)
        (grad_w_outer, grad_w_out, grad_w_inner, tail, grad_w_query, grad_w_key, grad_w_value) = unpack(
            info, mine, [sibling(after(x, grad_state)) for x in mine], part, out_rows
        )
    else:
        block.append(partners(pieces[3], 3))
        share = total_parts(own, [cross(sent, 2)])
        grad_state = add_state(2, add_state(0, base, blocks, w_order), block, w_order)
        whole = lax.all_gather(share, "ctx", axis=0).astype(f32)
        a, b, c = part // ctx, out_rows // ctx, width // ctx
        grad_w_outer = whole[:, :a].reshape(part, width)
        grad_w_out = whole[:, a : a + b].reshape(out_rows, width)
        grad_w_inner = whole[:, a + b : a + b + c].reshape(width, part)
        tail = whole[0, a + b + c :]
        own = lax.dynamic_update_index_in_dim(jnp.zeros((wsh,) + keep.shape, f32), keep, pair, 0)
        own = lax.psum(lax.psum_scatter(own.astype(bf16), "wsh", scatter_dimension=0).astype(f32), "ctx")
        grad_w_query, grad_w_key, grad_w_value = (own[:, i * WIDE : (i + 1) * WIDE] for i in range(3))
    grad_b_inner = tail[7]
    vec_grads = [tail[i, :out_rows] for i in range(6)]
    grad_b_halt = tail[6, :1] + tail[6, WIDE : WIDE + 1]

    return (
        final,
        blended,
        new_sum,
        grad_state,
        grad_prev,
        grad_halt_sum,
        grad_w_query,
        grad_w_key,
        grad_w_value,
        grad_w_out,
        grad_w_inner,
        grad_b_inner,
        grad_w_outer,
        vec_grads[0],
        vec_grads[1],
        vec_grads[2],
        vec_grads[3],
        vec_grads[4],
        vec_grads[5],
        grad_b_halt,
    )


def solution(mesh):
    rows = P("wsh", "ctx", None)
    marks = P("wsh", "ctx")
    column, row, vector = P(None, "wsh"), P("wsh", None), P("wsh")
    in_specs = (
        (rows, rows, marks, marks, marks, column, column, column, row, column, vector, row)
        + (vector,) * 6
        + (P(), rows, rows, marks)
    )
    out_specs = (
        (rows, rows, marks, rows, rows, marks, column, column, column, row, column, vector, row)
        + (vector,) * 6
        + (P(),)
    )
    return jax.shard_map(body, mesh=mesh, in_specs=in_specs, out_specs=out_specs, check_vma=False)
```

```python
import functools
import math

import jax
import jax.numpy as jnp
from jax import lax
from jax.experimental import pallas as pl
from jax.experimental.pallas import tpu as pltpu
from jax.sharding import PartitionSpec as P

HEADS = 8
PAIRS = 4
WIDE = 128
SMALL = 16
epsilon = 1e-06
f32 = jnp.float32
bf16 = jnp.bfloat16
LOG2E = math.log2(math.e)
NT = (((1,), (1,)), ((), ()))
TN = (((0,), (0,)), ((), ()))
NN = (((1,), (0,)), ((), ()))
MIB = 1024 * 1024
KEYS = 256


def room(mebibytes):
    return pltpu.CompilerParams(vmem_limit_bytes=int(mebibytes) * MIB)


def cost(micros):
    return pl.CostEstimate(flops=int(micros * 1.1e9), bytes_accessed=1024, transcendentals=0)


def dot(a, b, dims=NN):
    return lax.dot_general(a, b, dims, preferred_element_type=f32)


def lane_masks(shape):
    lane = lax.broadcasted_iota(jnp.int32, shape, 1)
    return lane < WIDE // 2


def largest_squares(refs):
    same = (
        lax.broadcasted_iota(jnp.int32, (WIDE, WIDE), 0) // (WIDE // 2)
        == lax.broadcasted_iota(jnp.int32, (WIDE, WIDE), 1) // (WIDE // 2)
    ).astype(bf16)
    most = None
    for ref in refs:
        for start in range(0, ref.shape[1], 1024):
            x = ref[0, start : start + 1024, :WIDE].astype(f32)
            top = jnp.max(dot((x * x).astype(bf16), same), axis=0, keepdims=True)
            most = top if most is None else jnp.maximum(most, top)
    return most


def attend_kernel(blocks, carried, q_ref, *refs):
    kv_refs = refs[:blocks]
    refs = refs[blocks + carried :]
    flag_ref = refs[-1]
    o_ref, mass_ref, low_refs = refs[0], refs[1], refs[2:-1]
    scale = 0.125 * LOG2E
    index = pl.program_id(0)
    step = o_ref.shape[1]

    @pl.when(index == 0)
    def _():
        bound = jnp.max(largest_squares([q_ref]) * largest_squares(kv_refs))
        flag_ref[0] = (bound < 0.98 * (8.0 * 70.0) ** 2).astype(jnp.int32)

    q = q_ref[0, pl.ds(pl.multiple_of(index * step, step), step)]
    first = lane_masks(q.shape)
    none = jnp.zeros_like(q)
    size = KEYS
    chunks = [(ref, start) for ref in kv_refs for start in range(0, ref.shape[1], size)]

    def finish(outs, masses):
        out = jnp.where(first, outs[0], outs[1])
        o_ref[0] = out
        low = out.astype(bf16)
        block = low_refs[0].shape[1]
        for d, ref in enumerate(low_refs):

            @pl.when(index == d * block // step)
            def _(ref=ref, at=d * block % step):
                ref[0] = low[at : at + block]

        table = jnp.where(first, masses[0], masses[1])
        turned = jnp.transpose(table)
        mass_ref[0] = jnp.concatenate([turned[0:4], turned[64:68]], axis=0)

    def masked(head):
        return jnp.where(first, q, none) if head == 0 else jnp.where(first, none, q)

    def lanes(e):
        return sum(e[:, i : i + 128] for i in range(0, size, 128))

    @pl.when(flag_ref[0] == 1)
    def _():
        outs, masses = [], []
        for head in range(2):
            mine = masked(head)
            total = None
            weighted = None
            for ref, start in chunks:
                e = jnp.exp2(dot(mine, ref[0, start : start + size, :WIDE], NT) * scale)
                w = dot(e.astype(bf16), ref[0, start : start + size, WIDE:])
                total = lanes(e) if total is None else total + lanes(e)
                weighted = w if weighted is None else weighted + w
            total = jnp.sum(total, axis=1, keepdims=True)
            outs.append(weighted * (1.0 / total))
            masses.append(jnp.log2(total))
        finish(outs, masses)

    @pl.when(flag_ref[0] != 1)
    def _():
        some = 128
        left = lane_masks((some, WIDE))
        block = low_refs[0].shape[1]

        def rows_body(r, carry):
            start = pl.multiple_of(r * some, some)
            x = q_ref[0, pl.ds(pl.multiple_of(index * step + start, some), some)]
            outs, masses = [], []
            for head in range(2):
                mine = jnp.where(left == (head == 0), x, jnp.zeros_like(x))
                fold = (
                    jnp.zeros((some, WIDE), f32),
                    jnp.full((some, 1), -jnp.inf, f32),
                    jnp.zeros((some, 1), f32),
                )
                for ref in kv_refs:

                    def body(i, fold, ref=ref, mine=mine):
                        weighted, top, total = fold
                        at = pl.ds(pl.multiple_of(i * size, size), size)
                        scores = dot(mine, ref[0, at, :WIDE], NT) * scale
                        now = jnp.maximum(top, jnp.max(scores, axis=1, keepdims=True))
                        factor = jnp.exp2(top - now)
                        e = jnp.exp2(scores - now)
                        total = total * factor + jnp.sum(e, axis=1, keepdims=True)
                        weighted = weighted * factor + dot(e.astype(bf16), ref[0, at, WIDE:])
                        return weighted, now, total

                    fold = lax.fori_loop(0, ref.shape[1] // size, body, fold)
                weighted, top, total = fold
                outs.append(weighted * (1.0 / total))
                masses.append(top + jnp.log2(total))
            out = jnp.where(left, outs[0], outs[1])
            o_ref[0, pl.ds(start, some)] = out
            low = out.astype(bf16)
            for d, ref in enumerate(low_refs):

                @pl.when((index * step + start) // block == d)
                def _(ref=ref):
                    ref[0, pl.ds(pl.multiple_of(lax.rem(start, block), some), some)] = low

            turned = jnp.transpose(jnp.where(left, masses[0], masses[1]))
            mass_ref[0, :, pl.ds(start, some)] = jnp.concatenate([turned[0:4], turned[64:68]], axis=0)
            return carry

        lax.fori_loop(0, step // some, rows_body, 0)


def attend(at, seqs, q, kvs, before):
    _, rows, _ = q.shape
    block = rows // PAIRS
    keys = sum(kv.shape[1] for kv in kvs)
    step = 2 * block if keys <= 2048 else block
    shapes = [
        jax.ShapeDtypeStruct((seqs, rows, WIDE), f32),
        jax.ShapeDtypeStruct((seqs, 8, rows), f32),
    ] + [jax.ShapeDtypeStruct((seqs, block, WIDE), bf16)] * PAIRS
    carried = len(shapes) if before else 0
    return pl.pallas_call(
        functools.partial(attend_kernel, len(kvs), carried),
        grid=(rows // step,),
        in_specs=[full_spec(q)]
        + [full_spec(kv) for kv in kvs]
        + [pl.BlockSpec(memory_space=pl.ANY)] * carried,
        out_specs=[
            pl.BlockSpec((1, step, WIDE), lambda i: (at, i, 0)),
            pl.BlockSpec((1, 8, step), lambda i: (at, 0, i)),
        ]
        + [pl.BlockSpec((1, block, WIDE), lambda i: (at, 0, 0))] * PAIRS,
        out_shape=shapes,
        input_output_aliases={1 + len(kvs) + i: i for i in range(carried)},
        scratch_shapes=[pltpu.SMEM((1,), jnp.int32)],
        compiler_params=room(24 if keys <= 2048 else 10 + keys // 256),
        cost_estimate=cost(1),
        name="attend",
    )(q, *kvs, *(before or ()))


def attend_back_kernel(blocks, q_ref, *refs):
    g_refs, o_ref, mass_ref = refs[:PAIRS], refs[PAIRS], refs[PAIRS + 1]
    refs = refs[PAIRS + 2 :]
    kv_refs = refs[:blocks]
    dq_ref = refs[blocks]
    dkv_refs = refs[blocks + 1 : 2 * blocks + 1]
    dq_acc = refs[2 * blocks + 1]
    scale = 0.125 * LOG2E
    q = q_ref[0]
    g = jnp.concatenate([ref[0] for ref in g_refs], axis=0)
    first = lane_masks(q.shape)
    none = jnp.zeros_like(q)
    qs = [jnp.where(first, q, none), jnp.where(first, none, q)]
    gs = [jnp.where(first, g, none), jnp.where(first, none, g)]
    product = g.astype(f32) * o_ref[0]
    which = lax.broadcasted_iota(jnp.int32, (8, WIDE), 0) == (
        lax.broadcasted_iota(jnp.int32, (8, WIDE), 1) // (WIDE // 2)
    )
    deltas = lax.dot_general(
        which.astype(f32), product, NT, precision=lax.Precision.HIGHEST, preferred_element_type=f32
    )
    delta = [deltas[0:1], deltas[1:2]]
    mass = [mass_ref[0, 0:1, :], mass_ref[0, 4:5, :]]
    dq_acc[...] = jnp.zeros_like(dq_acc)
    size = 256
    key_first = lane_masks((size, WIDE))
    key_none = jnp.zeros((size, WIDE), bf16)

    for kv_ref, dkv_ref in zip(kv_refs, dkv_refs):

        def chunk(i, carry, kv_ref=kv_ref, dkv_ref=dkv_ref):
            at = pl.ds(pl.multiple_of(i * size, size), size)
            k = kv_ref[0, at, :WIDE]
            v = kv_ref[0, at, WIDE:]
            dk = dv = dq = None
            for head in range(2):
                s = dot(k, qs[head], NT)
                p = jnp.exp2(s * scale - mass[head])
                dp = dot(v, gs[head], NT)
                ds = (p * (dp - delta[head])).astype(bf16)
                own_v = dot(p.astype(bf16), gs[head])
                own_k = dot(ds, qs[head])
                km = jnp.where(key_first, k, key_none) if head == 0 else jnp.where(key_first, key_none, k)
                own_q = dot(ds, km, TN)
                dv = own_v if dv is None else dv + own_v
                dk = own_k if dk is None else dk + own_k
                dq = own_q if dq is None else dq + own_q
            dkv_ref[0, at, :WIDE] = (dk * 0.125).astype(dkv_ref.dtype)
            dkv_ref[0, at, WIDE:] = dv.astype(dkv_ref.dtype)
            dq_acc[...] += dq
            return carry

        lax.fori_loop(0, kv_ref.shape[1] // size, chunk, 0, unroll=2)
    dq_ref[0] = (dq_acc[...] * 0.125).astype(bf16)


def attend_back(at, q, gs, o, mass, kvs, kinds):
    _, rows, _ = q.shape
    keys = sum(kv.shape[1] for kv in kvs)
    own = gs[0].shape[1]
    whole = lambda width: pl.BlockSpec((1, rows, width), lambda s: (0, 0, 0))
    kv_specs = [pl.BlockSpec((1, kv.shape[1], 2 * WIDE), lambda s: (0, 0, 0)) for kv in kvs]
    return pl.pallas_call(
        functools.partial(attend_back_kernel, len(kvs)),
        grid=(1,),
        in_specs=[whole(WIDE)]
        + [pl.BlockSpec((1, own, WIDE), lambda s: (at, 0, 0))] * PAIRS
        + [pl.BlockSpec((1, rows, WIDE), lambda s: (at, 0, 0)), pl.BlockSpec((1, 8, rows), lambda s: (at, 0, 0))]
        + kv_specs,
        out_specs=[whole(WIDE)] + kv_specs,
        out_shape=[jax.ShapeDtypeStruct((1, rows, WIDE), bf16)]
        + [jax.ShapeDtypeStruct(kv.shape, kind) for kv, kind in zip(kvs, kinds)],
        scratch_shapes=[pltpu.VMEM((rows, WIDE), f32)],
        compiler_params=room(14 + keys // 512),
        cost_estimate=cost(14),
        name="attend_back",
    )(q, *gs, o, mass, *kvs)


def full_spec(array):
    return pl.BlockSpec(array.shape, lambda *_: (0,) * array.ndim)


def pack_kernel(info_ref, *refs):
    parts, out_ref = refs[:-1], refs[-1]
    core = info_ref[0]
    half = out_ref.shape[0]

    @pl.when(core == 0)
    def _():
        out_ref[...] = jnp.concatenate([ref[:half] for ref in parts], axis=1)

    @pl.when(core != 0)
    def _():
        out_ref[...] = jnp.concatenate([ref[half:] for ref in parts], axis=1)


def pack(info, parts):
    rows, width = parts[0].shape
    shape = (rows // 2, len(parts) * width)
    return pl.pallas_call(
        pack_kernel,
        grid=(1,),
        in_specs=[pl.BlockSpec(memory_space=pltpu.SMEM)] + [full_spec(x) for x in parts],
        out_specs=pl.BlockSpec(shape, lambda i: (0, 0)),
        out_shape=jax.ShapeDtypeStruct(shape, bf16),
        compiler_params=room(6),
        cost_estimate=cost(1),
        name="pack",
    )(info, *parts)


def pack_feed_kernel(info_ref, inner_ref, outer_ref, wout_ref, bias_ref, *refs):
    vectors, out_ref = refs[:-1], refs[-1]
    core = info_ref[0]
    width = inner_ref.shape[0]
    cut = wout_ref.shape[0] // 2

    @pl.when(core == 0)
    def _():
        out_ref[:width] = inner_ref[...]
        out_ref[width : width + cut] = wout_ref[:cut]

    @pl.when(core != 0)
    def _():
        out_ref[:width] = outer_ref[...]
        out_ref[width : width + cut] = wout_ref[cut:]

    row = lax.broadcasted_iota(jnp.int32, (SMALL, WIDE), 0)
    table = jnp.zeros((SMALL, WIDE), f32)
    for i, ref in enumerate(vectors):
        table = jnp.where(row == i + 1, ref[...].astype(f32), table)
    row = lax.broadcasted_iota(jnp.int32, (SMALL, width), 0)
    table = jnp.concatenate([table, jnp.zeros((SMALL, width - WIDE), f32)], axis=1)
    table = jnp.where(row == 0, bias_ref[...].astype(f32), table)
    out_ref[width + cut :] = table.astype(bf16)


def pack_feed(info, w_inner, w_outer, w_out, b_inner, vectors):
    width = w_inner.shape[0]
    parts = [w_inner, w_outer, w_out, b_inner.reshape(1, -1)] + [v.reshape(1, -1) for v in vectors]
    shape = (width + w_out.shape[0] // 2 + SMALL, w_out.shape[1])
    return pl.pallas_call(
        pack_feed_kernel,
        grid=(1,),
        in_specs=[pl.BlockSpec(memory_space=pltpu.SMEM)] + [full_spec(x) for x in parts],
        out_specs=pl.BlockSpec(shape, lambda i: (0, 0)),
        out_shape=jax.ShapeDtypeStruct(shape, bf16),
        compiler_params=room(10),
        cost_estimate=cost(2),
        name="pack_feed",
    )(info, *parts)


def project_kernel(count, *refs):
    blocks, w_ref, q_ref, kv_ref = refs[:count], refs[count], refs[count + 1], refs[count + 2]
    at = 0
    for ref in blocks:
        rows = ref.shape[1]
        made = dot(ref[0], w_ref[...]).astype(bf16)
        q_ref[0, at : at + rows] = made[:, :WIDE]
        kv_ref[0, at : at + rows] = made[:, WIDE:]
        at += rows


def project(at, tokens, w_mine):
    total = sum(x.shape[1] for x in tokens)
    return pl.pallas_call(
        functools.partial(project_kernel, len(tokens)),
        grid=(1,),
        in_specs=[pl.BlockSpec((1,) + x.shape[1:], lambda i: (at, 0, 0)) for x in tokens]
        + [full_spec(w_mine)],
        out_specs=[
            pl.BlockSpec((1, total, WIDE), lambda i: (0, 0, 0)),
            pl.BlockSpec((1, total, 2 * WIDE), lambda i: (0, 0, 0)),
        ],
        out_shape=[
            jax.ShapeDtypeStruct((1, total, WIDE), bf16),
            jax.ShapeDtypeStruct((1, total, 2 * WIDE), bf16),
        ],
        compiler_params=room(10),
        cost_estimate=cost(1),
        name="project",
    )(*tokens, w_mine)


def combine_kernel(chosen, count, prior, final, info_ref, *refs):
    blocks, refs = refs[:count], refs[count:]
    backs, refs = refs[: 3 * len(chosen)], refs[3 * len(chosen) :]
    grad = None
    if prior:
        grad, refs = refs[0][...], refs[1:]
    outs, grad_refs = refs[:PAIRS], refs[PAIRS:]
    rows = outs[0].shape[1]
    for i, s in enumerate(chosen):
        dq_ref, kept_ref, got_ref = backs[3 * i : 3 * i + 3]
        at = 0
        for ref in blocks:
            size = ref.shape[1]
            part = slice(at, at + size)
            dkv = (kept_ref[0, part] + got_ref[0, part].astype(f32)).astype(bf16)
            piece = jnp.concatenate([dq_ref[0, part], dkv], axis=1)
            outs[at // rows][i, at % rows : at % rows + size] = piece
            term = dot(ref[s], piece, TN)
            grad = term if grad is None else grad + term
            at += size
    if not final:
        grad_refs[0][...] = grad
        return
    size = grad.shape[0] // (2 * PAIRS)

    def write(even_ref, odd_ref):
        for c in range(2 * PAIRS):
            ref = even_ref if c % 2 == 0 else odd_ref
            ref[jnp.bitwise_xor(c // 2, info_ref[2])] = grad[c * size : (c + 1) * size].astype(ref.dtype)

    @pl.when(info_ref[0] == 0)
    def _():
        write(grad_refs[0], grad_refs[1])

    @pl.when(info_ref[0] != 0)
    def _():
        write(grad_refs[1], grad_refs[0])


def combine(info, chosen, tokens, backs, prior, final):
    _, rows, width = tokens[0].shape
    flat = [x for back in backs for x in back]
    extra = [] if prior is None else [prior]
    if final:
        shape = (PAIRS, width // (2 * PAIRS), 3 * WIDE)
        grads = [jax.ShapeDtypeStruct(shape, f32), jax.ShapeDtypeStruct(shape, bf16)]
    else:
        grads = [jax.ShapeDtypeStruct((width, 3 * WIDE), f32)]
    pieces = [jax.ShapeDtypeStruct((len(chosen), rows, 3 * WIDE), bf16)] * PAIRS
    return pl.pallas_call(
        functools.partial(combine_kernel, chosen, len(tokens), len(extra), final),
        grid=(1,),
        in_specs=[pl.BlockSpec(memory_space=pltpu.SMEM)] + [full_spec(x) for x in tokens + flat + extra],
        out_specs=[full_spec(x) for x in pieces + grads],
        out_shape=pieces + grads,
        compiler_params=room(20),
        cost_estimate=cost(2),
        name="combine",
    )(info, *tokens, *flat, *extra)


def join_small_kernel(keep_ref, got_ref, *outs):
    for d, out in enumerate(outs):
        out[...] = (keep_ref[d] + got_ref[d].astype(f32)).astype(bf16)


def join_small(keep, got):
    return pl.pallas_call(
        join_small_kernel,
        grid=(1,),
        in_specs=[full_spec(keep), full_spec(got)],
        out_specs=[pl.BlockSpec(keep.shape[1:], lambda i: (0, 0))] * PAIRS,
        out_shape=[jax.ShapeDtypeStruct(keep.shape[1:], bf16)] * PAIRS,
        compiler_params=room(6),
        cost_estimate=cost(1),
        name="join_small",
    )(keep, got)


def pack_heads(total):
    kept = total.shape[0] * 3 // 4
    rest = [total[kept:, i * WIDE : (i + 1) * WIDE] for i in range(3)]
    return jnp.concatenate([total[:kept], jnp.concatenate(rest, axis=0)], axis=1)


def share_small_kernel(info_ref, feed_ref, *refs):
    parts, outs = refs[:PAIRS], refs[PAIRS:]
    for step, out in enumerate(outs):
        at = jnp.bitwise_xor(jnp.bitwise_xor(info_ref[1], info_ref[2]), step)
        value = parts[0][...]
        for d in range(1, PAIRS):
            value = jnp.where(at == d, parts[d][...], value)
        value = pack_heads(value)
        if step == 2:
            rows = feed_ref.shape[0]
            out[:rows] = feed_ref[...]
            out[rows:] = value
        else:
            out[...] = value


def share_small(info, feed, parts):
    small = (parts[0].shape[0] * 3 // 4, feed.shape[1])
    large = (small[0] + feed.shape[0], feed.shape[1])
    shapes = [small, small, large, small]
    return pl.pallas_call(
        share_small_kernel,
        grid=(1,),
        in_specs=[pl.BlockSpec(memory_space=pltpu.SMEM)] + [full_spec(x) for x in [feed] + parts],
        out_specs=[pl.BlockSpec(shape, lambda i: (0, 0)) for shape in shapes],
        out_shape=[jax.ShapeDtypeStruct(shape, bf16) for shape in shapes],
        compiler_params=room(6),
        cost_estimate=cost(1),
        name="share_small",
    )(info, feed, *parts)


def state_kernel(base_ref, *refs):
    blocks, weights, out_ref = refs[:PAIRS], refs[PAIRS : 2 * PAIRS], refs[2 * PAIRS]
    total = base_ref[0]
    for ref, w_ref in zip(blocks, weights):
        total = total + dot(ref[0], w_ref[...], NT)
    out_ref[0] = total


def add_state(at, base, blocks, weights):
    rows, width = base.shape[1:]
    count = blocks[0].shape[0]
    spec = pl.BlockSpec((1, rows, width), lambda i: (at + i, 0, 0))
    return pl.pallas_call(
        state_kernel,
        grid=(count,),
        in_specs=[spec]
        + [pl.BlockSpec((1,) + b.shape[1:], lambda i: (i, 0, 0)) for b in blocks]
        + [full_spec(w) for w in weights],
        out_specs=spec,
        out_shape=jax.ShapeDtypeStruct(base.shape, base.dtype),
        input_output_aliases={0: 0},
        compiler_params=room(10),
        cost_estimate=cost(2.5 * count),
        name="add_state",
    )(base, *blocks, *weights)


def choose_kernel(info_ref, near_ref, far_ref, out_ref):
    close = jnp.bitwise_xor(info_ref[1], info_ref[2]) < 2
    out_ref[...] = jnp.where(close, near_ref[...], far_ref[...])


def choose(info, near, far):
    return pl.pallas_call(
        choose_kernel,
        grid=(1,),
        in_specs=[pl.BlockSpec(memory_space=pltpu.SMEM), full_spec(near), full_spec(far)],
        out_specs=full_spec(near),
        out_shape=jax.ShapeDtypeStruct(near.shape, bf16),
        compiler_params=room(6),
        cost_estimate=cost(1),
        name="choose",
    )(info, near, far)


def assemble_kernel(info_ref, mine_ref, other_ref, out_ref):
    half = mine_ref.shape[0]
    out_ref[:half] = jnp.where(info_ref[0] == 0, mine_ref[...], other_ref[...])
    out_ref[half:] = jnp.where(info_ref[0] == 0, other_ref[...], mine_ref[...])


def assemble(info, mine, other):
    shape = (2 * mine.shape[0], mine.shape[1])
    return pl.pallas_call(
        assemble_kernel,
        grid=(1,),
        in_specs=[pl.BlockSpec(memory_space=pltpu.SMEM), full_spec(mine), full_spec(other)],
        out_specs=pl.BlockSpec(shape, lambda i: (0, 0)),
        out_shape=jax.ShapeDtypeStruct(shape, bf16),
        compiler_params=room(6),
        cost_estimate=cost(1),
        name="assemble",
    )(info, mine, other)


def keep_scalar(block):
    tail = block[-8:]
    total = tail[:, :WIDE] + tail[:, WIDE : 2 * WIDE]
    high = total.astype(bf16).astype(f32)
    split = jnp.concatenate([high, total - high, tail[:, 2 * WIDE :]], axis=1)
    row = lax.broadcasted_iota(jnp.int32, tail.shape, 0)
    tail = jnp.where(row == 6, split, tail)
    return tail if block.shape[0] == 8 else jnp.concatenate([block[:-8], tail], axis=0)


def flat_rows(ref):
    return ref[...].reshape(-1, ref.shape[-1])


def write_pieces(info_ref, even_ref, odd_ref, grads, small):
    pieces = 2 * PAIRS * even_ref.shape[1]

    def write(keep_ref, give_ref):
        for c in range(pieces):
            ref = keep_ref if c % 2 == 0 else give_ref
            order = jnp.bitwise_xor((c // 2) % PAIRS, info_ref[2])
            repeat = c // (2 * PAIRS)
            at = 0
            for grad in grads:
                size = grad.shape[0] // pieces
                ref[order, repeat, 0, at : at + size] = grad[c * size : (c + 1) * size]
                at += size
            if small is not None:
                ref[order, repeat, 0, at : at + 8] = small if c == 0 else jnp.zeros_like(small)

    @pl.when(info_ref[0] == 0)
    def _():
        write(even_ref, odd_ref)

    @pl.when(info_ref[0] != 0)
    def _():
        write(odd_ref, even_ref)


def outer_grad_kernel(
    info_ref, a0_ref, a1_ref, a2_ref, a3_ref, ilow_ref, gfeed_ref, gbranch_ref, even_ref, odd_ref
):
    g_outer = dot(flat_rows(ilow_ref), flat_rows(gfeed_ref), TN).astype(bf16)
    order = jnp.bitwise_xor(pl.program_id(0), info_ref[2])
    low, high = order % 2 == 0, order < 2
    att = jnp.where(
        high,
        jnp.where(low, flat_rows(a0_ref), flat_rows(a1_ref)),
        jnp.where(low, flat_rows(a2_ref), flat_rows(a3_ref)),
    )
    g_out = dot(att, flat_rows(gbranch_ref), TN).astype(bf16)
    write_pieces(info_ref, even_ref, odd_ref, (g_outer, g_out), None)


def inner_grad_kernel(info_ref, nlow_ref, gin_ref, vsum_ref, bsum_ref, even_ref, odd_ref):
    g_in = dot(flat_rows(nlow_ref), flat_rows(gin_ref), TN).astype(bf16)
    vectors = sum(vsum_ref[s] for s in range(vsum_ref.shape[0]))
    bias = sum(bsum_ref[s] for s in range(bsum_ref.shape[0]))
    width = g_in.shape[1]
    low = jnp.concatenate([vectors, jnp.zeros((8, width - WIDE), f32)], axis=1)
    row = lax.broadcasted_iota(jnp.int32, (8, width), 0)
    small = keep_scalar(jnp.where(row == 7, bias, low)).astype(bf16)
    write_pieces(info_ref, even_ref, odd_ref, (g_in,), small)


def split_grads(kernel, name, info, arrays, specs, piece, width, ctx):
    shape = (PAIRS, ctx // (2 * PAIRS), PAIRS, piece, width)
    out_spec = pl.BlockSpec(shape[:2] + (1, piece, width), lambda z, info: (0, 0, z, 0, 0))
    return pl.pallas_call(
        kernel,
        grid_spec=pltpu.PrefetchScalarGridSpec(
            num_scalar_prefetch=1, grid=(PAIRS,), in_specs=specs, out_specs=[out_spec, out_spec]
        ),
        out_shape=[jax.ShapeDtypeStruct(shape, bf16)] * 2,
        compiler_params=room(24),
        cost_estimate=cost(1),
        name=name,
    )(info, *arrays)


def hidden_spec(array):
    seqs, rows, hidden = array.shape
    return pl.BlockSpec(
        (seqs, rows, hidden // PAIRS), lambda z, info: (0, 0, lax.rem(z - info[1] + PAIRS, PAIRS))
    )


def outer_grads(info, att, ilow, gfeed, gbranch, ctx):
    width = gfeed.shape[2]
    piece = (ilow.shape[2] // PAIRS + width // PAIRS) // ctx
    arrays = [*att, ilow, gfeed, gbranch]
    specs = [full_spec(x) for x in arrays]
    specs[PAIRS] = hidden_spec(ilow)
    return split_grads(outer_grad_kernel, "outer_grads", info, arrays, specs, piece, width, ctx)


def inner_grads(info, nlow, gin, vsum, bsum, ctx):
    width = nlow.shape[2]
    seqs = vsum.shape[0]
    specs = [
        full_spec(nlow),
        hidden_spec(gin),
        pl.BlockSpec((seqs, 8, WIDE), lambda z, info: (0, 0, z)),
        hidden_spec(bsum),
    ]
    piece = width // ctx + 8
    return split_grads(
        inner_grad_kernel, "inner_grads", info, [nlow, gin, vsum, bsum], specs, piece, gin.shape[2] // PAIRS, ctx
    )


def join_kernel(scalar, keep_ref, got_ref, *outs):
    for d, out in enumerate(outs):
        for r in range(out.shape[0]):
            total = keep_ref[d, r, 0].astype(f32) + got_ref[d, r, 0].astype(f32)
            out[r, 0] = (keep_scalar(total) if scalar else total).astype(bf16)


def join(keep, got, scalar):
    _, repeats, wsh, piece, width = keep.shape
    spec = pl.BlockSpec((PAIRS, repeats, 1, piece, width), lambda z: (0, 0, z, 0, 0))
    return pl.pallas_call(
        functools.partial(join_kernel, scalar),
        grid=(wsh,),
        in_specs=[spec, spec],
        out_specs=[pl.BlockSpec((repeats, 1, piece, width), lambda z: (0, z, 0, 0))] * PAIRS,
        out_shape=[jax.ShapeDtypeStruct(keep.shape[1:], bf16)] * PAIRS,
        compiler_params=room(16),
        cost_estimate=cost(1.5),
        name="join",
    )(keep, got)


def share_kernel(info_ref, *refs):
    firsts, seconds, outs = refs[:PAIRS], refs[PAIRS : 2 * PAIRS], refs[2 * PAIRS :]
    for step in range(PAIRS):
        place = jnp.bitwise_xor(info_ref[1], step)
        out = outs[step % 2]
        for r in range(out.shape[0]):
            totals = []
            for parts in (firsts, seconds):
                total = parts[0][r, place].astype(f32)
                for part in parts[1:]:
                    total = total + part[r, place].astype(f32)
                totals.append(total)
            size = totals[0].shape[0]
            out[r, step // 2, :size] = totals[0].astype(bf16)
            out[r, step // 2, size:] = keep_scalar(totals[1]).astype(bf16)


def share_parts(info, firsts, seconds):
    repeats, wsh, piece, width = firsts[0].shape
    shape = (repeats, wsh // 2, piece + seconds[0].shape[2], width)
    return pl.pallas_call(
        share_kernel,
        grid=(1,),
        in_specs=[pl.BlockSpec(memory_space=pltpu.SMEM)] + [full_spec(x) for x in firsts + seconds],
        out_specs=[pl.BlockSpec(shape, lambda i: (0, 0, 0, 0))] * 2,
        out_shape=[jax.ShapeDtypeStruct(shape, bf16)] * 2,
        compiler_params=room(16),
        cost_estimate=cost(1.5),
        name="share",
    )(info, *firsts, *seconds)


def halve_kernel(keep_ref, got_ref, own_ref, send_ref):
    for at, out in enumerate((own_ref, send_ref)):
        out[...] = keep_scalar(keep_ref[at].astype(f32) + got_ref[at].astype(f32)).astype(bf16)


def halve(keep, got):
    shape = keep.shape[1:]
    return pl.pallas_call(
        halve_kernel,
        grid=(1,),
        in_specs=[full_spec(keep), full_spec(got)],
        out_specs=[pl.BlockSpec(shape, lambda i: (0, 0))] * 2,
        out_shape=[jax.ShapeDtypeStruct(shape, bf16)] * 2,
        compiler_params=room(6),
        cost_estimate=cost(1),
        name="halve",
    )(keep, got)


def total_kernel(own_ref, *refs):
    parts, out = refs[:-1], refs[-1]
    rows = own_ref.shape[0]
    if len(parts) == 1:
        out[...] = keep_scalar(own_ref[...].astype(f32) + parts[0][...].astype(f32)).astype(bf16)
        return
    out[:rows] = keep_scalar(own_ref[...].astype(f32) + parts[2][:rows].astype(f32)).astype(bf16)
    total = parts[2][rows:].astype(f32)
    for i in (0, 1, 3):
        total = total + parts[i][...].astype(f32)
    out[rows:] = total.astype(bf16)


def total_parts(own, parts):
    shape = max((x.shape for x in parts), key=lambda x: x[0])
    return pl.pallas_call(
        total_kernel,
        grid=(1,),
        in_specs=[full_spec(x) for x in [own] + parts],
        out_specs=pl.BlockSpec(shape, lambda i: (0, 0)),
        out_shape=jax.ShapeDtypeStruct(shape, bf16),
        compiler_params=room(6),
        cost_estimate=cost(1),
        name="total",
    )(own, *parts)


def unpack_kernel(info_ref, *refs):
    pieces = refs[: 2 * PAIRS]
    outer_ref, out_ref, in_ref, tail_ref, *heads = refs[2 * PAIRS :]
    core, pair = info_ref[0], info_ref[2]
    for side in range(2):
        for d in range(PAIRS):
            ref = pieces[side * PAIRS + d]
            place = jnp.bitwise_xor(pair, d) * 2 + jnp.bitwise_xor(core, side)
            at = 0
            for target in (outer_ref, out_ref, in_ref):
                size = target.shape[0] // (2 * PAIRS)
                start = pl.multiple_of(place * size, size)
                target[pl.ds(start, size)] = ref[at : at + size].astype(f32)
                at += size

            @pl.when(place == 0)
            def _(ref=ref, at=at):
                tail_ref[...] = ref[at : at + 8].astype(f32)

            at += 8
            size = heads[0].shape[0] // (2 * PAIRS)
            kept = size * 3 // 4
            for i, target in enumerate(heads):
                start = pl.multiple_of(place * size, size)
                target[pl.ds(start, kept)] = ref[at : at + kept, i * WIDE : (i + 1) * WIDE].astype(f32)
                more = (size - kept) * i + at
                target[pl.ds(start + kept, size - kept)] = ref[more : more + size - kept, 3 * WIDE :].astype(f32)


def unpack(info, mine, other, part, out_rows):
    width = mine[0].shape[1]
    shapes = [(part, width), (out_rows, width), (width, part), (8, width)] + [(width, WIDE)] * 3
    return pl.pallas_call(
        unpack_kernel,
        grid=(1,),
        in_specs=[pl.BlockSpec(memory_space=pltpu.SMEM)] + [full_spec(x) for x in mine + other],
        out_specs=[pl.BlockSpec(shape, lambda i: (0, 0)) for shape in shapes],
        out_shape=[jax.ShapeDtypeStruct(shape, f32) for shape in shapes],
        compiler_params=room(16),
        cost_estimate=cost(3),
        name="unpack",
    )(info, *mine, *other)


def gelu_parts(x):
    half = 0.5 * (1.0 + lax.erf(x * 2.0 ** (-0.5)))
    density = jnp.exp(-0.5 * x * x) * (2.0 * math.pi) ** (-0.5)
    return x * half, half + x * density


def mean_rows(x):
    return jnp.sum(x, axis=1, keepdims=True) * (1.0 / x.shape[1])


def norm_rows(z, gain, shift):
    centre = z - mean_rows(z)
    inverse = lax.rsqrt(mean_rows(centre * centre) + epsilon)
    normed = centre * inverse
    return normed * gain + shift, normed, inverse


def norm_back(g, normed, inverse, gain):
    scaled = g * gain
    return inverse * (scaled - mean_rows(scaled) - normed * mean_rows(scaled * normed))


def dense_kernel(info_ref, bhalt_ref, *refs):
    mine, other, refs = refs[:PAIRS], refs[PAIRS : 2 * PAIRS], refs[2 * PAIRS :]
    att_refs, refs = refs[:PAIRS], refs[PAIRS:]
    emb_ref, prev_ref, gt_ref, gb_ref, hsum_ref, code_ref, gsum_ref = refs[:7]
    refs = refs[7:]
    final_ref, blend_ref, nsum_ref, ghalt_ref, gprev_ref, base_ref = refs[:6]
    gatt_refs = refs[6:10]
    nlow_ref, ilow_ref, gin_ref, gfeed_ref, gbranch_ref, vsum_ref, bsum_ref = refs[10:17]
    slope_ref, win_ref, wouter_ref, wout_ref, small_ref, sem = refs[17:23]
    buffers, row_sem = refs[23:27], refs[27]
    me = pl.program_id(0)

    def fetch(step):
        slot = lax.rem(step, 2)
        return [
            pltpu.make_async_copy(source.at[step], buffer.at[slot], row_sem.at[i, slot])
            for i, (source, buffer) in enumerate(zip((emb_ref, prev_ref, gt_ref, gb_ref), buffers))
        ]

    @pl.when(me == 0)
    def _():
        for one in fetch(0):
            one.start()

    @pl.when(me + 1 < pl.num_programs(0))
    def _():
        for one in fetch(me + 1):
            one.start()

    blocks, columns, width = win_ref.shape
    cut = wout_ref.shape[1] // 2
    core, zed, pair = info_ref[0], info_ref[1], info_ref[2]

    def load(firsts, seconds):
        copies = []

        def copy(source, start, size, target):
            copies.append(pltpu.make_async_copy(source.at[pl.ds(start, size)], target, sem.at[len(copies)]))

        for a in range(PAIRS):
            place = lax.rem(zed + a, PAIRS)
            order = jnp.bitwise_xor(place, pair)
            first, second = firsts[(-a) % PAIRS], seconds[a]
            copy(first, columns, cut, wout_ref.at[order, pl.ds(0, cut)])
            copy(second, width, cut, wout_ref.at[order, pl.ds(cut, cut)])
            copy(first, columns + cut, SMALL, small_ref.at[place])
            copy(first, 0, columns, win_ref.at[a])
            copy(second, 0, width, wouter_ref.at[a])
        for one in copies:
            one.start()
        for one in copies:
            one.wait()

    @pl.when((pl.program_id(0) == 0) & (core == 0))
    def _():
        load(mine, other)

    @pl.when((pl.program_id(0) == 0) & (core != 0))
    def _():
        load(other, mine)

    for one in fetch(me):
        one.wait()
    emb, prev, gt, gb = [buffer[lax.rem(me, 2)] for buffer in buffers]
    att = jnp.concatenate([ref[0] for ref in att_refs], axis=1)
    w_out = wout_ref[...].reshape(emb.shape[1], emb.shape[1])
    b_outer, g1, s1, g2, s2, halt = [
        jnp.concatenate([small_ref[a, i + 1 : i + 2, :WIDE] for a in range(PAIRS)], axis=1).astype(f32)
        for i in range(6)
    ]
    at_row = pl.ds(pl.program_id(0), 1)
    row = lax.broadcasted_iota(jnp.int32, (8, emb.shape[0]), 0)
    lines = jnp.where(row == 0, hsum_ref[at_row], jnp.where(row == 1, code_ref[at_row].astype(f32), gsum_ref[at_row]))
    cols = jnp.transpose(lines)
    sum_col, code_col, gsum_col = cols[:, 0:1], cols[:, 1:2], cols[:, 2:3]
    z1 = emb + dot(att, w_out)
    one, n1, i1 = norm_rows(z1, g1, s1)
    nlow = one.astype(bf16)
    nlow_ref[0] = nlow
    feed = None
    for j in range(blocks):
        pre = dot(nlow, win_ref[j]) + small_ref[lax.rem(zed + j, PAIRS), 0:1, :].astype(f32)
        act, slope = gelu_parts(pre)
        act = act.astype(bf16)
        ilow_ref[0, :, j * width : (j + 1) * width] = act
        slope_ref[:, j * width : (j + 1) * width] = slope
        part = dot(act, wouter_ref[j])
        feed = part if feed is None else feed + part
    z2 = one + (feed + b_outer)
    final, n2, i2 = norm_rows(z2, g2, s2)
    halt_logit = jnp.sum(emb * halt, axis=1, keepdims=True) + bhalt_ref[0, 0]
    halt_prob = jax.nn.sigmoid(halt_logit)
    running = (code_col > 0.5).astype(f32)
    halting = (code_col > 1.5).astype(f32)
    update = running * (halting * (1.0 - sum_col) + (1.0 - halting) * halt_prob)
    prev = prev.astype(f32)
    gb = gb.astype(f32)
    final_ref[0] = final.astype(bf16)
    blend_ref[0] = (prev * (1.0 - update) + final * update).astype(bf16)
    gprev_ref[0] = gb * (1.0 - update)
    g_update = jnp.sum(gb * (final - prev), axis=1, keepdims=True) + gsum_col
    g_halt_sum = gsum_col - running * halting * g_update
    g_logit = g_update * running * (1.0 - halting) * halt_prob * (1.0 - halt_prob)
    lane = lax.broadcasted_iota(jnp.int32, (emb.shape[0], WIDE), 1)
    packed = jnp.where(lane == 0, sum_col + update, jnp.where(lane == 1, g_halt_sum, 0.0))
    turned = jnp.transpose(packed)
    nsum_ref[at_row] = turned[0:1]
    ghalt_ref[at_row] = turned[1:2]
    gf = gt.astype(f32) + update * gb
    g_two = norm_back(gf, n2, i2, g2)
    gfeed = g_two.astype(bf16)
    gfeed_ref[0] = gfeed
    g_one = g_two
    for j in range(blocks):
        at = slice(j * width, (j + 1) * width)
        back = dot(gfeed, wouter_ref[j], NT)
        gin_f = back * slope_ref[:, at]
        gin = gin_f.astype(bf16)
        gin_ref[0, :, at] = gin
        bsum_ref[0, :, at] = jnp.sum(gin.astype(f32), axis=0, keepdims=True)
        g_one = g_one + dot(gin, win_ref[j], NT)
    g_emb = norm_back(g_one, n1, i1, g1)
    gbranch = g_emb.astype(bf16)
    gbranch_ref[0] = gbranch
    gatt = dot(gbranch, w_out, NT).astype(bf16)
    for d, ref in enumerate(gatt_refs):
        ref[0] = gatt[:, d * WIDE : (d + 1) * WIDE]
    base_ref[0] = g_emb + g_logit * halt
    total = lambda x: jnp.sum(x, axis=0, keepdims=True)
    logit_sum = jnp.broadcast_to(total(g_logit), (1, emb.shape[1]))
    vsum_ref[0] = jnp.concatenate(
        [
            total(gfeed.astype(f32)),
            total(g_one * n1),
            total(g_one),
            total(gf * n2),
            total(gf),
            total(g_logit * emb),
            logit_sum,
            jnp.zeros((1, emb.shape[1]), f32),
        ],
        axis=0,
    )


def dense(info, b_halt, mine, other, emb, att, prev, gt, gb, marks, part, out_rows):
    seqs, rows, width = emb.shape
    hidden = PAIRS * part
    outside = pl.BlockSpec(memory_space=pltpu.HBM)
    scalars = pl.BlockSpec(memory_space=pltpu.SMEM)
    rowspec = lambda w: pl.BlockSpec((1, rows, w), lambda s: (s, 0, 0))
    shape = lambda w, kind: jax.ShapeDtypeStruct((seqs, rows, w), kind)
    return pl.pallas_call(
        dense_kernel,
        grid=(seqs,),
        in_specs=[scalars, scalars]
        + [outside] * (2 * PAIRS)
        + [rowspec(WIDE)] * PAIRS
        + [outside] * 4
        + [full_spec(x) for x in marks],
        out_specs=[
            rowspec(width),
            rowspec(width),
            pl.BlockSpec((seqs, rows), lambda s: (0, 0)),
            pl.BlockSpec((seqs, rows), lambda s: (0, 0)),
            rowspec(width),
            rowspec(width),
            rowspec(WIDE),
            rowspec(WIDE),
            rowspec(WIDE),
            rowspec(WIDE),
            rowspec(width),
            rowspec(hidden),
            rowspec(hidden),
            rowspec(width),
            rowspec(width),
            pl.BlockSpec((1, 8, width), lambda s: (s, 0, 0)),
            pl.BlockSpec((1, 1, hidden), lambda s: (s, 0, 0)),
        ],
        out_shape=[
            shape(width, bf16),
            shape(width, bf16),
            jax.ShapeDtypeStruct((seqs, rows), f32),
            jax.ShapeDtypeStruct((seqs, rows), f32),
            shape(width, f32),
            shape(width, f32),
            shape(WIDE, bf16),
            shape(WIDE, bf16),
            shape(WIDE, bf16),
            shape(WIDE, bf16),
            shape(width, bf16),
            shape(hidden, bf16),
            shape(hidden, bf16),
            shape(width, bf16),
            shape(width, bf16),
            jax.ShapeDtypeStruct((seqs, 8, width), f32),
            jax.ShapeDtypeStruct((seqs, 1, hidden), f32),
        ],
        scratch_shapes=[
            pltpu.VMEM((rows, hidden), f32),
            pltpu.VMEM((PAIRS, width, part), bf16),
            pltpu.VMEM((PAIRS, part, width), bf16),
            pltpu.VMEM((PAIRS, out_rows, width), bf16),
            pltpu.VMEM((PAIRS, SMALL, width), bf16),
            pltpu.SemaphoreType.DMA((5 * PAIRS,)),
            pltpu.VMEM((2, rows, width), f32),
            pltpu.VMEM((2, rows, width), bf16),
            pltpu.VMEM((2, rows, width), bf16),
            pltpu.VMEM((2, rows, width), bf16),
            pltpu.SemaphoreType.DMA((4, 2)),
        ],
        compiler_params=room(36),
        cost_estimate=cost(20),
        name="dense",
    )(info, b_halt, *mine, *other, *att, emb, prev, gt, gb, *marks)


def frequencies(half):
    return jnp.exp(-math.log(10000.0) * jnp.arange(half, dtype=f32) / (half - 1))


def position_rows(first, rows, columns):
    half = columns // 2
    freq = frequencies(half)[None, :]
    coarse = (first + 16 * jnp.arange(rows // 16, dtype=jnp.int32)).astype(f32)[:, None] * freq
    fine = jnp.arange(16, dtype=f32)[:, None] * freq
    sa, ca = jnp.sin(coarse)[:, None], jnp.cos(coarse)[:, None]
    sb, cb = jnp.sin(fine)[None], jnp.cos(fine)[None]
    both = jnp.concatenate([sa * cb + ca * sb, ca * cb - sa * sb], axis=2)
    return both.reshape(rows, columns)


def step_rows(columns):
    half = columns // 2
    angles = jnp.arange(4, dtype=f32)[:, None] * frequencies(half)[None, :]
    return jnp.concatenate([jnp.sin(angles), jnp.cos(angles)], axis=1)


def body(
    hidden_state,
    prev_state,
    halt_sum,
    halt_code,
    step_count,
    w_query,
    w_key,
    w_value,
    w_out,
    w_inner,
    b_inner,
    w_outer,
    b_outer,
    gain_attention,
    shift_attention,
    gain_feedforward,
    shift_feedforward,
    w_halt,
    b_halt,
    grad_transformed,
    grad_blended,
    grad_sum,
):
    seqs, rows, width = hidden_state.shape
    ctx = lax.axis_size("ctx")
    wsh = lax.axis_size("wsh")
    repeats = ctx // (2 * PAIRS)
    me = lax.axis_index("ctx")
    zed = lax.axis_index("wsh")
    core = me % 2
    pair = (me // 2) % PAIRS

    def swap(x, distance):
        return lax.ppermute(x, "ctx", [(i, i ^ distance) for i in range(ctx)])

    def sibling(x):
        return swap(x, 1)

    def partners(x, distance):
        return swap(x, 2 * distance)

    freq_rows = position_rows(me * rows, rows, width)
    table = step_rows(width)
    steps = step_count[:, :, None]
    step_signal = jnp.where(
        steps == 0, table[0], jnp.where(steps == 1, table[1], jnp.where(steps == 2, table[2], table[3]))
    )
    emb = hidden_state.astype(f32) + freq_rows[None] + step_signal
    emb_low = emb.astype(bf16)

    after = lambda x, *others: lax.optimization_barrier((x,) + others)[0]

    info = jnp.stack([core, zed, pair]).astype(jnp.int32)
    ring = [
        (c * wsh + z, c * wsh + (z + (1 if c % 2 == 0 else -1)) % wsh) for c in range(ctx) for z in range(wsh)
    ]
    turn = lambda x: lax.ppermute(x, ("ctx", "wsh"), ring)
    out_rows = w_out.shape[0]
    part = w_inner.shape[1]
    half = rows // 2

    tokens = [emb_low] + [partners(emb_low, d) for d in (1, 2)]
    pair_of = lambda c: (c // 2) % PAIRS
    held = pack(info, [w_query, w_key, w_value])
    hop = lambda x, starts, step: lax.ppermute(
        x,
        ("ctx", "wsh"),
        [(c * wsh + (pair_of(c) ^ z), c * wsh + (pair_of(c) ^ z ^ step)) for c in range(ctx) for z in starts],
    )
    near = jnp.where(zed == pair, held, hop(held, (0,), 1))
    far = hop(near, (0, 1), 2)
    tokens.append(partners(tokens[2][:, :half], 1))
    tokens.append(partners(tokens[1][:, half:], 2))
    vectors = [b_outer, gain_attention, shift_attention, gain_feedforward, shift_feedforward, w_halt]
    feed = pack_feed(after(info, held), w_inner, w_outer, w_out, b_inner, vectors)
    feed_mine = [feed, turn(feed)]
    feed_first = sibling(feed)
    chosen = choose(after(info, feed_mine[1], feed_first, *tokens[1:3]), near, far)
    w_mine = assemble(info, chosen, sibling(chosen))

    groups = [[r * 2 * PAIRS + i for r in range(repeats)] for i in range(2 * PAIRS)]
    q_list, kvs_list, fold = [], [], None
    w_now = w_mine
    own_list = []
    for s in range(seqs):
        q, own = project(s, tokens, w_now)
        w_now = after(w_mine, q)
        q_list.append(q)
        own_list.append(own)

    def keys_values(own):
        other = sibling(own)
        if repeats == 1:
            return [own, other]
        both = jnp.concatenate([own, other], axis=1)
        return [lax.all_gather(both, "ctx", axis=1, tiled=True, axis_index_groups=groups)]

    feed_mine.append(turn(feed_mine[1]))
    kvs_list = [keys_values(own) for own in own_list]
    fold = attend(0, seqs, q_list[0], kvs_list[0], None)
    feed_mine.append(turn(after(feed_mine[2], fold[1])))
    fold = attend(1, seqs, after(q_list[1], feed_mine[2], kvs_list[2][-1]), kvs_list[1], fold)
    feed_other = [feed_first, sibling(after(feed_mine[1], fold[1]))]
    fold = attend(2, seqs, after(q_list[2], *feed_other), kvs_list[2], fold)
    o32, mass, *low = fold
    att = [low[0]] + [partners(low[d], d) for d in range(1, PAIRS)]
    feed_other.append(sibling(after(feed_mine[2], mass)))
    feed_other.append(sibling(after(feed_mine[3], *att[1:])))
    w_order = [w_mine] + [partners(after(w_mine, *att[1:]), d) for d in range(1, PAIRS)]

    (
        final,
        blended,
        new_sum,
        grad_halt_sum,
        grad_prev,
        base,
        gatt0,
        gatt1,
        gatt2,
        gatt3,
        nlow,
        ilow,
        gin,
        gfeed,
        gbranch,
        vsum,
        bsum,
    ) = dense(
        info, b_halt.reshape(1, 1), feed_mine, feed_other, emb, att, prev_state, grad_transformed, grad_blended,
        [halt_sum, halt_code, grad_sum], part, out_rows,
    )
    gs = [gatt0] + [partners(x, d + 1) for d, x in enumerate((gatt1, gatt2, gatt3))]

    keep_a, give_a = outer_grads(after(info, vsum, *w_order[1:]), att, ilow, gfeed, gbranch, ctx)
    keep_b, give_b = inner_grads(after(info, keep_a), nlow, gin, vsum, bsum, ctx)
    joined_a = join(after(keep_a, keep_b), sibling(give_a), False)

    def spread_pieces(pieces):
        return [pieces[0]] + [partners(pieces[d], d) for d in range(1, PAIRS)]

    shared_a = spread_pieces(joined_a)

    kinds = [f32, bf16] if repeats == 1 else [bf16]

    def split_back(s, token):
        dq, *dkv = attend_back(s, q_list[s], gs, o32, token, kvs_list[s], kinds)
        if repeats == 1:
            kept, sent = dkv
        else:
            summed = lax.psum_scatter(
                dkv[0], "ctx", scatter_dimension=1, tiled=True, axis_index_groups=groups
            )
            kept, sent = summed[:, : PAIRS * rows].astype(f32), summed[:, PAIRS * rows :]
        return dq, kept, sent

    backs = [split_back(0, after(mass, *joined_a))]
    joined_b = join(after(keep_b, backs[0][0], *shared_a), sibling(give_b), True)
    shared_b = spread_pieces(joined_b)
    backs.append(split_back(1, after(mass, *joined_b)))
    got = lambda back, *others: back[:2] + (sibling(after(back[2], *others)),)
    share_keep, share_send = share_parts(after(info, backs[1][0]), shared_a, shared_b)
    if repeats > 1:
        share_keep, share_send = (
            lax.psum_scatter(x, "ctx", scatter_dimension=0, tiled=True, axis_index_groups=groups)
            for x in (share_keep, share_send)
        )
    cross = lambda x, step: lax.ppermute(x, "wsh", [(z, z ^ step) for z in range(wsh)])
    moved = cross(share_send[0], 1)
    *pieces, gq = combine(
        after(info, share_keep), (0, 1), tokens, [got(backs[0]), got(backs[1], share_keep)], None, False
    )
    blocks = spread_pieces(pieces)
    backs.append(split_back(2, after(mass, gq)))
    own, sent = halve(after(share_keep[0], backs[2][0], *blocks[1:]), moved)
    made = combine(info, (2,), tokens, [got(backs[2], own)], gq, repeats == 1)
    pieces, keep, give = made[:PAIRS], made[PAIRS], made[-1]
    if repeats == 1:
        small = join_small(keep, sibling(give))
        block = [pieces[0]] + [partners(after(pieces[d], small[0]), d) for d in (1, 2)]
        heads = share_small(info, sent, spread_pieces(small))
        heads = [heads[0]] + [cross(heads[step], step) for step in range(1, wsh)]
        grad_state = add_state(0, after(base, heads[0]), blocks, w_order)
        share = total_parts(after(own, grad_state, *block[1:]), heads)
        block.append(partners(after(pieces[3], grad_state), 3))
        grad_state = add_state(2, after(grad_state, share), block, w_order)
        mine = spread_pieces([share] * PAIRS)
        (grad_w_outer, grad_w_out, grad_w_inner, tail, grad_w_query, grad_w_key, grad_w_value) = unpack(
            info, mine, [sibling(after(x, grad_state)) for x in mine], part, out_rows
        )
    else:
        block = spread_pieces(pieces)
        share = total_parts(own, [cross(sent, 2)])
        grad_state = add_state(2, add_state(0, base, blocks, w_order), block, w_order)
        whole = lax.all_gather(share, "ctx", axis=0).astype(f32)
        a, b, c = part // ctx, out_rows // ctx, width // ctx
        grad_w_outer = whole[:, :a].reshape(part, width)
        grad_w_out = whole[:, a : a + b].reshape(out_rows, width)
        grad_w_inner = whole[:, a + b : a + b + c].reshape(width, part)
        tail = whole[0, a + b + c :]
        own = lax.dynamic_update_index_in_dim(jnp.zeros((wsh,) + keep.shape, f32), keep, pair, 0)
        own = lax.psum(lax.psum_scatter(own.astype(bf16), "wsh", scatter_dimension=0).astype(f32), "ctx")
        grad_w_query, grad_w_key, grad_w_value = (own[:, i * WIDE : (i + 1) * WIDE] for i in range(3))
    grad_b_inner = tail[7]
    vec_grads = [tail[i, :out_rows] for i in range(6)]
    grad_b_halt = tail[6, :1] + tail[6, WIDE : WIDE + 1]

    return (
        final,
        blended,
        new_sum,
        grad_state,
        grad_prev,
        grad_halt_sum,
        grad_w_query,
        grad_w_key,
        grad_w_value,
        grad_w_out,
        grad_w_inner,
        grad_b_inner,
        grad_w_outer,
        vec_grads[0],
        vec_grads[1],
        vec_grads[2],
        vec_grads[3],
        vec_grads[4],
        vec_grads[5],
        grad_b_halt,
    )


def solution(mesh):
    rows = P("wsh", "ctx", None)
    marks = P("wsh", "ctx")
    column, row, vector = P(None, "wsh"), P("wsh", None), P("wsh")
    in_specs = (
        (rows, rows, marks, marks, marks, column, column, column, row, column, vector, row)
        + (vector,) * 6
        + (P(), rows, rows, marks)
    )
    out_specs = (
        (rows, rows, marks, rows, rows, marks, column, column, column, row, column, vector, row)
        + (vector,) * 6
        + (P(),)
    )
    return jax.shard_map(body, mesh=mesh, in_specs=in_specs, out_specs=out_specs, check_vma=False)
```
